32 devices in a mesh: row: 4 (over z), col: 8 (over y, x, core).
Axes of the slice: x: 2, y: 2, z: 4, core: 2. Of those that a mesh axis runs over, the one named last changes fastest.
Arguments:
- atom_feat: bfloat16 [4096, 128], P(('row', 'col')), may hold values from -12 to 12
- atom_token: int32 [4096], P(('row', 'col')), may hold values from 0 to 767, as said below
- window_start: int32 [128], P(('row', 'col')), may hold values from -64 to 4032, as said below
- token_cond: bfloat16 [768, 768], P('row'), may hold values from -6 to 6
- token_mask: int32 [768], replicated, may hold values from 0 to 1, as said below
- pair: bfloat16 [768, 768, 128], P('row', 'col'), may hold values from -300 to 300
- enc_in: bfloat16 [4, 128, 128], replicated, may hold values from -2 to 2
- enc_out: bfloat16 [128, 128], replicated, may hold values from -0.5 to 0.5
- pool_weight: bfloat16 [128, 768], replicated, may hold values from -0.5 to 0.5
- tok_in: bfloat16 [2, 4, 768, 768], replicated, may hold values from -0.21875 to 0.21875
- tok_out: bfloat16 [2, 768, 768], replicated, may hold values from -0.21875 to 0.21875
- pair_weight: bfloat16 [2, 128, 16], replicated, may hold values from -0.5 to 0.5
- trans_in: bfloat16 [2, 2, 768, 1536], P(None, None, None, 'col'), may hold values from -0.21875 to 0.21875
- trans_out: bfloat16 [2, 1536, 768], P(None, 'col'), may hold values from -0.15625 to 0.15625
- tok_atom: bfloat16 [768, 128], replicated, may hold values from -0.21875 to 0.21875
- dec_in: bfloat16 [4, 128, 128], replicated, may hold values from -2 to 2
- dec_out: bfloat16 [128, 128], replicated, may hold values from -0.5 to 0.5
- pos_out: bfloat16 [3, 128], replicated, may hold values from -0.5 to 0.5
Outputs:
- position_update: float32 [3, 4096], P(None, ('row', 'col'))
The draws below stay inside these ranges and needn't reach their ends.
Inputs may be any that keep to these rules, and one draw needn't show every extreme that they name: `atom_token`: non-decreasing; every token number 0 to 767 occurs; for every r, the atoms r * 1024 to (r + 1) * 1024 - 1 belong to the tokens r * 192 to (r + 1) * 192 - 1. window_start[b] lies between 32 b - 64 and 32 b - 32. `token_mask`: ones on a leading run of 384 tokens or more, zeros after, at least one zero.
All inputs are finite; a program needn't handle non-finite values.
Results may differ from the reference program's by a relative error of at most 0.029.
Values may be sent and summed in bfloat16 or wider, within the bound.
No kernel may reach another device: no remote copies, remote signals or barrier semaphores. Data moves between devices by JAX's collectives and lax.ppermute only.
A program may use at most 128 MiB of HBM per device.

```python
import math
import jax
import jax.numpy as jnp
from jax import lax

CA = 128
HA = 4
C = 768
H = 16
CZ = 128
FFT = 1536
QB = 32
KW = 128
HALO = 64
BLOCKS = 2
TOK_ROW = 192
TOKENS = 768
ATOM_ROW = 1024
NATOM = 4096


def sign_vector(key):
    key = jax.random.fold_in(key, 700)
    return (jax.random.randint(key, (CA,), 0, 2) * 2 - 1).astype(jnp.float32)


def lift_terms(key, signs):
    hsize = CA // HA
    size = (300.0 / (CA * math.sqrt(hsize))) ** 0.5
    lift = (jax.random.randint(key, (hsize,), 0, 2) * 2 - 1).astype(jnp.float32) * size
    column = jnp.concatenate([lift, jnp.zeros((CA - hsize,), jnp.float32)])
    outer = (signs * CA ** (-0.5))[:, None] * column[None, :]
    empty = jnp.zeros((CA, CA), jnp.float32)
    return jnp.stack([outer, outer, empty, empty])


def draw_atom_feat(key, part):
    signs = sign_vector(key)
    key = jax.random.fold_in(key, 21)
    base_key, pick_key, spot_key, power_key = jax.random.split(key, 4)
    base = jnp.clip(jax.random.normal(base_key, (NATOM, CA), jnp.float32), -6.0, 6.0)
    nblk = NATOM // QB
    chosen = jax.random.randint(pick_key, (nblk,), 0, 4) == 0
    first = jax.random.randint(spot_key, (nblk,), 0, QB)
    inner = jnp.arange(QB, dtype=jnp.int32)[None, :]
    offset = (inner - first[:, None]) % QB
    spot = (offset == 0) | (offset == 11) | (offset == 21)
    hot = (chosen[:, None] & spot).reshape(NATOM)
    power = 1.5 * 4.0 ** jax.random.uniform(power_key, (NATOM,), jnp.float32)
    lifted = jnp.where(hot, power, 0.0)[:, None] * signs[None, :]
    return (base + lifted).astype(jnp.bfloat16)


def draw_enc_in(key, part):
    signs = sign_vector(key)
    key = jax.random.fold_in(key, 41)
    base_key, lift_key = jax.random.split(key)
    spread = CA ** (-0.5)
    base = jnp.clip(jax.random.normal(base_key, (4, CA, CA), jnp.float32), -6.0, 6.0) * spread
    return (base + lift_terms(lift_key, signs)).astype(jnp.bfloat16)


def draw_dec_in(key, part):
    signs = sign_vector(key)
    key = jax.random.fold_in(key, 42)
    base_key, lift_key = jax.random.split(key)
    spread = CA ** (-0.5)
    base = jnp.clip(jax.random.normal(base_key, (4, CA, CA), jnp.float32), -6.0, 6.0) * spread
    return (base + lift_terms(lift_key, signs)).astype(jnp.bfloat16)


def draw_pair(key, part):
    key = jax.random.fold_in(key, 31)
    base_key, row_key, force_key, near_key, gap_key, power_key, sign_key = jax.random.split(key, 7)
    shape = (TOKENS, TOKENS, CZ)
    base = jnp.clip(jax.random.normal(base_key, shape, jnp.float32), -6.0, 6.0)
    half = TOKENS // 2
    rows = jnp.arange(TOKENS, dtype=jnp.int32)
    forced = jax.random.randint(force_key, (), 0, TOKENS)
    hot = (jax.random.randint(row_key, (TOKENS,), 0, 32) == 0) | (rows == forced)
    near = jax.random.randint(near_key, (TOKENS,), 0, half)
    far = (near + 1 + jax.random.randint(gap_key, (TOKENS,), 0, half - 1)) % half
    power = 150.0 * 2.0 ** jax.random.uniform(power_key, (TOKENS,), jnp.float32)
    signs = (jax.random.randint(sign_key, (TOKENS, CZ), 0, 2) * 2 - 1).astype(jnp.float32)
    cols = rows[None, :]
    lead = hot[:, None] & (cols == near[:, None])
    second = hot[:, None] & (cols == far[:, None])
    factor = jnp.where(lead, 1.0, jnp.where(second, 0.992, 0.0)) * power[:, None]
    planted = factor[:, :, None] * signs[:, None, :]
    return jnp.where((lead | second)[:, :, None], planted, base).astype(jnp.bfloat16)


def draw_atom_token(key, part):
    key = jax.random.fold_in(key, 11)
    nrows = NATOM // ATOM_ROW
    scores = jax.random.randint(key, (nrows, ATOM_ROW), 0, 2 ** 17)
    scores = scores * ATOM_ROW + jnp.arange(ATOM_ROW, dtype=jnp.int32)[None, :]
    scores = scores.at[:, 0].set(-1)
    ranks = jnp.argsort(jnp.argsort(scores, axis=1), axis=1)
    starts = (ranks < TOK_ROW).astype(jnp.int32)
    within = jnp.cumsum(starts, axis=1) - 1
    tokens = within + TOK_ROW * jnp.arange(nrows, dtype=jnp.int32)[:, None]
    return tokens.reshape(NATOM).astype(jnp.int32)


def draw_window_start(key, part):
    key = jax.random.fold_in(key, 12)
    first_key, low_key, high_key = jax.random.split(key, 3)
    nblk = NATOM // QB
    reach = HALO - (KW - QB) // 2
    shifts = jax.random.randint(first_key, (nblk,), -reach, reach + 1)
    low = jax.random.randint(low_key, (), 0, nblk // 2)
    high = jax.random.randint(high_key, (), nblk // 2, nblk)
    shifts = shifts.at[low].set(-reach).at[high].set(reach)
    shifts = shifts.at[0].set(-reach).at[nblk - 1].set(reach)
    return (QB * jnp.arange(nblk, dtype=jnp.int32) - (KW - QB) // 2 + shifts).astype(jnp.int32)


def draw_token_mask(key, part):
    key = jax.random.fold_in(key, 13)
    count = jax.random.randint(key, (), TOKENS // 2, TOKENS)
    return (jnp.arange(TOKENS, dtype=jnp.int32) < count).astype(jnp.int32)


def steps_of(own_key, dims, cuts, least, top_value):
    def one(dim, shards_of):
        steps = jax.random.uniform(jax.random.fold_in(jax.random.fold_in(own_key, 6), dim), (shards_of,), jnp.float32, least / len(cuts), top_value / len(cuts))
        return jnp.repeat(jnp.exp(steps), dims[dim] // shards_of).reshape((-1,) + (1,) * (len(dims) - dim - 1))

    gain = one(*cuts[0])
    for cut in cuts[1:]:
        gain = gain * one(*cut)
    return gain


def scatter_about(rng, dims, scale, most, cuts=(), held_as=jnp.bfloat16):
    result = scale * jax.random.normal(rng, dims, jnp.float32)
    if cuts:
        result = result * steps_of(rng, dims, cuts, -0.22, 0.18)
    return jnp.clip(result, -most, most).astype(held_as)


def setup_inputs(seed: int = 0) -> dict:
    streams_of = jax.random.split(jax.random.key(seed), 19)
    atom_feat = draw_atom_feat(jax.random.fold_in(streams_of[18], 71), 0)
    atom_token = draw_atom_token(jax.random.fold_in(streams_of[18], 71), 0)
    window_start = draw_window_start(jax.random.fold_in(streams_of[18], 71), 0)
    token_cond = scatter_about(streams_of[3], (TOKENS, C), 1.0, 6.0, ((0, 4),))
    token_mask = draw_token_mask(jax.random.fold_in(streams_of[18], 71), 0)
    pair = draw_pair(jax.random.fold_in(streams_of[18], 71), 0)
    enc_in = draw_enc_in(jax.random.fold_in(streams_of[18], 71), 0)
    enc_out = scatter_about(streams_of[7], (CA, CA), CA ** -0.5, 0.5)
    pool_weight = scatter_about(streams_of[8], (CA, C), CA ** -0.5, 0.5)
    tok_in = scatter_about(streams_of[9], (BLOCKS, 4, C, C), C ** -0.5, 0.21875)
    tok_out = scatter_about(streams_of[10], (BLOCKS, C, C), C ** -0.5, 0.21875)
    pair_weight = scatter_about(streams_of[11], (BLOCKS, CZ, H), CZ ** -0.5, 0.5)
    trans_in = scatter_about(streams_of[12], (BLOCKS, 2, C, FFT), C ** -0.5, 0.21875, ((3, 8),))
    trans_out = scatter_about(streams_of[13], (BLOCKS, FFT, C), FFT ** -0.5, 0.15625, ((1, 8),))
    tok_atom = scatter_about(streams_of[14], (C, CA), C ** -0.5, 0.21875)
    dec_in = draw_dec_in(jax.random.fold_in(streams_of[18], 71), 0)
    dec_out = scatter_about(streams_of[16], (CA, CA), CA ** -0.5, 0.5)
    pos_out = scatter_about(streams_of[17], (3, CA), CA ** -0.5, 0.5)
    return {"atom_feat": atom_feat, "atom_token": atom_token, "window_start": window_start, "token_cond": token_cond, "token_mask": token_mask, "pair": pair, "enc_in": enc_in, "enc_out": enc_out, "pool_weight": pool_weight, "tok_in": tok_in, "tok_out": tok_out, "pair_weight": pair_weight, "trans_in": trans_in, "trans_out": trans_out, "tok_atom": tok_atom, "dec_in": dec_in, "dec_out": dec_out, "pos_out": pos_out}


def normed(x):
    x = x.astype(jnp.float32)
    cent = x - lax.optimization_barrier(jnp.mean(x, -1, keepdims=True))
    var = lax.optimization_barrier(jnp.mean(cent * cent, -1, keepdims=True))
    return cent * lax.rsqrt(var + 1e-05)

def atom_layer(x, starts, w_in, w_out):
    width = x.shape[1]
    hsize = width // HA
    xn = normed(x).astype(jnp.bfloat16)
    query = jnp.dot(xn, w_in[0], preferred_element_type=jnp.float32).astype(jnp.bfloat16)
    keys = jnp.dot(xn, w_in[1], preferred_element_type=jnp.float32).astype(jnp.bfloat16)
    vals = jnp.dot(xn, w_in[2], preferred_element_type=jnp.float32).astype(jnp.bfloat16)
    gate = jnp.dot(xn, w_in[3], preferred_element_type=jnp.float32)
    both = jnp.concatenate([keys, vals], 1)
    padded = jnp.pad(both, ((HALO, HALO), (0, 0)))
    nblk = NATOM // QB
    local = (starts + HALO).astype(jnp.int32)
    windows = jax.vmap(lambda s: lax.dynamic_slice_in_dim(padded, s, KW, 0))(local)
    glob = starts[:, None] + jnp.arange(KW, dtype=jnp.int32)[None, :]
    valid = (glob >= 0) & (glob < NATOM)
    qblk = query.reshape(nblk, QB, HA, hsize).astype(jnp.float32)
    kblk = windows[:, :, :width].reshape(nblk, KW, HA, hsize).astype(jnp.float32)
    vblk = windows[:, :, width:].reshape(nblk, KW, HA, hsize).astype(jnp.float32)
    scores = jnp.einsum('bqhd,bkhd->bhqk', qblk, kblk) / jnp.sqrt(jnp.float32(hsize))
    scores = jnp.where(valid[:, None, None, :], scores, -1000000000.0)
    top = lax.optimization_barrier(jnp.max(scores, -1, keepdims=True))
    expd = jnp.exp(scores - top)
    total = lax.optimization_barrier(jnp.sum(expd, -1))
    outs = jnp.einsum('bhqk,bkhd->bqhd', expd.astype(jnp.bfloat16).astype(jnp.float32), vblk)
    outs = outs / jnp.transpose(total, (0, 2, 1))[:, :, :, None]
    outs = outs.reshape(NATOM, width)
    gated = (jax.nn.sigmoid(gate) * outs).astype(jnp.bfloat16)
    return (x.astype(jnp.float32) + jnp.dot(gated, w_out, preferred_element_type=jnp.float32)).astype(jnp.bfloat16)

def token_block(act, pair, key_valid, w_in, w_out, w_pair, t_in, t_out):
    hsize = C // H
    xn = normed(act).astype(jnp.bfloat16)
    query = jnp.dot(xn, w_in[0], preferred_element_type=jnp.float32).astype(jnp.bfloat16)
    keys = jnp.dot(xn, w_in[1], preferred_element_type=jnp.float32).astype(jnp.bfloat16)
    vals = jnp.dot(xn, w_in[2], preferred_element_type=jnp.float32).astype(jnp.bfloat16)
    gate = jnp.dot(xn, w_in[3], preferred_element_type=jnp.float32)
    kh = keys.reshape(TOKENS, H, hsize).astype(jnp.float32)
    vh = vals.reshape(TOKENS, H, hsize).astype(jnp.float32)
    qrows = min(128, TOKENS)
    qblocks = query.reshape(TOKENS // qrows, qrows, H, hsize)
    pblocks = pair.reshape(TOKENS // qrows, qrows, TOKENS, CZ)
    wpair = w_pair.astype(jnp.float32)

    def one_block(args):
        qblk, zblk = args
        bias = jnp.einsum('qkc,ch->hqk', zblk.astype(jnp.float32), wpair)
        scores = jnp.einsum('qhd,khd->hqk', qblk.astype(jnp.float32), kh) / jnp.sqrt(jnp.float32(hsize)) + bias
        scores = jnp.where(key_valid[None, None, :], scores, -1000000000.0)
        top = lax.optimization_barrier(jnp.max(scores, -1, keepdims=True))
        expd = jnp.exp(scores - top)
        total = lax.optimization_barrier(jnp.sum(expd, -1))
        outs = jnp.einsum('hqk,khd->qhd', expd.astype(jnp.bfloat16).astype(jnp.float32), vh)
        outs = outs / jnp.transpose(total)[:, :, None]
        return outs.reshape(qrows, C)
    attn = lax.map(one_block, (qblocks, pblocks)).reshape(TOKENS, C)
    gated = (jax.nn.sigmoid(gate) * attn).astype(jnp.bfloat16)
    act = act + jnp.dot(gated, w_out, preferred_element_type=jnp.float32)
    xn2 = normed(act).astype(jnp.bfloat16)
    swish = jax.nn.silu(jnp.dot(xn2, t_in[0], preferred_element_type=jnp.float32))
    hidden = (swish * jnp.dot(xn2, t_in[1], preferred_element_type=jnp.float32)).astype(jnp.bfloat16)
    return act + jnp.dot(hidden, t_out, preferred_element_type=jnp.float32)

def reference(atom_feat, atom_token, window_start, token_cond, token_mask, pair, enc_in, enc_out, pool_weight, tok_in, tok_out, pair_weight, trans_in, trans_out, tok_atom, dec_in, dec_out, pos_out):
    first = atom_layer(atom_feat, window_start, enc_in, enc_out)
    feats = jax.nn.relu(jnp.dot(first, pool_weight, preferred_element_type=jnp.float32)).astype(jnp.bfloat16)
    sums = jax.ops.segment_sum(feats.astype(jnp.float32), atom_token, TOKENS)
    counts = jax.ops.segment_sum(jnp.ones((NATOM,), jnp.float32), atom_token, TOKENS)
    act = sums / counts[:, None] + token_cond.astype(jnp.float32)
    key_valid = token_mask == 1
    for layer in range(BLOCKS):
        act = token_block(act, pair, key_valid, tok_in[layer], tok_out[layer], pair_weight[layer], trans_in[layer], trans_out[layer])
    proj = jnp.dot(normed(act).astype(jnp.bfloat16), tok_atom, preferred_element_type=jnp.float32).astype(jnp.bfloat16)
    spread = jnp.take(proj, atom_token.astype(jnp.int32), axis=0)
    second = (first.astype(jnp.float32) + spread.astype(jnp.float32)).astype(jnp.bfloat16)
    third = atom_layer(second, window_start, dec_in, dec_out)
    return jnp.dot(pos_out, jnp.transpose(normed(third).astype(jnp.bfloat16)), preferred_element_type=jnp.float32)
```

```python
import functools
import math

import jax
import jax.numpy as jnp
from jax import lax
from jax.experimental import pallas as pl
from jax.experimental.pallas import tpu as pltpu
from jax.sharding import PartitionSpec as P

HA = 4
QB = 32
KW = 128
HALO = 64
BLOCKS = 2
EXTRA = 16
MIB = 1 << 20
F32 = jnp.float32
BF16 = jnp.bfloat16


def call(kernel, outs, *args, scalars=(), far=(), scratch=(), grant=8, flops=0, moved=0):
    smem = pl.BlockSpec(memory_space=pltpu.SMEM)
    vmem = pl.BlockSpec(memory_space=pltpu.VMEM)
    hbm = pl.BlockSpec(memory_space=pltpu.HBM)
    return pl.pallas_call(
        kernel,
        out_shape=outs,
        in_specs=[smem] * len(scalars) + [vmem] * len(args) + [hbm] * len(far),
        out_specs=jax.tree.map(lambda _: vmem, outs),
        scratch_shapes=list(scratch),
        compiler_params=pltpu.CompilerParams(vmem_limit_bytes=grant * MIB),
        cost_estimate=pl.CostEstimate(flops=flops, bytes_accessed=moved, transcendentals=0),
    )(*scalars, *args, *far)


def dot(a, b):
    return jnp.dot(a, b, preferred_element_type=F32)


def dot_nt(a, b):
    return lax.dot_general(a, b, (((1,), (1,)), ((), ())), preferred_element_type=F32)


def dot_tn(a, b):
    return lax.dot_general(a, b, (((0,), (0,)), ((), ())), preferred_element_type=F32)


def normed(x):
    x = x.astype(F32)
    cent = x - jnp.mean(x, -1, keepdims=True)
    var = jnp.mean(cent * cent, -1, keepdims=True)
    return cent * lax.rsqrt(var + 1e-05)


def iota(shape, dim):
    return lax.broadcasted_iota(jnp.int32, shape, dim)


def window_mask(shifts, first, natom, nkeys):
    shape = (len(shifts) * QB, nkeys)
    block = iota(shape, 0) // QB
    low = jnp.zeros(shape, jnp.int32)
    for i, shift in enumerate(shifts):
        low = jnp.where(block == i, shift + QB * i, low)
    key = iota(shape, 1)
    atom = key + first
    return (key >= low) & (key < low + KW) & (atom >= 0) & (atom < natom)


def attend(x, xn, gate, query, keys, vals, mask, w_out):
    width = x.shape[1]
    hsize = width // HA
    lane = iota((1, width), 1) // hsize
    outs = jnp.zeros(x.shape, F32)
    for h in range(HA):
        pick = (lane == h).astype(BF16)
        scores = dot_nt(query, keys * pick) * (1.0 / math.sqrt(hsize))
        scores = jnp.where(mask, scores, -1000000000.0)
        top = jnp.max(scores, -1, keepdims=True)
        expd = jnp.exp(scores - top)
        total = jnp.sum(expd, -1, keepdims=True)
        outs = outs + dot(expd.astype(BF16), vals * pick) / total
    gated = (jax.nn.sigmoid(gate) * outs).astype(BF16)
    return (x.astype(F32) + dot(gated, w_out)).astype(BF16)


def shifts_of(tail_ref, lanes):
    tail = tail_ref[tail_ref.shape[0] - EXTRA :, :].astype(F32)
    return [tail[1:2, k : k + 1].astype(jnp.int32) for k in lanes]


def encoder_kernel(natom, place, own_ref, prev_ref, next_ref, w_in, w_out, ext_ref, all_ref):
    rows = own_ref.shape[0] - EXTRA
    nblk = rows // QB
    half = HALO // QB
    x = jnp.concatenate([prev_ref[:rows], own_ref[:rows], next_ref[:rows]], 0)
    xn = normed(x).astype(BF16)
    keys = dot(xn, w_in[1]).astype(BF16)
    vals = dot(xn, w_in[2]).astype(BF16)
    qx, qn = x[HALO : 3 * rows - HALO], xn[HALO : 3 * rows - HALO]
    query = dot(qn, w_in[0]).astype(BF16)
    gate = dot(qn, w_in[3])
    shifts = (
        shifts_of(prev_ref, range(nblk - half, nblk))
        + shifts_of(own_ref, range(nblk))
        + shifts_of(next_ref, range(half))
    )
    first = place[0] * rows - rows
    for part in range(2):
        mine = slice(part * rows, (part + 1) * rows)
        seen = slice(part * rows, (part + 2) * rows)
        mask = window_mask(
            shifts[part * nblk : (part + 1) * nblk], first + part * rows, natom, 2 * rows
        )
        ext_ref[mine] = attend(
            qx[mine], qn[mine], gate[mine], query[mine], keys[seen], vals[seen], mask, w_out[...]
        )
    new = ext_ref[HALO : HALO + rows]
    tail = own_ref[rows:]
    for j in range(all_ref.shape[0]):
        all_ref[j, :rows] = new
        all_ref[j, rows:] = tail


def pool_kernel(place, both_ref, weight, cond, act_ref, xn_ref, send_ref):
    count, rows = both_ref.shape[0], both_ref.shape[1] - EXTRA
    tokens = cond.shape[0]
    sums = jnp.zeros(cond.shape, F32)
    counts = jnp.zeros((tokens, 1), F32)
    step = 4 if count % 4 == 0 else 1
    for j in range(0, count, step):
        atoms = jnp.concatenate([both_ref[j + k, :rows] for k in range(step)], 0)
        feats = jnp.maximum(dot(atoms, weight[...]), 0.0).astype(BF16)
        spot = jnp.concatenate(
            [both_ref[j + k, rows:].astype(F32)[0:1] for k in range(step)], 1
        ).astype(jnp.int32)
        onehot = (iota((tokens, step * rows), 0) == spot).astype(F32)
        sums = sums + dot(onehot.astype(BF16), feats)
        counts = counts + jnp.sum(onehot, -1, keepdims=True)
    act = sums / counts + cond[...].astype(F32)
    xn = normed(act)
    xn_ref[...] = xn.astype(BF16)
    cols = send_ref.shape[0]
    part = xn[:cols]
    for k in range(1, tokens // cols):
        part = jnp.where(place[2] == k, xn[k * cols : (k + 1) * cols], part)
    send_ref[...] = part.astype(BF16)
    own = act_ref.shape[0]
    mine = act[:own]
    for c in range(1, tokens // own):
        mine = jnp.where(place[1] == c, act[c * own : (c + 1) * own], mine)
    act_ref[...] = mine


def decoder_kernel(natom, place, x1_ref, own_ref, prev_ref, next_ref, proj, w_in, w_out, pos, out):
    rows = own_ref.shape[0] - EXTRA
    tokens = proj.shape[0]
    spread = []
    for k, ref in enumerate((prev_ref, own_ref, next_ref)):
        spot = ref[rows:].astype(F32)[0:1].astype(jnp.int32) + place[7 + k]
        onehot = (iota((tokens, rows), 0) == spot).astype(F32).astype(BF16)
        spread.append(dot_tn(onehot, proj[...]))
    spread = jnp.concatenate([spread[0][rows - HALO :], spread[1], spread[2][:HALO]], 0)
    x = (x1_ref[...].astype(F32) + spread).astype(BF16)
    xn = normed(x).astype(BF16)
    keys = dot(xn, w_in[1]).astype(BF16)
    vals = dot(xn, w_in[2]).astype(BF16)
    qx, qn = x[HALO : HALO + rows], xn[HALO : HALO + rows]
    query = dot(qn, w_in[0]).astype(BF16)
    gate = dot(qn, w_in[3])
    shifts = shifts_of(own_ref, range(rows // QB))
    mask = window_mask(shifts, place[0] * rows - HALO, natom, 2 * rows)
    third = attend(qx, qn, gate, query, keys, vals, mask, w_out[...])
    out[...] = dot_nt(pos[...], normed(third).astype(BF16))


def pack_kernel(first, second, *outs):
    hid = second.shape[1]
    for layer, out in enumerate(outs):
        out[:hid] = first[layer, 0]
        out[hid : 2 * hid] = first[layer, 1]
        out[2 * hid :] = second[layer]


def bias_kernel(pair_ref, weight, out_ref):
    rows, cols, _ = pair_ref.shape
    pad = out_ref.shape[2] - cols

    for q in range(rows):
        bias = dot_nt(weight[...], pair_ref[q])
        out_ref[q] = jnp.concatenate([bias, jnp.zeros((bias.shape[0], pad), F32)], 1)


def prepare(sources, targets, sems):
    return [
        pltpu.make_async_copy(source, target, sems.at[i])
        for i, (source, target) in enumerate(zip(sources, targets))
    ]


def attention_kernel(
    layer,
    place,
    xn_ref,
    here_ref,
    came_ref,
    bias_ref,
    w_in,
    out_ref,
    w_query,
    w_key,
    w_val,
    sems,
):
    fetches = prepare([w_in.at[layer, k] for k in range(3)], [w_query, w_key, w_val], sems)
    fetches[0].start()
    fetches[1].start()
    rows, width = xn_ref.shape
    cols = here_ref.shape[0]
    heads = bias_ref.shape[1] // BLOCKS
    hsize = width // heads
    span = bias_ref.shape[2]
    key_xn = jnp.where(place[3] == place[4], here_ref[...].astype(F32), came_ref[...].astype(F32))
    key_xn = jnp.concatenate([key_xn, jnp.zeros((span - cols, width), F32)], 0).astype(BF16)
    fetches[0].wait()
    fetches[2].start()
    query = dot(xn_ref[...], w_query[...]).astype(BF16)
    fetches[1].wait()
    keys = dot(key_xn, w_key[...]).astype(BF16)
    fetches[2].wait()
    vals = dot(key_xn, w_val[...]).astype(BF16)
    valid = iota((1, span), 1) + place[5] < place[6]
    valid = valid & (iota((1, span), 1) < cols)
    group = heads // 2
    part = group * hsize
    lane = iota((1, part), 1) // hsize
    spot = iota((1, span), 1)
    levels = jnp.zeros((rows, span), F32)
    for g in range(2):
        wide = slice(g * part, (g + 1) * part)
        kg, vg = keys[:, wide], vals[:, wide]
        picks = [(lane == h).astype(BF16) for h in range(group)]
        stacked = jnp.concatenate([kg * p for p in picks], 0)
        scores = dot_nt(query[:, wide], stacked) * (1.0 / math.sqrt(hsize))
        probs = []
        for h in range(group):
            head = g * group + h
            score = scores[:, h * span : (h + 1) * span] + bias_ref[:, layer * heads + head, :]
            score = jnp.where(valid, score, -1000000000.0)
            top = jnp.max(score, -1, keepdims=True)
            expd = jnp.exp(score - top)
            total = jnp.sum(expd, -1, keepdims=True)
            probs.append((expd / total).astype(BF16))
            levels = jnp.where(spot % heads == head, top + jnp.log(total), levels)
        stacked = jnp.concatenate([vg * p for p in picks], 0)
        out_ref[:, wide] = dot(jnp.concatenate(probs, 1), stacked).astype(BF16)
    high = levels.astype(BF16).astype(F32)
    rest = levels - high
    middle = rest.astype(BF16).astype(F32)
    low = rest - middle
    packed = jnp.where(spot < heads, high, jnp.where(spot < 2 * heads, middle, low))
    out_ref[:, width:] = jnp.where(spot < 3 * heads, packed, 0.0).astype(BF16)


def finish_kernel(
    layer,
    heads,
    project,
    message,
    act_ref,
    *refs,
):
    if project:
        tok_atom, *refs = refs
    w_in, w_out, trans, act_out, all_ref, w_gate, w_mix, w_first, w_second, sems = refs
    blocks, hid = w_second.shape[:2]
    fetches = prepare(
        [w_in.at[layer, 3], w_out.at[layer]]
        + [trans.at[j, pl.ds(0, 2 * hid)] for j in range(blocks)]
        + [trans.at[j, pl.ds(2 * hid, hid)] for j in range(blocks)],
        [w_gate, w_mix]
        + [w_first.at[j] for j in range(blocks)]
        + [w_second.at[j] for j in range(blocks)],
        sems,
    )
    firsts, seconds = fetches[2 : 2 + blocks], fetches[2 + blocks :]
    for copy in fetches[:2]:
        copy.start()
    width = act_ref.shape[1]
    hsize = width // heads
    parts = [message[j, :, width:].astype(F32) for j in range(message.shape[0])]
    span = parts[0].shape[1]
    levels = [
        p + pltpu.roll(p, span - heads, 1) + pltpu.roll(p, span - 2 * heads, 1) for p in parts
    ]
    top = functools.reduce(jnp.maximum, levels)
    weights = [jnp.exp(level - top) for level in levels]
    whole = functools.reduce(jnp.add, weights)
    lane = iota((1, span), 1)
    row = iota((span, width), 0)
    expand = (row % heads == iota((span, width), 1) // hsize) & (row < 2 * heads)
    expand = expand.astype(F32).astype(BF16)
    attn = jnp.zeros(act_ref.shape, F32)
    for j, weight in enumerate(weights):
        weight = weight / whole
        high = weight.astype(BF16).astype(F32)
        packed = jnp.where(lane < heads, high, pltpu.roll(weight - high, heads, 1))
        packed = jnp.where(lane < 2 * heads, packed, 0.0).astype(BF16)
        attn = attn + dot(packed, expand) * message[j, :, :width].astype(F32)
    fetches[0].wait()
    for copy in firsts:
        copy.start()
    gate = dot(normed(act_ref[...]).astype(BF16), w_gate[...])
    gated = (jax.nn.sigmoid(gate) * attn).astype(BF16)
    fetches[1].wait()
    for copy in seconds:
        copy.start()
    act = act_ref[...] + dot(gated, w_mix[...])
    xn2 = normed(act).astype(BF16)
    hidden = []
    for j in range(blocks):
        firsts[j].wait()
        both = dot_nt(xn2, w_first[j])
        left, right = both[:, :hid], both[:, hid:]
        hidden.append((left * jax.nn.sigmoid(left) * right).astype(BF16))
    for j in range(blocks):
        seconds[j].wait()
        act = act + dot(hidden[j], w_second[j])
    act_out[...] = act
    normal = normed(act).astype(BF16)
    if project:
        normal = dot(normal, tok_atom[...]).astype(BF16)
    for j in range(all_ref.shape[0]):
        all_ref[j] = normal


def finish(layer, message, act, w_in, w_out, trans, heads, copies, tok_atom=None):
    own, width = act.shape
    last = width if tok_atom is None else tok_atom.shape[1]
    blocks, packed, _ = trans.shape
    hid = packed // 3
    return call(
        functools.partial(finish_kernel, layer, heads, tok_atom is not None),
        [
            jax.ShapeDtypeStruct((own, width), F32),
            jax.ShapeDtypeStruct((copies, own, last), BF16),
        ],
        message,
        act,
        *(() if tok_atom is None else (tok_atom,)),
        far=(w_in, w_out, trans),
        scratch=[
            pltpu.VMEM((width, width), BF16),
            pltpu.VMEM((width, width), BF16),
            pltpu.VMEM((blocks, 2 * hid, width), BF16),
            pltpu.VMEM((blocks, hid, width), BF16),
            pltpu.SemaphoreType.DMA((2 + 2 * blocks,)),
        ],
        grant=59,
        flops=2 * own * trans.size,
        moved=2 * trans.size,
    )


def key_source(rows, cols):
    nrow, ncol = lax.axis_size("row"), lax.axis_size("col")
    shares = rows // cols
    pairs = []
    for owner in range(nrow):
        free = [list(range(share, ncol, shares)) for share in range(shares)]
        for r in range(nrow):
            for share in range(shares):
                if r != owner:
                    spot = (2 * ((r + owner) % 2) + share) % (ncol // shares) * shares + share
                    source = spot if spot in free[share] else free[share][0]
                    free[share].remove(source)
                    pairs.append((owner * ncol + source, r * ncol + owner * shares + share))
    return pairs


def body(
    atom_feat,
    atom_token,
    window_start,
    token_cond,
    token_mask,
    pair,
    enc_in,
    enc_out,
    pool_weight,
    tok_in,
    tok_out,
    pair_weight,
    trans_in,
    trans_out,
    tok_atom,
    dec_in,
    dec_out,
    pos_out,
):
    nrow, ncol = lax.axis_size("row"), lax.axis_size("col")
    everyone = ("row", "col")
    count = nrow * ncol
    me_row, me_col = lax.axis_index("row"), lax.axis_index("col")
    me = me_row * ncol + me_col
    rows, width = token_cond.shape
    cols = pair.shape[1]
    heads = pair_weight.shape[2]
    own = rows // ncol
    atoms, afeat = atom_feat.shape
    natom = atoms * count
    nblk = atoms // QB

    hid = trans_out.shape[1]
    packed = call(
        pack_kernel,
        [jax.ShapeDtypeStruct((3 * hid, width), BF16)] * BLOCKS,
        jnp.swapaxes(trans_in, 2, 3),
        trans_out,
        grant=60,
        moved=12 * trans_out.size,
    )
    trans = [lax.all_gather(part, "col") for part in packed]

    share = me_col % (rows // cols)
    start = me_col * cols
    place = jnp.stack(
        [me, me_col, share, start // rows, me_row, start, jnp.sum(token_mask)]
        + [(me + step) // ncol * rows for step in (-1, 0, 1)]
    )

    local_token = atom_token - me_row * rows
    first_block = me * nblk
    shift = window_start - QB * (first_block + jnp.arange(nblk, dtype=jnp.int32)) + HALO
    tail = jnp.stack([local_token, jnp.pad(shift, (0, atoms - nblk))])
    tail = jnp.pad(tail, ((0, EXTRA - 2), (0, afeat - atoms))).astype(BF16)
    feat = jnp.concatenate([atom_feat, tail], 0)
    up = [(i, i + 1) for i in range(count - 1)]
    prev = lax.ppermute(feat, everyone, up)
    after = lax.ppermute(feat, everyone, [(b, a) for a, b in up])

    ext, copies = call(
        functools.partial(encoder_kernel, natom),
        [
            jax.ShapeDtypeStruct((atoms + 2 * HALO, afeat), BF16),
            jax.ShapeDtypeStruct((ncol, atoms + EXTRA, afeat), BF16),
        ],
        feat,
        prev,
        after,
        enc_in,
        enc_out,
        scalars=(place,),
        flops=10**8,
        moved=10**6,
    )
    both = lax.all_to_all(copies, "col", 0, 0)

    span = -(-cols // 128) * 128
    weights = jnp.swapaxes(pair_weight, 1, 2).reshape(BLOCKS * heads, -1)
    step = 24
    bias = pl.pallas_call(
        bias_kernel,
        grid=(rows // step,),
        out_shape=jax.ShapeDtypeStruct((rows, BLOCKS * heads, span), F32),
        in_specs=[
            pl.BlockSpec((step, cols, pair.shape[2]), lambda i: (i, 0, 0)),
            pl.BlockSpec(weights.shape, lambda i: (0, 0)),
        ],
        out_specs=pl.BlockSpec((step, BLOCKS * heads, span), lambda i: (i, 0, 0)),
        compiler_params=pltpu.CompilerParams(vmem_limit_bytes=56 * MIB),
        cost_estimate=pl.CostEstimate(flops=4 * 10**9, bytes_accessed=8 * 10**6, transcendentals=0),
    )(pair, weights)

    act, xn, send = call(
        pool_kernel,
        [
            jax.ShapeDtypeStruct((own, width), F32),
            jax.ShapeDtypeStruct((rows, width), BF16),
            jax.ShapeDtypeStruct((cols, width), BF16),
        ],
        both,
        pool_weight,
        token_cond,
        scalars=(place,),
        flops=10**9,
        moved=10**6,
    )

    pairs = key_source(rows, cols)
    for layer in range(BLOCKS):
        if layer:
            send = lax.dynamic_slice_in_dim(xn, share * cols, cols, 0)
        came = lax.ppermute(send, everyone, pairs)
        message = call(
            functools.partial(attention_kernel, layer),
            jax.ShapeDtypeStruct((rows, width + span), BF16),
            xn,
            send,
            came,
            bias,
            scalars=(place,),
            far=(tok_in,),
            scratch=[pltpu.VMEM((width, width), BF16)] * 3 + [pltpu.SemaphoreType.DMA((3,))],
            grant=54,
            flops=10**9,
            moved=8 * 10**6,
        )
        message = lax.all_to_all(message.reshape(ncol, own, -1), "col", 0, 0)
        last = layer == BLOCKS - 1
        act, copies = finish(
            layer,
            message,
            act,
            tok_in,
            tok_out,
            trans[layer],
            heads,
            count if last else ncol,
            tok_atom if last else None,
        )
        if not last:
            xn = lax.all_to_all(copies, "col", 0, 0).reshape(rows, width)
    proj = lax.all_to_all(copies, everyone, 0, 0).reshape(count * own, afeat)

    return call(
        functools.partial(decoder_kernel, natom),
        jax.ShapeDtypeStruct((pos_out.shape[0], atoms), F32),
        ext,
        feat,
        prev,
        after,
        proj,
        dec_in,
        dec_out,
        pos_out,
        scalars=(place,),
        flops=10**8,
        moved=10**6,
    )


def solution(mesh):
    in_specs = (
        P(("row", "col"), None),
        P(("row", "col")),
        P(("row", "col")),
        P("row", None),
        P(),
        P("row", "col", None),
        P(),
        P(),
        P(),
        P(),
        P(),
        P(),
        P(None, None, None, "col"),
        P(None, "col", None),
        P(),
        P(),
        P(),
        P(),
    )
    out_specs = P(None, ("row", "col"))
    return jax.shard_map(body, mesh=mesh, in_specs=in_specs, out_specs=out_specs, check_vma=False)
```

```python
import functools
import math

import jax
import jax.numpy as jnp
from jax import lax
from jax.experimental import pallas as pl
from jax.experimental.pallas import tpu as pltpu
from jax.sharding import PartitionSpec as P

HA = 4
QB = 32
KW = 128
HALO = 64
BLOCKS = 2
EXTRA = 16
MIB = 1 << 20
F32 = jnp.float32
BF16 = jnp.bfloat16


def call(kernel, outs, *args, scalars=(), far=(), scratch=(), grant=8, flops=0, moved=0):
    smem = pl.BlockSpec(memory_space=pltpu.SMEM)
    vmem = pl.BlockSpec(memory_space=pltpu.VMEM)
    hbm = pl.BlockSpec(memory_space=pltpu.HBM)
    return pl.pallas_call(
        kernel,
        out_shape=outs,
        in_specs=[smem] * len(scalars) + [vmem] * len(args) + [hbm] * len(far),
        out_specs=jax.tree.map(lambda _: vmem, outs),
        scratch_shapes=list(scratch),
        compiler_params=pltpu.CompilerParams(vmem_limit_bytes=grant * MIB),
        cost_estimate=pl.CostEstimate(flops=flops, bytes_accessed=moved, transcendentals=0),
    )(*scalars, *args, *far)


def dot(a, b):
    return jnp.dot(a, b, preferred_element_type=F32)


def dot_nt(a, b):
    return lax.dot_general(a, b, (((1,), (1,)), ((), ())), preferred_element_type=F32)


def dot_tn(a, b):
    return lax.dot_general(a, b, (((0,), (0,)), ((), ())), preferred_element_type=F32)


def normed(x):
    x = x.astype(F32)
    cent = x - jnp.mean(x, -1, keepdims=True)
    var = jnp.mean(cent * cent, -1, keepdims=True)
    return cent * lax.rsqrt(var + 1e-05)


def iota(shape, dim):
    return lax.broadcasted_iota(jnp.int32, shape, dim)


def device():
    row, col = lax.axis_index("row"), lax.axis_index("col")
    return row, col, row * lax.axis_size("col") + col


def window_mask(shifts, first, natom, nkeys):
    shape = (len(shifts) * QB, nkeys)
    block = iota(shape, 0) // QB
    low = jnp.zeros(shape, jnp.int32)
    for i, shift in enumerate(shifts):
        low = jnp.where(block == i, shift + QB * i, low)
    key = iota(shape, 1)
    atom = key + first
    return (key >= low) & (key < low + KW) & (atom >= 0) & (atom < natom)


def attend(x, xn, gate, query, keys, vals, mask, w_out):
    width = x.shape[1]
    hsize = width // HA
    lane = iota((1, width), 1) // hsize
    outs = jnp.zeros(x.shape, F32)
    for h in range(HA):
        pick = (lane == h).astype(BF16)
        scores = dot_nt(query, keys * pick) * (1.0 / math.sqrt(hsize))
        scores = jnp.where(mask, scores, -1000000000.0)
        top = jnp.max(scores, -1, keepdims=True)
        expd = jnp.exp(scores - top)
        total = jnp.sum(expd, -1, keepdims=True)
        outs = outs + dot(expd.astype(BF16), vals * pick) / total
    gated = (jax.nn.sigmoid(gate) * outs).astype(BF16)
    return (x.astype(F32) + dot(gated, w_out)).astype(BF16)


def shifts_of(tail_ref, lanes):
    tail = tail_ref[tail_ref.shape[0] - EXTRA :, :].astype(F32)
    return [tail[1:2, k : k + 1].astype(jnp.int32) for k in lanes]


def encoder_kernel(natom, own_ref, prev_ref, next_ref, w_in, w_out, ext_ref, all_ref):
    rows = own_ref.shape[0] - EXTRA
    nblk = rows // QB
    half = HALO // QB
    x = jnp.concatenate([prev_ref[:rows], own_ref[:rows], next_ref[:rows]], 0)
    xn = normed(x).astype(BF16)
    keys = dot(xn, w_in[1]).astype(BF16)
    vals = dot(xn, w_in[2]).astype(BF16)
    qx, qn = x[HALO : 3 * rows - HALO], xn[HALO : 3 * rows - HALO]
    query = dot(qn, w_in[0]).astype(BF16)
    gate = dot(qn, w_in[3])
    shifts = (
        shifts_of(prev_ref, range(nblk - half, nblk))
        + shifts_of(own_ref, range(nblk))
        + shifts_of(next_ref, range(half))
    )
    first = device()[2] * rows - rows
    for part in range(2):
        mine = slice(part * rows, (part + 1) * rows)
        seen = slice(part * rows, (part + 2) * rows)
        mask = window_mask(
            shifts[part * nblk : (part + 1) * nblk], first + part * rows, natom, 2 * rows
        )
        ext_ref[mine] = attend(
            qx[mine], qn[mine], gate[mine], query[mine], keys[seen], vals[seen], mask, w_out[...]
        )
    new = ext_ref[HALO : HALO + rows]
    tail = own_ref[rows:]
    for j in range(all_ref.shape[0]):
        all_ref[j, :rows] = new
        all_ref[j, rows:] = tail


def pool_kernel(both_ref, weight, cond, act_ref, xn_ref, send_ref):
    count, rows = both_ref.shape[0], both_ref.shape[1] - EXTRA
    tokens = cond.shape[0]
    sums = jnp.zeros(cond.shape, F32)
    counts = jnp.zeros((tokens, 1), F32)
    step = 4 if count % 4 == 0 else 1
    for j in range(0, count, step):
        atoms = jnp.concatenate([both_ref[j + k, :rows] for k in range(step)], 0)
        feats = jnp.maximum(dot(atoms, weight[...]), 0.0).astype(BF16)
        spot = jnp.concatenate(
            [both_ref[j + k, rows:].astype(F32)[0:1] for k in range(step)], 1
        ).astype(jnp.int32)
        onehot = (iota((tokens, step * rows), 0) == spot).astype(F32)
        sums = sums + dot(onehot.astype(BF16), feats)
        counts = counts + jnp.sum(onehot, -1, keepdims=True)
    act = sums / counts + cond[...].astype(F32)
    xn = normed(act)
    xn_ref[...] = xn.astype(BF16)
    cols = send_ref.shape[0]
    part = xn[:cols]
    for k in range(1, tokens // cols):
        part = jnp.where(device()[1] % (tokens // cols) == k, xn[k * cols : (k + 1) * cols], part)
    send_ref[...] = part.astype(BF16)
    own = act_ref.shape[0]
    col = device()[1]
    mine = act[:own]
    for c in range(1, tokens // own):
        mine = jnp.where(col == c, act[c * own : (c + 1) * own], mine)
    act_ref[...] = mine


def decoder_kernel(natom, row_tokens, x1_ref, own_ref, prev_ref, next_ref, proj, w_in, w_out, pos, out):
    rows = own_ref.shape[0] - EXTRA
    tokens = proj.shape[0]
    me = device()[2]
    spread = []
    for k, ref in enumerate((prev_ref, own_ref, next_ref)):
        spot = ref[rows:].astype(F32)[0:1].astype(jnp.int32)
        spot = spot + (me + k - 1) // lax.axis_size("col") * row_tokens
        onehot = (iota((tokens, rows), 0) == spot).astype(F32).astype(BF16)
        spread.append(dot_tn(onehot, proj[...]))
    spread = jnp.concatenate([spread[0][rows - HALO :], spread[1], spread[2][:HALO]], 0)
    x = (x1_ref[...].astype(F32) + spread).astype(BF16)
    xn = normed(x).astype(BF16)
    keys = dot(xn, w_in[1]).astype(BF16)
    vals = dot(xn, w_in[2]).astype(BF16)
    qx, qn = x[HALO : HALO + rows], xn[HALO : HALO + rows]
    query = dot(qn, w_in[0]).astype(BF16)
    gate = dot(qn, w_in[3])
    shifts = shifts_of(own_ref, range(rows // QB))
    mask = window_mask(shifts, me * rows - HALO, natom, 2 * rows)
    third = attend(qx, qn, gate, query, keys, vals, mask, w_out[...])
    out[...] = dot_nt(pos[...], normed(third).astype(BF16))


def pack_kernel(row_tokens, starts, first, second, feat, token, *outs):
    out, own = outs
    hid = second.shape[1]
    for layer in range(BLOCKS):
        out[layer, :hid] = first[layer, 0]
        out[layer, hid : 2 * hid] = first[layer, 1]
        out[layer, 2 * hid :] = second[layer]
    rows, width = feat.shape
    row, _, me = device()
    nblk = starts.shape[0]
    lane = iota((EXTRA, width), 1)
    line = iota((EXTRA, width), 0)
    tail = jnp.where(line == 0, token[...] - row * row_tokens, 0)
    for k in range(nblk):
        shift = starts[k] - QB * (me * nblk + k) + HALO
        tail = jnp.where((line == 1) & (lane == k), shift, tail)
    own[:rows] = feat[...]
    own[rows:] = tail.astype(F32).astype(BF16)


def bias_kernel(pair_ref, weight, *outs):
    rows, cols, _ = pair_ref.shape
    _, heads, pad = outs[0].shape
    pad = pad - cols

    for q in range(rows):
        bias = dot_nt(weight[...], pair_ref[q])
        bias = jnp.concatenate([bias, jnp.zeros((bias.shape[0], pad), F32)], 1)
        for layer, out in enumerate(outs):
            out[q] = bias[layer * heads : (layer + 1) * heads]


def prepare(sources, targets, sems):
    return [
        pltpu.make_async_copy(source, target, sems.at[i])
        for i, (source, target) in enumerate(zip(sources, targets))
    ]


def query_kernel(layer, xn_ref, w_in, query, w_query, sems):
    (copy,) = prepare([w_in.at[layer, 0]], [w_query], sems)
    copy.start()
    copy.wait()
    query[...] = dot(xn_ref[...], w_query[...]).astype(BF16)


def attention_kernel(layer, mask_ref, *refs):
    far, out_ref, near, sems = refs[:5], refs[5], refs[6:-1], refs[-1]
    query, here, came, bias, w_in = far
    fetches = prepare([here, came, w_in.at[layer, 1], w_in.at[layer, 2], query, bias], near, sems)
    here_ref, came_ref, w_key, w_val, query, bias_ref = near
    for copy in fetches:
        copy.start()
    rows, width = query.shape
    cols = here_ref.shape[0]
    heads = bias_ref.shape[1]
    hsize = width // heads
    span = bias_ref.shape[2]
    row, col, _ = device()
    mine = col * cols // rows == row
    fetches[0].wait()
    fetches[1].wait()
    key_xn = jnp.where(mine, here_ref[...].astype(F32), came_ref[...].astype(F32))
    key_xn = jnp.concatenate([key_xn, jnp.zeros((span - cols, width), F32)], 0).astype(BF16)
    fetches[2].wait()
    keys = dot(key_xn, w_key[...]).astype(BF16)
    fetches[3].wait()
    vals = dot(key_xn, w_val[...]).astype(BF16)
    tokens = mask_ref.shape[0]
    count = jnp.int32(0)
    for bit in range(tokens.bit_length() - 1, -1, -1):
        longer = count + (1 << bit)
        inside = longer <= tokens
        last = mask_ref[jnp.where(inside, longer - 1, 0)]
        count = jnp.where(inside & (last == 1), longer, count)
    valid = iota((1, span), 1) + col * cols < count
    valid = valid & (iota((1, span), 1) < cols)
    fetches[4].wait()
    fetches[5].wait()
    group = heads // 2
    part = group * hsize
    lane = iota((1, part), 1) // hsize
    spot = iota((1, span), 1)
    levels = jnp.zeros((rows, span), F32)
    for g in range(2):
        wide = slice(g * part, (g + 1) * part)
        kg, vg = keys[:, wide], vals[:, wide]
        picks = [(lane == h).astype(BF16) for h in range(group)]
        stacked = jnp.concatenate([kg * p for p in picks], 0)
        scores = dot_nt(query[:, wide], stacked) * (1.0 / math.sqrt(hsize))
        probs = []
        for h in range(group):
            head = g * group + h
            score = scores[:, h * span : (h + 1) * span] + bias_ref[:, head, :]
            score = jnp.where(valid, score, -1000000000.0)
            top = jnp.max(score, -1, keepdims=True)
            expd = jnp.exp(score - top)
            total = jnp.sum(expd, -1, keepdims=True)
            probs.append((expd / total).astype(BF16))
            levels = jnp.where(spot % heads == head, top + jnp.log(total), levels)
        stacked = jnp.concatenate([vg * p for p in picks], 0)
        out_ref[:, wide] = dot(jnp.concatenate(probs, 1), stacked).astype(BF16)
    high = levels.astype(BF16).astype(F32)
    rest = levels - high
    middle = rest.astype(BF16).astype(F32)
    low = rest - middle
    packed = jnp.where(spot < heads, high, jnp.where(spot < 2 * heads, middle, low))
    out_ref[:, width:] = jnp.where(spot < 3 * heads, packed, 0.0).astype(BF16)


def mix_kernel(layer, heads, message, act_ref, w_in, w_out, act_out, xn2_out, w_gate, w_mix, sems):
    fetches = prepare([w_in.at[layer, 3], w_out.at[layer]], [w_gate, w_mix], sems)
    for copy in fetches:
        copy.start()
    width = act_ref.shape[1]
    hsize = width // heads
    parts = [message[j, :, width:].astype(F32) for j in range(message.shape[0])]
    span = parts[0].shape[1]
    levels = [
        p + pltpu.roll(p, span - heads, 1) + pltpu.roll(p, span - 2 * heads, 1) for p in parts
    ]
    top = functools.reduce(jnp.maximum, levels)
    weights = [jnp.exp(level - top) for level in levels]
    whole = functools.reduce(jnp.add, weights)
    lane = iota((1, span), 1)
    row = iota((span, width), 0)
    expand = (row % heads == iota((span, width), 1) // hsize) & (row < 2 * heads)
    expand = expand.astype(F32).astype(BF16)
    packed = []
    for weight in weights:
        weight = weight / whole
        high = weight.astype(BF16).astype(F32)
        both = jnp.where(lane < heads, high, pltpu.roll(weight - high, heads, 1))
        packed.append(jnp.where(lane < 2 * heads, both, 0.0))
    spread = dot(jnp.concatenate(packed, 0).astype(BF16), expand)
    own = act_ref.shape[0]
    attn = jnp.zeros(act_ref.shape, F32)
    for j in range(message.shape[0]):
        attn = attn + spread[j * own : (j + 1) * own] * message[j, :, :width].astype(F32)
    normal = normed(act_ref[...]).astype(BF16)
    fetches[0].wait()
    gated = (jax.nn.sigmoid(dot(normal, w_gate[...])) * attn).astype(BF16)
    fetches[1].wait()
    act = act_ref[...] + dot(gated, w_mix[...])
    act_out[...] = act
    xn2_out[...] = normed(act).astype(BF16)


def mix(layer, message, act, w_in, w_out, heads):
    own, width = act.shape
    return call(
        functools.partial(mix_kernel, layer, heads),
        [jax.ShapeDtypeStruct((own, width), F32), jax.ShapeDtypeStruct((own, width), BF16)],
        message,
        act,
        far=(w_in, w_out),
        scratch=[pltpu.VMEM((width, width), BF16)] * 2 + [pltpu.SemaphoreType.DMA((2,))],
        grant=60,
        flops=4 * own * width * width,
        moved=4 * width * width,
    )


def transition_kernel(layer, act_ref, xn2, *refs):
    groups = len(refs) // 2 - 3
    others, blocks = refs[: groups - 1], refs[groups - 1 : groups + 3]
    outs, (w_first, w_second, sems) = refs[groups + 3 : -3], refs[-3:]
    count, hid = w_second.shape[:2]
    fetches = prepare(
        [ref.at[layer, pl.ds(0, 2 * hid)] for ref in blocks]
        + [ref.at[layer, pl.ds(2 * hid, hid)] for ref in blocks],
        [w_first.at[j] for j in range(count)] + [w_second.at[j] for j in range(count)],
        sems,
    )
    for copy in fetches:
        copy.start()
    own = act_ref.shape[0]
    rows = jnp.concatenate([ref[...].astype(F32) for ref in (xn2, *others)], 0).astype(BF16)
    total = jnp.zeros((rows.shape[0], rows.shape[1]), F32)
    hidden = []
    for j in range(count):
        fetches[j].wait()
        both = dot_nt(rows, w_first[j])
        left, right = both[:, :hid], both[:, hid:]
        hidden.append((left * jax.nn.sigmoid(left) * right).astype(BF16))
    for j in range(count):
        fetches[count + j].wait()
        total = total + dot(hidden[j], w_second[j])
    outs[0][...] = act_ref[...] + total[:own]
    for k, out in enumerate(outs[1:], 1):
        out[...] = total[k * own : (k + 1) * own].astype(BF16)


def transition(layer, act, xn2, others, weights):
    own, width = act.shape
    blocks = len(weights)
    hid = weights[0].shape[1] // 3
    return call(
        functools.partial(transition_kernel, layer),
        [jax.ShapeDtypeStruct((own, width), F32)]
        + [jax.ShapeDtypeStruct((own, width), BF16)] * len(others),
        act,
        xn2,
        *others,
        far=weights,
        scratch=[
            pltpu.VMEM((blocks, 2 * hid, width), BF16),
            pltpu.VMEM((blocks, hid, width), BF16),
            pltpu.SemaphoreType.DMA((2 * blocks,)),
        ],
        grant=60,
        flops=12 * own * hid * width * blocks,
        moved=6 * hid * width * blocks,
    )


def close_kernel(project, act_ref, *refs):
    *refs, act_out, all_ref = refs
    if project:
        *refs, tok_atom = refs
    act = act_ref[...]
    for ref in refs:
        act = act + ref[...].astype(F32)
    act_out[...] = act
    normal = normed(act).astype(BF16)
    if project:
        normal = dot(normal, tok_atom[...]).astype(BF16)
    for j in range(all_ref.shape[0]):
        all_ref[j] = normal


def close(act, parts, copies, tok_atom):
    own, width = act.shape
    project = tok_atom is not None
    last = tok_atom.shape[1] if project else width
    return call(
        functools.partial(close_kernel, project),
        [
            jax.ShapeDtypeStruct((own, width), F32),
            jax.ShapeDtypeStruct((copies, own, last), BF16),
        ],
        act,
        *parts,
        *([tok_atom] if project else []),
        flops=10**7,
        moved=10**6,
    )


def key_source(rows, cols):
    nrow, ncol = lax.axis_size("row"), lax.axis_size("col")
    shares = rows // cols
    pairs = []
    for owner in range(nrow):
        free = [list(range(share, ncol, shares)) for share in range(shares)]
        for r in range(nrow):
            for share in range(shares):
                if r != owner:
                    spot = (2 * ((r + owner) % 2) + share) % (ncol // shares) * shares + share
                    source = spot if spot in free[share] else free[share][0]
                    free[share].remove(source)
                    pairs.append((owner * ncol + source, r * ncol + owner * shares + share))
    return pairs


def body(
    atom_feat,
    atom_token,
    window_start,
    token_cond,
    token_mask,
    pair,
    enc_in,
    enc_out,
    pool_weight,
    tok_in,
    tok_out,
    pair_weight,
    trans_in,
    trans_out,
    tok_atom,
    dec_in,
    dec_out,
    pos_out,
):
    nrow, ncol = lax.axis_size("row"), lax.axis_size("col")
    everyone = ("row", "col")
    count = nrow * ncol
    me_col = lax.axis_index("col")
    rows, width = token_cond.shape
    cols = pair.shape[1]
    heads = pair_weight.shape[2]
    own = rows // ncol
    atoms, afeat = atom_feat.shape
    natom = atoms * count
    nblk = atoms // QB

    hid = trans_out.shape[1]
    packed, feat = call(
        functools.partial(pack_kernel, rows),
        [
            jax.ShapeDtypeStruct((BLOCKS, 3 * hid, width), BF16),
            jax.ShapeDtypeStruct((atoms + EXTRA, afeat), BF16),
        ],
        jnp.swapaxes(trans_in, 2, 3),
        trans_out,
        atom_feat,
        atom_token[None],
        scalars=(window_start,),
        grant=60,
        moved=12 * trans_out.size,
    )

    up = [(i, i + 1) for i in range(count - 1)]
    prev = lax.ppermute(feat, everyone, up)
    after = lax.ppermute(feat, everyone, [(b, a) for a, b in up])

    across = lax.ppermute(packed, everyone, [(i, i ^ 2) for i in range(count)])
    sibling = lax.ppermute(packed, everyone, [(i, i ^ 1) for i in range(count)])

    ext, copies = call(
        functools.partial(encoder_kernel, natom),
        [
            jax.ShapeDtypeStruct((atoms + 2 * HALO, afeat), BF16),
            jax.ShapeDtypeStruct((ncol, atoms + EXTRA, afeat), BF16),
        ],
        feat,
        prev,
        after,
        enc_in,
        enc_out,
        flops=10**8,
        moved=10**6,
    )
    both = lax.all_to_all(copies, "col", 0, 0)

    span = -(-cols // 128) * 128
    weights = jnp.swapaxes(pair_weight, 1, 2).reshape(BLOCKS * heads, -1)
    step = 24
    bias = pl.pallas_call(
        bias_kernel,
        grid=(rows // step,),
        out_shape=[jax.ShapeDtypeStruct((rows, heads, span), F32)] * BLOCKS,
        in_specs=[
            pl.BlockSpec((step, cols, pair.shape[2]), lambda i: (i, 0, 0)),
            pl.BlockSpec(weights.shape, lambda i: (0, 0)),
        ],
        out_specs=[pl.BlockSpec((step, heads, span), lambda i: (i, 0, 0))] * BLOCKS,
        compiler_params=pltpu.CompilerParams(vmem_limit_bytes=56 * MIB),
        cost_estimate=pl.CostEstimate(flops=4 * 10**9, bytes_accessed=8 * 10**6, transcendentals=0),
    )(pair, weights)

    act, xn, send = call(
        pool_kernel,
        [
            jax.ShapeDtypeStruct((own, width), F32),
            jax.ShapeDtypeStruct((rows, width), BF16),
            jax.ShapeDtypeStruct((cols, width), BF16),
        ],
        both,
        pool_weight,
        token_cond,
        flops=10**9,
        moved=10**6,
    )

    pairs = key_source(rows, cols)
    share = me_col % (rows // cols)
    for layer in range(BLOCKS):
        if layer:
            send = lax.dynamic_slice_in_dim(xn, share * cols, cols, 0)
        came = lax.ppermute(send, everyone, pairs)
        query = call(
            functools.partial(query_kernel, layer),
            jax.ShapeDtypeStruct((rows, width), BF16),
            xn,
            far=(tok_in,),
            scratch=[pltpu.VMEM((width, width), BF16), pltpu.SemaphoreType.DMA((1,))],
            grant=60,
            flops=2 * rows * width * width,
            moved=2 * width * width,
        )
        message = call(
            functools.partial(attention_kernel, layer),
            jax.ShapeDtypeStruct((rows, width + span), BF16),
            scalars=(token_mask,),
            far=(query, send, came, bias[layer], tok_in),
            scratch=[pltpu.VMEM((cols, width), BF16)] * 2
            + [pltpu.VMEM((width, width), BF16)] * 2
            + [
                pltpu.VMEM((rows, width), BF16),
                pltpu.VMEM((rows, heads, span), F32),
                pltpu.SemaphoreType.DMA((6,)),
            ],
            grant=60,
            flops=10**9,
            moved=8 * 10**6,
        )
        if not layer:
            message, across = lax.optimization_barrier((message, across))
            beyond = lax.ppermute(across, everyone, [(i, i ^ 1) for i in range(count)])
            weights = (packed, sibling, across, beyond)
        message = lax.all_to_all(message.reshape(ncol, own, -1), "col", 0, 0)
        last = layer == BLOCKS - 1
        act, xn2 = mix(layer, message, act, tok_in, tok_out, heads)
        peers = ncol // 4
        shifts = [
            [(r * ncol + c, r * ncol + (c + 4 * d) % ncol) for r in range(nrow) for c in range(ncol)]
            for d in range(peers)
        ]
        back = [[(b, a) for a, b in pairs_of] for pairs_of in shifts]
        came_rows = [lax.ppermute(xn2, everyone, shifts[d]) for d in range(1, peers)]
        act, *parts = transition(layer, act, xn2, came_rows, weights)
        parts = [lax.ppermute(part, everyone, back[d]) for d, part in enumerate(parts, 1)]
        act, copies = close(act, parts, count if last else ncol, tok_atom if last else None)
        if not last:
            xn = lax.all_to_all(copies, "col", 0, 0).reshape(rows, width)
    proj = lax.all_to_all(copies, everyone, 0, 0).reshape(count * own, afeat)

    return call(
        functools.partial(decoder_kernel, natom, rows),
        jax.ShapeDtypeStruct((pos_out.shape[0], atoms), F32),
        ext,
        feat,
        prev,
        after,
        proj,
        dec_in,
        dec_out,
        pos_out,
        flops=10**8,
        moved=10**6,
    )


def solution(mesh):
    in_specs = (
        P(("row", "col"), None),
        P(("row", "col")),
        P(("row", "col")),
        P("row", None),
        P(),
        P("row", "col", None),
        P(),
        P(),
        P(),
        P(),
        P(),
        P(),
        P(None, None, None, "col"),
        P(None, "col", None),
        P(),
        P(),
        P(),
        P(),
    )
    out_specs = P(None, ("row", "col"))
    return jax.shard_map(body, mesh=mesh, in_specs=in_specs, out_specs=out_specs, check_vma=False)
```

```python
import functools
import math

import jax
import jax.numpy as jnp
from jax import lax
from jax.experimental import pallas as pl
from jax.experimental.pallas import tpu as pltpu
from jax.sharding import PartitionSpec as P

HA = 4
QB = 32
KW = 128
HALO = 64
BLOCKS = 2
EXTRA = 16
MIB = 1 << 20
F32 = jnp.float32
BF16 = jnp.bfloat16


def call(kernel, outs, *args, scalars=(), far=(), scratch=(), grant=8, flops=0, moved=0):
    smem = pl.BlockSpec(memory_space=pltpu.SMEM)
    vmem = pl.BlockSpec(memory_space=pltpu.VMEM)
    hbm = pl.BlockSpec(memory_space=pltpu.HBM)
    return pl.pallas_call(
        kernel,
        out_shape=outs,
        in_specs=[smem] * len(scalars) + [vmem] * len(args) + [hbm] * len(far),
        out_specs=jax.tree.map(lambda _: vmem, outs),
        scratch_shapes=list(scratch),
        compiler_params=pltpu.CompilerParams(vmem_limit_bytes=grant * MIB),
        cost_estimate=pl.CostEstimate(flops=flops, bytes_accessed=moved, transcendentals=0),
    )(*scalars, *args, *far)


def dot(a, b):
    return jnp.dot(a, b, preferred_element_type=F32)


def dot_nt(a, b):
    return lax.dot_general(a, b, (((1,), (1,)), ((), ())), preferred_element_type=F32)


def dot_tn(a, b):
    return lax.dot_general(a, b, (((0,), (0,)), ((), ())), preferred_element_type=F32)


def normed(x):
    x = x.astype(F32)
    cent = x - jnp.mean(x, -1, keepdims=True)
    var = jnp.mean(cent * cent, -1, keepdims=True)
    return cent * lax.rsqrt(var + 1e-05)


def iota(shape, dim):
    return lax.broadcasted_iota(jnp.int32, shape, dim)


def device():
    row, col = lax.axis_index("row"), lax.axis_index("col")
    return row, col, row * lax.axis_size("col") + col


def window_mask(shifts, first, natom, nkeys):
    shape = (len(shifts) * QB, nkeys)
    block = iota(shape, 0) // QB
    low = jnp.zeros(shape, jnp.int32)
    for i, shift in enumerate(shifts):
        low = jnp.where(block == i, shift + QB * i, low)
    key = iota(shape, 1)
    atom = key + first
    return (key >= low) & (key < low + KW) & (atom >= 0) & (atom < natom)


def attend(x, xn, gate, query, keys, vals, mask, w_out):
    width = x.shape[1]
    hsize = width // HA
    lane = iota((1, width), 1) // hsize
    outs = jnp.zeros(x.shape, F32)
    for h in range(HA):
        pick = (lane == h).astype(BF16)
        scores = dot_nt(query, keys * pick) * (1.0 / math.sqrt(hsize))
        scores = jnp.where(mask, scores, -1000000000.0)
        top = jnp.max(scores, -1, keepdims=True)
        expd = jnp.exp(scores - top)
        total = jnp.sum(expd, -1, keepdims=True)
        outs = outs + dot(expd.astype(BF16), vals * pick) / total
    gated = (jax.nn.sigmoid(gate) * outs).astype(BF16)
    return (x.astype(F32) + dot(gated, w_out)).astype(BF16)


def shifts_of(tail_ref, lanes):
    tail = tail_ref[tail_ref.shape[0] - EXTRA :, :].astype(F32)
    return [tail[1:2, k : k + 1].astype(jnp.int32) for k in lanes]


def encoder_kernel(natom, own_ref, prev_ref, next_ref, w_in, w_out, ext_ref, all_ref):
    rows = own_ref.shape[0] - EXTRA
    nblk = rows // QB
    half = HALO // QB
    x = jnp.concatenate([prev_ref[:rows], own_ref[:rows], next_ref[:rows]], 0)
    xn = normed(x).astype(BF16)
    keys = dot(xn, w_in[1]).astype(BF16)
    vals = dot(xn, w_in[2]).astype(BF16)
    qx, qn = x[HALO : 3 * rows - HALO], xn[HALO : 3 * rows - HALO]
    query = dot(qn, w_in[0]).astype(BF16)
    gate = dot(qn, w_in[3])
    shifts = (
        shifts_of(prev_ref, range(nblk - half, nblk))
        + shifts_of(own_ref, range(nblk))
        + shifts_of(next_ref, range(half))
    )
    first = device()[2] * rows - rows
    for part in range(2):
        mine = slice(part * rows, (part + 1) * rows)
        seen = slice(part * rows, (part + 2) * rows)
        mask = window_mask(
            shifts[part * nblk : (part + 1) * nblk], first + part * rows, natom, 2 * rows
        )
        ext_ref[mine] = attend(
            qx[mine], qn[mine], gate[mine], query[mine], keys[seen], vals[seen], mask, w_out[...]
        )
    new = ext_ref[HALO : HALO + rows]
    tail = own_ref[rows:]
    for j in range(all_ref.shape[0]):
        all_ref[j, :rows] = new
        all_ref[j, rows:] = tail


def pool_kernel(both_ref, weight, cond, act_ref, xn_ref, send_ref):
    count, rows = both_ref.shape[0], both_ref.shape[1] - EXTRA
    tokens = cond.shape[0]
    sums = jnp.zeros(cond.shape, F32)
    counts = jnp.zeros((tokens, 1), F32)
    step = 4 if count % 4 == 0 else 1
    for j in range(0, count, step):
        atoms = jnp.concatenate([both_ref[j + k, :rows] for k in range(step)], 0)
        feats = jnp.maximum(dot(atoms, weight[...]), 0.0).astype(BF16)
        spot = jnp.concatenate(
            [both_ref[j + k, rows:].astype(F32)[0:1] for k in range(step)], 1
        ).astype(jnp.int32)
        onehot = (iota((tokens, step * rows), 0) == spot).astype(F32)
        sums = sums + dot(onehot.astype(BF16), feats)
        counts = counts + jnp.sum(onehot, -1, keepdims=True)
    act = sums / counts + cond[...].astype(F32)
    xn = normed(act)
    xn_ref[...] = xn.astype(BF16)
    cols = send_ref.shape[0]
    part = xn[:cols]
    for k in range(1, tokens // cols):
        part = jnp.where(device()[1] % (tokens // cols) == k, xn[k * cols : (k + 1) * cols], part)
    send_ref[...] = part.astype(BF16)
    own = act_ref.shape[0]
    col = device()[1]
    mine = act[:own]
    for c in range(1, tokens // own):
        mine = jnp.where(col == c, act[c * own : (c + 1) * own], mine)
    act_ref[...] = mine


def decoder_kernel(
    natom, x1_ref, own_ref, prev_ref, next_ref, proj_ref, *refs
):
    *edges, w_in, w_out, pos, out = refs
    rows = own_ref.shape[0] - EXTRA
    proj = proj_ref[...].astype(F32)
    tokens = proj.shape[0]
    _, col, me = device()
    edges = [edge[...].astype(F32) for edge in edges]
    reach = len(edges) * edges[0].shape[0]
    rest = tokens - reach
    edge_low = jnp.where(col == 0, jnp.concatenate(edges[::-1], 0), proj[rest:])
    edge_high = jnp.where(
        col == lax.axis_size("col") - 1, jnp.concatenate(edges, 0), proj[:reach]
    )
    tables = (
        jnp.concatenate([proj[:rest], edge_low], 0),
        proj,
        jnp.concatenate([edge_high, proj[reach:]], 0),
    )
    spread = []
    for table, ref in zip(tables, (prev_ref, own_ref, next_ref)):
        spot = ref[rows:].astype(F32)[0:1].astype(jnp.int32)
        onehot = (iota((tokens, rows), 0) == spot).astype(F32).astype(BF16)
        spread.append(dot_tn(onehot, table.astype(BF16)))
    spread = jnp.concatenate([spread[0][rows - HALO :], spread[1], spread[2][:HALO]], 0)
    x = (x1_ref[...].astype(F32) + spread).astype(BF16)
    xn = normed(x).astype(BF16)
    keys = dot(xn, w_in[1]).astype(BF16)
    vals = dot(xn, w_in[2]).astype(BF16)
    qx, qn = x[HALO : HALO + rows], xn[HALO : HALO + rows]
    query = dot(qn, w_in[0]).astype(BF16)
    gate = dot(qn, w_in[3])
    shifts = shifts_of(own_ref, range(rows // QB))
    mask = window_mask(shifts, me * rows - HALO, natom, 2 * rows)
    third = attend(qx, qn, gate, query, keys, vals, mask, w_out[...])
    out[...] = dot_nt(pos[...], normed(third).astype(BF16))


def feat_kernel(row_tokens, starts, feat, token, own):
    rows, width = feat.shape
    row, _, me = device()
    nblk = starts.shape[0]
    lane = iota((EXTRA, width), 1)
    line = iota((EXTRA, width), 0)
    tail = jnp.where(line == 0, token[...] - row * row_tokens, 0)
    for k in range(nblk):
        shift = starts[k] - QB * (me * nblk + k) + HALO
        tail = jnp.where((line == 1) & (lane == k), shift, tail)
    own[:rows] = feat[...]
    own[rows:] = tail.astype(F32).astype(BF16)


def pack_kernel(first, second, upper, lower, *outs):
    hid = second.shape[1]
    half = upper.shape[0]
    for layer, out in enumerate(outs):
        out[:hid] = first[layer, 0]
        out[hid : 2 * hid] = first[layer, 1]
        out[2 * hid :] = second[layer]
    upper[...] = outs[0][:half]
    lower[...] = outs[0][half:]


def bias_kernel(pair_ref, weight, *outs):
    rows, cols, _ = pair_ref.shape
    _, heads, pad = outs[0].shape
    pad = pad - cols

    for q in range(rows):
        bias = dot_nt(weight[...], pair_ref[q])
        bias = jnp.concatenate([bias, jnp.zeros((bias.shape[0], pad), F32)], 1)
        for layer, out in enumerate(outs):
            out[q] = bias[layer * heads : (layer + 1) * heads]


def prepare(sources, targets, sems):
    return [
        pltpu.make_async_copy(source, target, sems.at[i])
        for i, (source, target) in enumerate(zip(sources, targets))
    ]


def query_kernel(
    layer, xn_ref, act_ref, w_in, query, w_key, w_val, gate, w_query, w_gate, sems
):
    fetches = prepare(
        [w_in.at[layer, k] for k in range(4)], [w_query, w_key, w_val, w_gate], sems
    )
    for k in (0, 3, 1, 2):
        fetches[k].start()
    fetches[0].wait()
    query[...] = dot(xn_ref[...], w_query[...]).astype(BF16)
    fetches[3].wait()
    gate[...] = jax.nn.sigmoid(dot(normed(act_ref[...]).astype(BF16), w_gate[...]))
    fetches[1].wait()
    fetches[2].wait()


def attention_kernel(mask_ref, query, here_ref, came_ref, low, high, w_key, w_val, out_ref):
    rows, width = query.shape
    cols = here_ref.shape[0]
    heads = low.shape[1]
    hsize = width // heads
    span = low.shape[2]
    row, col, _ = device()
    mine = col * cols // rows == row
    key_xn = jnp.where(mine, here_ref[...].astype(F32), came_ref[...].astype(F32))
    key_xn = jnp.concatenate([key_xn, jnp.zeros((span - cols, width), F32)], 0).astype(BF16)
    keys = dot(key_xn, w_key[...]).astype(BF16)
    vals = dot(key_xn, w_val[...]).astype(BF16)
    tokens = mask_ref.shape[0]
    count = jnp.int32(0)
    for bit in range(tokens.bit_length() - 1, -1, -1):
        longer = count + (1 << bit)
        inside = longer <= tokens
        last = mask_ref[jnp.where(inside, longer - 1, 0)]
        count = jnp.where(inside & (last == 1), longer, count)
    valid = iota((1, span), 1) + col * cols < count
    valid = valid & (iota((1, span), 1) < cols)
    group = heads // 2
    part = group * hsize
    lane = iota((1, part), 1) // hsize
    spot = iota((1, span), 1)
    levels = jnp.zeros((rows, span), F32)
    for g in range(2):
        wide = slice(g * part, (g + 1) * part)
        kg, vg = keys[:, wide], vals[:, wide]
        picks = [(lane == h).astype(BF16) for h in range(group)]
        stacked = jnp.concatenate([kg * p for p in picks], 0)
        scores = dot_nt(query[:, wide], stacked) * (1.0 / math.sqrt(hsize))
        probs = []
        for h in range(group):
            head = g * group + h
            bias = jnp.concatenate([low[:, head, :], high[:, head, :]], 0)
            score = scores[:, h * span : (h + 1) * span] + bias
            score = jnp.where(valid, score, -1000000000.0)
            top = jnp.max(score, -1, keepdims=True)
            expd = jnp.exp(score - top)
            total = jnp.sum(expd, -1, keepdims=True)
            probs.append((expd / total).astype(BF16))
            levels = jnp.where(spot % heads == head, top + jnp.log(total), levels)
        stacked = jnp.concatenate([vg * p for p in picks], 0)
        out_ref[:, wide] = dot(jnp.concatenate(probs, 1), stacked).astype(BF16)
    high = levels.astype(BF16).astype(F32)
    rest = levels - high
    middle = rest.astype(BF16).astype(F32)
    low = rest - middle
    packed = jnp.where(spot < heads, high, jnp.where(spot < 2 * heads, middle, low))
    out_ref[:, width:] = jnp.where(spot < 3 * heads, packed, 0.0).astype(BF16)


def mix_kernel(layer, heads, message, act_ref, gate, w_out, act_out, xn2_out, w_mix, sems):
    (copy,) = prepare([w_out.at[layer]], [w_mix], sems)
    copy.start()
    width = act_ref.shape[1]
    hsize = width // heads
    parts = [message[j, :, width:].astype(F32) for j in range(message.shape[0])]
    span = parts[0].shape[1]
    levels = [
        p + pltpu.roll(p, span - heads, 1) + pltpu.roll(p, span - 2 * heads, 1) for p in parts
    ]
    top = functools.reduce(jnp.maximum, levels)
    weights = [jnp.exp(level - top) for level in levels]
    whole = functools.reduce(jnp.add, weights)
    lane = iota((1, span), 1)
    row = iota((span, width), 0)
    expand = (row % heads == iota((span, width), 1) // hsize) & (row < 2 * heads)
    expand = expand.astype(F32).astype(BF16)
    packed = []
    for weight in weights:
        weight = weight / whole
        high = weight.astype(BF16).astype(F32)
        both = jnp.where(lane < heads, high, pltpu.roll(weight - high, heads, 1))
        packed.append(jnp.where(lane < 2 * heads, both, 0.0))
    spread = dot(jnp.concatenate(packed, 0).astype(BF16), expand)
    own = act_ref.shape[0]
    attn = jnp.zeros(act_ref.shape, F32)
    for j in range(message.shape[0]):
        attn = attn + spread[j * own : (j + 1) * own] * message[j, :, :width].astype(F32)
    gated = (gate[...] * attn).astype(BF16)
    copy.wait()
    act = act_ref[...] + dot(gated, w_mix[...])
    act_out[...] = act
    xn2_out[...] = normed(act).astype(BF16)


def mix(layer, message, act, gate, w_out, heads):
    own, width = act.shape
    return call(
        functools.partial(mix_kernel, layer, heads),
        [jax.ShapeDtypeStruct((own, width), F32), jax.ShapeDtypeStruct((own, width), BF16)],
        message,
        act,
        gate,
        far=(w_out,),
        scratch=[pltpu.VMEM((width, width), BF16), pltpu.SemaphoreType.DMA((1,))],
        grant=48,
        flops=4 * own * width * width,
        moved=4 * width * width,
    )


def transition_kernel(groups, pieces, act_ref, xn2, *refs):
    others, refs = refs[: groups - 1], refs[groups - 1 :]
    sources = []
    for number in pieces:
        sources.append(refs[:number])
        refs = refs[number:]
    outs, (w_first, w_second, sems) = refs[:groups], refs[groups:]
    count, hid = w_second.shape[:2]
    plan = []
    for wanted, target in (((0, 2 * hid), w_first), ((2 * hid, 3 * hid), w_second)):
        for j, source in enumerate(sources):
            begin = 0
            for ref in source:
                end = begin + ref.shape[0]
                low, high = max(begin, wanted[0]), min(end, wanted[1])
                if low < high:
                    near = target.at[j, pl.ds(low - wanted[0], high - low)]
                    plan.append((target is w_first, j, ref.at[pl.ds(low - begin, high - low)], near))
                begin = end
    fetches = prepare([item[2] for item in plan], [item[3] for item in plan], sems)
    for copy in fetches:
        copy.start()

    def arrived(first, j):
        for item, copy in zip(plan, fetches):
            if item[:2] == (first, j):
                copy.wait()

    own = act_ref.shape[0]
    rows = jnp.concatenate([ref[...].astype(F32) for ref in (xn2, *others)], 0).astype(BF16)
    total = jnp.zeros((rows.shape[0], rows.shape[1]), F32)
    hidden = []
    for j in range(count):
        arrived(True, j)
        both = dot_nt(rows, w_first[j])
        left, right = both[:, :hid], both[:, hid:]
        hidden.append((left * jax.nn.sigmoid(left) * right).astype(BF16))
    for j in range(count):
        arrived(False, j)
        total = total + dot(hidden[j], w_second[j])
    outs[0][...] = act_ref[...] + total[:own]
    for k, out in enumerate(outs[1:], 1):
        out[...] = total[k * own : (k + 1) * own].astype(BF16)


def transition(act, xn2, others, weights):
    own, width = act.shape
    blocks = len(weights)
    hid = sum(part.shape[0] for part in weights[0]) // 3
    parts = [part for source in weights for part in source]
    return call(
        functools.partial(transition_kernel, len(others) + 1, [len(source) for source in weights]),
        [jax.ShapeDtypeStruct((own, width), F32)]
        + [jax.ShapeDtypeStruct((own, width), BF16)] * len(others),
        act,
        xn2,
        *others,
        far=parts,
        scratch=[
            pltpu.VMEM((blocks, 2 * hid, width), BF16),
            pltpu.VMEM((blocks, hid, width), BF16),
            pltpu.SemaphoreType.DMA((2 * len(parts),)),
        ],
        grant=48,
        flops=12 * own * hid * width * blocks,
        moved=6 * hid * width * blocks,
    )


def close_kernel(project, act_ref, *refs):
    *refs, act_out, all_ref = refs
    if project:
        *refs, tok_atom = refs
    act = act_ref[...]
    for ref in refs:
        act = act + ref[...].astype(F32)
    act_out[...] = act
    normal = normed(act).astype(BF16)
    if project:
        normal = dot(normal, tok_atom[...]).astype(BF16)
    for j in range(all_ref.shape[0]):
        all_ref[j] = normal


def close(act, parts, copies, tok_atom):
    own, width = act.shape
    project = tok_atom is not None
    last = tok_atom.shape[1] if project else width
    return call(
        functools.partial(close_kernel, project),
        [
            jax.ShapeDtypeStruct((own, width), F32),
            jax.ShapeDtypeStruct((copies, own, last), BF16),
        ],
        act,
        *parts,
        *([tok_atom] if project else []),
        flops=10**7,
        moved=10**6,
    )


def key_source(rows, cols):
    nrow, ncol = lax.axis_size("row"), lax.axis_size("col")
    shares = rows // cols
    pairs = []
    for owner in range(nrow):
        free = [list(range(share, ncol, shares)) for share in range(shares)]
        for r in range(nrow):
            for share in range(shares):
                if r != owner:
                    spot = (2 * ((r + owner) % 2) + share) % (ncol // shares) * shares + share
                    source = spot if spot in free[share] else free[share][0]
                    free[share].remove(source)
                    pairs.append((owner * ncol + source, r * ncol + owner * shares + share))
    return pairs


def body(
    atom_feat,
    atom_token,
    window_start,
    token_cond,
    token_mask,
    pair,
    enc_in,
    enc_out,
    pool_weight,
    tok_in,
    tok_out,
    pair_weight,
    trans_in,
    trans_out,
    tok_atom,
    dec_in,
    dec_out,
    pos_out,
):
    nrow, ncol = lax.axis_size("row"), lax.axis_size("col")
    everyone = ("row", "col")
    count = nrow * ncol
    me_col = lax.axis_index("col")
    rows, width = token_cond.shape
    cols = pair.shape[1]
    heads = pair_weight.shape[2]
    own = rows // ncol
    atoms, afeat = atom_feat.shape
    natom = atoms * count
    nblk = atoms // QB

    hid = trans_out.shape[1]
    feat = call(
        functools.partial(feat_kernel, rows),
        jax.ShapeDtypeStruct((atoms + EXTRA, afeat), BF16),
        atom_feat,
        atom_token[None],
        scalars=(window_start,),
        grant=48,
        moved=10**5,
    )
    up = [(i, i + 1) for i in range(count - 1)]
    prev = lax.ppermute(feat, everyone, up)
    after = lax.ppermute(feat, everyone, [(b, a) for a, b in up])
    _, first_part, second_part = lax.optimization_barrier(
        (feat, jnp.swapaxes(trans_in, 2, 3), trans_out)
    )
    matrix = jax.ShapeDtypeStruct((3 * hid, width), BF16)
    piece = jax.ShapeDtypeStruct((3 * hid // 2, width), BF16)
    upper, lower, *packed = call(
        pack_kernel,
        [piece, piece] + [matrix] * BLOCKS,
        first_part,
        second_part,
        grant=48,
        moved=12 * trans_out.size,
    )
    prev, after, upper = lax.optimization_barrier((prev, after, upper))
    neighbour = [(i, i ^ 2) for i in range(count)]
    sibling = [(i, i ^ 1) for i in range(count)]
    across = [[lax.ppermute(upper, everyone, neighbour)], []]

    ext, copies = call(
        functools.partial(encoder_kernel, natom),
        [
            jax.ShapeDtypeStruct((atoms + 2 * HALO, afeat), BF16),
            jax.ShapeDtypeStruct((ncol, atoms + EXTRA, afeat), BF16),
        ],
        feat,
        prev,
        after,
        enc_in,
        enc_out,
        flops=10**8,
        moved=10**6,
    )
    span = -(-cols // 128) * 128
    half = rows // 2
    step = 24

    def bias_of(part, weights):
        return pl.pallas_call(
            bias_kernel,
            grid=(half // step,),
            out_shape=[jax.ShapeDtypeStruct((half, heads, span), F32)] * BLOCKS,
            in_specs=[
                pl.BlockSpec(
                    (step, cols, pair.shape[2]), lambda i: (i + part * (half // step), 0, 0)
                ),
                pl.BlockSpec(weights.shape, lambda i: (0, 0)),
            ],
            out_specs=[pl.BlockSpec((step, heads, span), lambda i: (i, 0, 0))] * BLOCKS,
            compiler_params=pltpu.CompilerParams(vmem_limit_bytes=(52 if part else 60) * MIB),
            cost_estimate=pl.CostEstimate(
                flops=2 * 10**9, bytes_accessed=4 * 10**6, transcendentals=0
            ),
        )(pair, weights)

    weights = jnp.swapaxes(pair_weight, 1, 2).reshape(BLOCKS * heads, -1)
    copies, first_weights = lax.optimization_barrier((copies, weights))
    low = bias_of(0, first_weights)
    both = lax.all_to_all(copies, "col", 0, 0)
    both, low, across[0][0] = lax.optimization_barrier((both, low, across[0][0]))

    act, xn, send = call(
        pool_kernel,
        [
            jax.ShapeDtypeStruct((own, width), F32),
            jax.ShapeDtypeStruct((rows, width), BF16),
            jax.ShapeDtypeStruct((cols, width), BF16),
        ],
        both,
        pool_weight,
        token_cond,
        flops=10**9,
        moved=10**6,
    )

    pairs = key_source(rows, cols)
    share = me_col % (rows // cols)
    peers = ncol // 4
    shifts = [
        [(r * ncol + c, r * ncol + (c + 4 * d) % ncol) for r in range(nrow) for c in range(ncol)]
        for d in range(peers)
    ]
    back = [[(b, a) for a, b in pairs_of] for pairs_of in shifts]
    xn, weights = lax.optimization_barrier((xn, weights))
    beside, beyond = [], [[], []]
    for layer in range(BLOCKS):
        last = layer == BLOCKS - 1
        if layer:
            send = lax.dynamic_slice_in_dim(xn, share * cols, cols, 0)
            send, xn, ready = lax.optimization_barrier((send, xn, across[1][0]))
        came = lax.ppermute(send, everyone, pairs)
        matrix = jax.ShapeDtypeStruct((width, width), BF16)
        query, w_key, w_val, gate = call(
            functools.partial(query_kernel, layer),
            [
                jax.ShapeDtypeStruct((rows, width), BF16),
                matrix,
                matrix,
                jax.ShapeDtypeStruct((own, width), F32),
            ],
            xn,
            act,
            far=(tok_in,),
            scratch=[pltpu.VMEM((width, width), BF16)] * 2 + [pltpu.SemaphoreType.DMA((4,))],
            grant=48,
            flops=2 * rows * width * width,
            moved=8 * width * width,
        )
        if not layer:
            high = list(bias_of(1, weights))
            high[0], lower, *ready = lax.optimization_barrier(
                (high[0], lower, across[0][0], *packed)
            )
            across[0].append(lax.ppermute(lower, everyone, neighbour))
            beyond[0].append(lax.ppermute(ready[0], everyone, sibling))
            beside = [lax.ppermute(part, everyone, sibling) for part in ready[1:]]
        else:
            beyond[1].append(lax.ppermute(ready, everyone, sibling))
        message = call(
            attention_kernel,
            jax.ShapeDtypeStruct((rows, width + span), BF16),
            query,
            send,
            came,
            low[layer],
            high[layer],
            w_key,
            w_val,
            scalars=(token_mask,),
            grant=16,
            flops=10**9,
            moved=8 * 10**6,
        )
        message = lax.all_to_all(message.reshape(ncol, own, -1), "col", 0, 0)
        if not layer:
            message, ready = lax.optimization_barrier((message, packed[1]))
            across[1].append(lax.ppermute(ready, everyone, neighbour))
        act, xn2 = mix(layer, message, act, gate, tok_out, heads)
        came_rows = [lax.ppermute(xn2, everyone, shifts[d]) for d in range(1, peers)]
        if not layer:
            xn2, ready = lax.optimization_barrier((xn2, across[0][1]))
            beyond[0].append(lax.ppermute(ready, everyone, sibling))
        act, *parts = transition(
            act, xn2, came_rows, ([packed[layer]], [beside[layer]], across[layer], beyond[layer])
        )
        parts = [lax.ppermute(part, everyone, back[d]) for d, part in enumerate(parts, 1)]
        act, copies = close(act, parts, ncol, tok_atom if last else None)
        if last:
            reach = -(-HALO // own)
            edges = []
            for d in range(reach):
                edge = [(r * ncol + ncol - 1 - d, (r + 1) * ncol) for r in range(nrow - 1)]
                edge += [(r * ncol + d, r * ncol - 1) for r in range(1, nrow)]
                edges.append(lax.ppermute(copies[0], everyone, edge))
        gathered = lax.all_to_all(copies, "col", 0, 0).reshape(rows, -1)
        if not last:
            xn = gathered

    return call(
        functools.partial(decoder_kernel, natom),
        jax.ShapeDtypeStruct((pos_out.shape[0], atoms), F32),
        ext,
        feat,
        prev,
        after,
        gathered,
        *edges,
        dec_in,
        dec_out,
        pos_out,
        flops=10**8,
        moved=10**6,
    )


def solution(mesh):
    in_specs = (
        P(("row", "col"), None),
        P(("row", "col")),
        P(("row", "col")),
        P("row", None),
        P(),
        P("row", "col", None),
        P(),
        P(),
        P(),
        P(),
        P(),
        P(),
        P(None, None, None, "col"),
        P(None, "col", None),
        P(),
        P(),
        P(),
        P(),
    )
    out_specs = P(None, ("row", "col"))
    return jax.shard_map(body, mesh=mesh, in_specs=in_specs, out_specs=out_specs, check_vma=False)
```

```python
import functools
import math

import jax
import jax.numpy as jnp
from jax import lax
from jax.experimental import pallas as pl
from jax.experimental.pallas import tpu as pltpu
from jax.sharding import PartitionSpec as P

HA = 4
QB = 32
KW = 128
HALO = 64
BLOCKS = 2
EXTRA = 16
MIB = 1 << 20
F32 = jnp.float32
BF16 = jnp.bfloat16


def call(kernel, outs, *args, scalars=(), far=(), scratch=(), grant=8, flops=0, moved=0):
    smem = pl.BlockSpec(memory_space=pltpu.SMEM)
    vmem = pl.BlockSpec(memory_space=pltpu.VMEM)
    hbm = pl.BlockSpec(memory_space=pltpu.HBM)
    return pl.pallas_call(
        kernel,
        out_shape=outs,
        in_specs=[smem] * len(scalars) + [vmem] * len(args) + [hbm] * len(far),
        out_specs=jax.tree.map(lambda _: vmem, outs),
        scratch_shapes=list(scratch),
        compiler_params=pltpu.CompilerParams(vmem_limit_bytes=grant * MIB),
        cost_estimate=pl.CostEstimate(flops=flops, bytes_accessed=moved, transcendentals=0),
    )(*scalars, *args, *far)


def dot(a, b):
    return jnp.dot(a, b, preferred_element_type=F32)


def dot_nt(a, b):
    return lax.dot_general(a, b, (((1,), (1,)), ((), ())), preferred_element_type=F32)


def dot_tn(a, b):
    return lax.dot_general(a, b, (((0,), (0,)), ((), ())), preferred_element_type=F32)


def normed(x):
    x = x.astype(F32)
    cent = x - jnp.mean(x, -1, keepdims=True)
    var = jnp.mean(cent * cent, -1, keepdims=True)
    return cent * lax.rsqrt(var + 1e-05)


def iota(shape, dim):
    return lax.broadcasted_iota(jnp.int32, shape, dim)


def device():
    row, col = lax.axis_index("row"), lax.axis_index("col")
    return row, col, row * lax.axis_size("col") + col


def window_mask(shifts, first, natom, nkeys):
    shape = (len(shifts) * QB, nkeys)
    block = iota(shape, 0) // QB
    low = jnp.zeros(shape, jnp.int32)
    for i, shift in enumerate(shifts):
        low = jnp.where(block == i, shift + QB * i, low)
    key = iota(shape, 1)
    atom = key + first
    return (key >= low) & (key < low + KW) & (atom >= 0) & (atom < natom)


def attend(x, xn, gate, query, keys, vals, mask, w_out):
    width = x.shape[1]
    hsize = width // HA
    lane = iota((1, width), 1) // hsize
    outs = jnp.zeros(x.shape, F32)
    for h in range(HA):
        pick = (lane == h).astype(BF16)
        scores = dot_nt(query, keys * pick) * (1.0 / math.sqrt(hsize))
        scores = jnp.where(mask, scores, -1000000000.0)
        top = jnp.max(scores, -1, keepdims=True)
        expd = jnp.exp(scores - top)
        total = jnp.sum(expd, -1, keepdims=True)
        outs = outs + dot(expd.astype(BF16), vals * pick) / total
    gated = (jax.nn.sigmoid(gate) * outs).astype(BF16)
    return (x.astype(F32) + dot(gated, w_out)).astype(BF16)


def shifts_of(tail_ref, lanes):
    tail = tail_ref[tail_ref.shape[0] - EXTRA :, :].astype(F32)
    return [tail[1:2, k : k + 1].astype(jnp.int32) for k in lanes]


def encoder_kernel(natom, own_ref, prev_ref, next_ref, w_in, w_out, ext_ref, all_ref):
    rows = own_ref.shape[0] - EXTRA
    nblk = rows // QB
    half = HALO // QB
    x = jnp.concatenate([prev_ref[:rows], own_ref[:rows], next_ref[:rows]], 0)
    xn = normed(x).astype(BF16)
    keys = dot(xn, w_in[1]).astype(BF16)
    vals = dot(xn, w_in[2]).astype(BF16)
    qx, qn = x[HALO : 3 * rows - HALO], xn[HALO : 3 * rows - HALO]
    query = dot(qn, w_in[0]).astype(BF16)
    gate = dot(qn, w_in[3])
    shifts = (
        shifts_of(prev_ref, range(nblk - half, nblk))
        + shifts_of(own_ref, range(nblk))
        + shifts_of(next_ref, range(half))
    )
    first = device()[2] * rows - rows
    for part in range(2):
        mine = slice(part * rows, (part + 1) * rows)
        seen = slice(part * rows, (part + 2) * rows)
        mask = window_mask(
            shifts[part * nblk : (part + 1) * nblk], first + part * rows, natom, 2 * rows
        )
        ext_ref[mine] = attend(
            qx[mine], qn[mine], gate[mine], query[mine], keys[seen], vals[seen], mask, w_out[...]
        )
    new = ext_ref[HALO : HALO + rows]
    tail = own_ref[rows:]
    for j in range(all_ref.shape[0]):
        all_ref[j, :rows] = new
        all_ref[j, rows:] = tail


def pool_kernel(both_ref, weight, cond, act_ref, xn_ref, send_ref):
    count, rows = both_ref.shape[0], both_ref.shape[1] - EXTRA
    tokens = cond.shape[0]
    sums = jnp.zeros(cond.shape, F32)
    counts = jnp.zeros((tokens, 1), F32)
    step = 4 if count % 4 == 0 else 1
    for j in range(0, count, step):
        atoms = jnp.concatenate([both_ref[j + k, :rows] for k in range(step)], 0)
        feats = jnp.maximum(dot(atoms, weight[...]), 0.0).astype(BF16)
        spot = jnp.concatenate(
            [both_ref[j + k, rows:].astype(F32)[0:1] for k in range(step)], 1
        ).astype(jnp.int32)
        onehot = (iota((tokens, step * rows), 0) == spot).astype(F32)
        sums = sums + dot(onehot.astype(BF16), feats)
        counts = counts + jnp.sum(onehot, -1, keepdims=True)
    act = sums / counts + cond[...].astype(F32)
    xn = normed(act)
    xn_ref[...] = xn.astype(BF16)
    cols = send_ref.shape[0]
    part = xn[:cols]
    for k in range(1, tokens // cols):
        part = jnp.where(device()[1] % (tokens // cols) == k, xn[k * cols : (k + 1) * cols], part)
    send_ref[...] = part.astype(BF16)
    own = act_ref.shape[0]
    col = device()[1]
    mine = act[:own]
    for c in range(1, tokens // own):
        mine = jnp.where(col == c, act[c * own : (c + 1) * own], mine)
    act_ref[...] = mine


def decoder_kernel(
    natom, row_tokens, x1_ref, own_ref, prev_ref, next_ref, proj, w_in, w_out, pos, out
):
    rows = own_ref.shape[0] - EXTRA
    tokens = proj.shape[0]
    me = device()[2]
    spread = []
    for k, ref in enumerate((prev_ref, own_ref, next_ref)):
        spot = ref[rows:].astype(F32)[0:1].astype(jnp.int32)
        spot = spot + (me + k - 1) // lax.axis_size("col") * row_tokens
        onehot = (iota((tokens, rows), 0) == spot).astype(F32).astype(BF16)
        spread.append(dot_tn(onehot, proj[...]))
    spread = jnp.concatenate([spread[0][rows - HALO :], spread[1], spread[2][:HALO]], 0)
    x = (x1_ref[...].astype(F32) + spread).astype(BF16)
    xn = normed(x).astype(BF16)
    keys = dot(xn, w_in[1]).astype(BF16)
    vals = dot(xn, w_in[2]).astype(BF16)
    qx, qn = x[HALO : HALO + rows], xn[HALO : HALO + rows]
    query = dot(qn, w_in[0]).astype(BF16)
    gate = dot(qn, w_in[3])
    shifts = shifts_of(own_ref, range(rows // QB))
    mask = window_mask(shifts, me * rows - HALO, natom, 2 * rows)
    third = attend(qx, qn, gate, query, keys, vals, mask, w_out[...])
    out[...] = dot_nt(pos[...], normed(third).astype(BF16))


def feat_kernel(row_tokens, starts, feat, token, own):
    rows, width = feat.shape
    row, _, me = device()
    nblk = starts.shape[0]
    lane = iota((EXTRA, width), 1)
    line = iota((EXTRA, width), 0)
    tail = jnp.where(line == 0, token[...] - row * row_tokens, 0)
    for k in range(nblk):
        shift = starts[k] - QB * (me * nblk + k) + HALO
        tail = jnp.where((line == 1) & (lane == k), shift, tail)
    own[:rows] = feat[...]
    own[rows:] = tail.astype(F32).astype(BF16)


def pack_kernel(first, second, upper, lower, *outs):
    hid = second.shape[1]
    part = upper.shape[0]
    for layer, out in enumerate(outs):
        out[:hid] = first[layer, 0]
        out[hid : 2 * hid] = first[layer, 1]
        out[2 * hid :] = second[layer]
    upper[...] = outs[0][:part]
    lower[...] = outs[0][part:]


def bias_kernel(pair_ref, weight, *outs):
    rows, cols, _ = pair_ref.shape
    _, heads, pad = outs[0].shape
    pad = pad - cols

    for q in range(rows):
        bias = dot_nt(weight[...], pair_ref[q])
        bias = jnp.concatenate([bias, jnp.zeros((bias.shape[0], pad), F32)], 1)
        for layer, out in enumerate(outs):
            out[q] = bias[layer * heads : (layer + 1) * heads]


def prepare(sources, targets, sems):
    return [
        pltpu.make_async_copy(source, target, sems.at[i])
        for i, (source, target) in enumerate(zip(sources, targets))
    ]


def query_kernel(
    layer, xn_ref, act_ref, w_in, query, w_key, w_val, gate, w_query, w_gate, sems
):
    fetches = prepare(
        [w_in.at[layer, k] for k in range(4)], [w_query, w_key, w_val, w_gate], sems
    )
    for k in (0, 3, 1, 2):
        fetches[k].start()
    fetches[0].wait()
    query[...] = dot(xn_ref[...], w_query[...]).astype(BF16)
    fetches[3].wait()
    gate[...] = jax.nn.sigmoid(dot(normed(act_ref[...]).astype(BF16), w_gate[...]))
    fetches[1].wait()
    fetches[2].wait()


def attention_kernel(mask_ref, query, here_ref, came_ref, low, high, w_key, w_val, out_ref):
    rows, width = query.shape
    cols = here_ref.shape[0]
    heads = low.shape[1]
    hsize = width // heads
    span = low.shape[2]
    row, col, _ = device()
    mine = col * cols // rows == row
    key_xn = jnp.where(mine, here_ref[...].astype(F32), came_ref[...].astype(F32))
    key_xn = jnp.concatenate([key_xn, jnp.zeros((span - cols, width), F32)], 0).astype(BF16)
    keys = dot(key_xn, w_key[...]).astype(BF16)
    vals = dot(key_xn, w_val[...]).astype(BF16)
    tokens = mask_ref.shape[0]
    count = jnp.int32(0)
    for bit in range(tokens.bit_length() - 1, -1, -1):
        longer = count + (1 << bit)
        inside = longer <= tokens
        last = mask_ref[jnp.where(inside, longer - 1, 0)]
        count = jnp.where(inside & (last == 1), longer, count)
    valid = iota((1, span), 1) + col * cols < count
    valid = valid & (iota((1, span), 1) < cols)
    group = heads // 2
    part = group * hsize
    lane = iota((1, part), 1) // hsize
    spot = iota((1, span), 1)
    levels = jnp.zeros((rows, span), F32)
    for g in range(2):
        wide = slice(g * part, (g + 1) * part)
        kg, vg = keys[:, wide], vals[:, wide]
        picks = [(lane == h).astype(BF16) for h in range(group)]
        stacked = jnp.concatenate([kg * p for p in picks], 0)
        scores = dot_nt(query[:, wide], stacked) * (1.0 / math.sqrt(hsize))
        probs = []
        for h in range(group):
            head = g * group + h
            bias = jnp.concatenate([low[:, head, :], high[:, head, :]], 0)
            score = scores[:, h * span : (h + 1) * span] + bias
            score = jnp.where(valid, score, -1000000000.0)
            top = jnp.max(score, -1, keepdims=True)
            expd = jnp.exp(score - top)
            total = jnp.sum(expd, -1, keepdims=True)
            probs.append((expd / total).astype(BF16))
            levels = jnp.where(spot % heads == head, top + jnp.log(total), levels)
        stacked = jnp.concatenate([vg * p for p in picks], 0)
        out_ref[:, wide] = dot(jnp.concatenate(probs, 1), stacked).astype(BF16)
    high = levels.astype(BF16).astype(F32)
    rest = levels - high
    middle = rest.astype(BF16).astype(F32)
    low = rest - middle
    packed = jnp.where(spot < heads, high, jnp.where(spot < 2 * heads, middle, low))
    out_ref[:, width:] = jnp.where(spot < 3 * heads, packed, 0.0).astype(BF16)


def mix_kernel(layer, heads, message, act_ref, gate, w_out, act_out, xn2_out, w_mix, sems):
    (copy,) = prepare([w_out.at[layer]], [w_mix], sems)
    copy.start()
    width = act_ref.shape[1]
    hsize = width // heads
    parts = [message[j, :, width:].astype(F32) for j in range(message.shape[0])]
    span = parts[0].shape[1]
    levels = [
        p + pltpu.roll(p, span - heads, 1) + pltpu.roll(p, span - 2 * heads, 1) for p in parts
    ]
    top = functools.reduce(jnp.maximum, levels)
    weights = [jnp.exp(level - top) for level in levels]
    whole = functools.reduce(jnp.add, weights)
    lane = iota((1, span), 1)
    row = iota((span, width), 0)
    expand = (row % heads == iota((span, width), 1) // hsize) & (row < 2 * heads)
    expand = expand.astype(F32).astype(BF16)
    packed = []
    for weight in weights:
        weight = weight / whole
        high = weight.astype(BF16).astype(F32)
        both = jnp.where(lane < heads, high, pltpu.roll(weight - high, heads, 1))
        packed.append(jnp.where(lane < 2 * heads, both, 0.0))
    spread = dot(jnp.concatenate(packed, 0).astype(BF16), expand)
    own = act_ref.shape[0]
    attn = jnp.zeros(act_ref.shape, F32)
    for j in range(message.shape[0]):
        attn = attn + spread[j * own : (j + 1) * own] * message[j, :, :width].astype(F32)
    gated = (gate[...] * attn).astype(BF16)
    copy.wait()
    act = act_ref[...] + dot(gated, w_mix[...])
    act_out[...] = act
    xn2_out[...] = normed(act).astype(BF16)


def mix(layer, message, act, gate, w_out, heads):
    own, width = act.shape
    return call(
        functools.partial(mix_kernel, layer, heads),
        [jax.ShapeDtypeStruct((own, width), F32), jax.ShapeDtypeStruct((own, width), BF16)],
        message,
        act,
        gate,
        far=(w_out,),
        scratch=[pltpu.VMEM((width, width), BF16), pltpu.SemaphoreType.DMA((1,))],
        grant=48,
        flops=4 * own * width * width,
        moved=4 * width * width,
    )


def transition_kernel(groups, pieces, act_ref, xn2, *refs):
    others, refs = refs[: groups - 1], refs[groups - 1 :]
    sources = []
    for number in pieces:
        sources.append(refs[:number])
        refs = refs[number:]
    outs, (w_first, w_second, sems) = refs[:groups], refs[groups:]
    count, hid = w_second.shape[:2]
    plan = []
    for wanted, target in (((0, 2 * hid), w_first), ((2 * hid, 3 * hid), w_second)):
        for j, source in enumerate(sources):
            begin = 0
            for ref in source:
                end = begin + ref.shape[0]
                low, high = max(begin, wanted[0]), min(end, wanted[1])
                if low < high:
                    near = target.at[j, pl.ds(low - wanted[0], high - low)]
                    plan.append((target is w_first, j, ref.at[pl.ds(low - begin, high - low)], near))
                begin = end
    fetches = prepare([item[2] for item in plan], [item[3] for item in plan], sems)
    for copy in fetches:
        copy.start()

    def arrived(first, j):
        for item, copy in zip(plan, fetches):
            if item[:2] == (first, j):
                copy.wait()

    own = act_ref.shape[0]
    rows = jnp.concatenate([ref[...].astype(F32) for ref in (xn2, *others)], 0).astype(BF16)
    total = jnp.zeros((rows.shape[0], rows.shape[1]), F32)
    hidden = []
    for j in range(count):
        arrived(True, j)
        both = dot_nt(rows, w_first[j])
        left, right = both[:, :hid], both[:, hid:]
        hidden.append((left * jax.nn.sigmoid(left) * right).astype(BF16))
    for j in range(count):
        arrived(False, j)
        total = total + dot(hidden[j], w_second[j])
    outs[0][...] = act_ref[...] + total[:own]
    for k, out in enumerate(outs[1:], 1):
        out[...] = total[k * own : (k + 1) * own].astype(BF16)


def transition(act, xn2, others, weights):
    own, width = act.shape
    blocks = len(weights)
    hid = sum(part.shape[0] for part in weights[0]) // 3
    parts = [part for source in weights for part in source]
    return call(
        functools.partial(transition_kernel, len(others) + 1, [len(source) for source in weights]),
        [jax.ShapeDtypeStruct((own, width), F32)]
        + [jax.ShapeDtypeStruct((own, width), BF16)] * len(others),
        act,
        xn2,
        *others,
        far=parts,
        scratch=[
            pltpu.VMEM((blocks, 2 * hid, width), BF16),
            pltpu.VMEM((blocks, hid, width), BF16),
            pltpu.SemaphoreType.DMA((2 * len(parts),)),
        ],
        grant=48,
        flops=12 * own * hid * width * blocks,
        moved=6 * hid * width * blocks,
    )


def close_kernel(project, act_ref, *refs):
    *refs, act_out, all_ref = refs
    if project:
        *refs, tok_atom = refs
    act = act_ref[...]
    for ref in refs:
        act = act + ref[...].astype(F32)
    act_out[...] = act
    normal = normed(act).astype(BF16)
    if project:
        normal = dot(normal, tok_atom[...]).astype(BF16)
    for j in range(all_ref.shape[0]):
        all_ref[j] = normal


def close(act, parts, copies, tok_atom):
    own, width = act.shape
    project = tok_atom is not None
    last = tok_atom.shape[1] if project else width
    return call(
        functools.partial(close_kernel, project),
        [
            jax.ShapeDtypeStruct((own, width), F32),
            jax.ShapeDtypeStruct((copies, own, last), BF16),
        ],
        act,
        *parts,
        *([tok_atom] if project else []),
        flops=10**7,
        moved=10**6,
    )


def key_source(rows, cols):
    nrow, ncol = lax.axis_size("row"), lax.axis_size("col")
    shares = rows // cols
    pairs = []
    for owner in range(nrow):
        free = [list(range(share, ncol, shares)) for share in range(shares)]
        for r in range(nrow):
            for share in range(shares):
                if r != owner:
                    spot = (2 * ((r + owner) % 2) + share) % (ncol // shares) * shares + share
                    source = spot if spot in free[share] else free[share][0]
                    free[share].remove(source)
                    pairs.append((owner * ncol + source, r * ncol + owner * shares + share))
    return pairs


def body(
    atom_feat,
    atom_token,
    window_start,
    token_cond,
    token_mask,
    pair,
    enc_in,
    enc_out,
    pool_weight,
    tok_in,
    tok_out,
    pair_weight,
    trans_in,
    trans_out,
    tok_atom,
    dec_in,
    dec_out,
    pos_out,
):
    nrow, ncol = lax.axis_size("row"), lax.axis_size("col")
    everyone = ("row", "col")
    count = nrow * ncol
    me_col = lax.axis_index("col")
    rows, width = token_cond.shape
    cols = pair.shape[1]
    heads = pair_weight.shape[2]
    own = rows // ncol
    atoms, afeat = atom_feat.shape
    natom = atoms * count
    nblk = atoms // QB

    hid = trans_out.shape[1]
    feat = call(
        functools.partial(feat_kernel, rows),
        jax.ShapeDtypeStruct((atoms + EXTRA, afeat), BF16),
        atom_feat,
        atom_token[None],
        scalars=(window_start,),
        grant=48,
        moved=10**5,
    )
    up = [(i, i + 1) for i in range(count - 1)]
    prev = lax.ppermute(feat, everyone, up)
    after = lax.ppermute(feat, everyone, [(b, a) for a, b in up])
    _, first_part, second_part = lax.optimization_barrier(
        (feat, jnp.swapaxes(trans_in, 2, 3), trans_out)
    )
    matrix = jax.ShapeDtypeStruct((3 * hid, width), BF16)
    upper, lower, *packed = call(
        pack_kernel,
        [jax.ShapeDtypeStruct((rows_of * hid, width), BF16) for rows_of in (1, 2)]
        + [matrix] * BLOCKS,
        first_part,
        second_part,
        grant=48,
        moved=12 * trans_out.size,
    )
    prev, after, upper = lax.optimization_barrier((prev, after, upper))
    neighbour = [(i, i ^ 2) for i in range(count)]
    sibling = [(i, i ^ 1) for i in range(count)]
    across = [[lax.ppermute(upper, everyone, neighbour)], []]

    ext, copies = call(
        functools.partial(encoder_kernel, natom),
        [
            jax.ShapeDtypeStruct((atoms + 2 * HALO, afeat), BF16),
            jax.ShapeDtypeStruct((ncol, atoms + EXTRA, afeat), BF16),
        ],
        feat,
        prev,
        after,
        enc_in,
        enc_out,
        flops=10**8,
        moved=10**6,
    )
    span = -(-cols // 128) * 128
    half = rows // 2
    step = 24

    def bias_of(part, weights):
        return pl.pallas_call(
            bias_kernel,
            grid=(half // step,),
            out_shape=[jax.ShapeDtypeStruct((half, heads, span), F32)] * BLOCKS,
            in_specs=[
                pl.BlockSpec(
                    (step, cols, pair.shape[2]), lambda i: (i + part * (half // step), 0, 0)
                ),
                pl.BlockSpec(weights.shape, lambda i: (0, 0)),
            ],
            out_specs=[pl.BlockSpec((step, heads, span), lambda i: (i, 0, 0))] * BLOCKS,
            compiler_params=pltpu.CompilerParams(vmem_limit_bytes=(52 if part else 60) * MIB),
            cost_estimate=pl.CostEstimate(
                flops=2 * 10**9, bytes_accessed=4 * 10**6, transcendentals=0
            ),
        )(pair, weights)

    weights = jnp.swapaxes(pair_weight, 1, 2).reshape(BLOCKS * heads, -1)
    copies, first_weights = lax.optimization_barrier((copies, weights))
    low = bias_of(0, first_weights)
    both = lax.all_to_all(copies, "col", 0, 0)
    both, low, across[0][0] = lax.optimization_barrier((both, low, across[0][0]))

    act, xn, send = call(
        pool_kernel,
        [
            jax.ShapeDtypeStruct((own, width), F32),
            jax.ShapeDtypeStruct((rows, width), BF16),
            jax.ShapeDtypeStruct((cols, width), BF16),
        ],
        both,
        pool_weight,
        token_cond,
        flops=10**9,
        moved=10**6,
    )

    pairs = key_source(rows, cols)
    share = me_col % (rows // cols)
    peers = ncol // 4
    shifts = [
        [(r * ncol + c, r * ncol + (c + 4 * d) % ncol) for r in range(nrow) for c in range(ncol)]
        for d in range(peers)
    ]
    back = [[(b, a) for a, b in pairs_of] for pairs_of in shifts]
    xn, weights = lax.optimization_barrier((xn, weights))
    beside, beyond = [], [[], []]
    for layer in range(BLOCKS):
        last = layer == BLOCKS - 1
        if layer:
            send = lax.dynamic_slice_in_dim(xn, share * cols, cols, 0)
            send, xn, ready = lax.optimization_barrier((send, xn, across[1][0]))
        came = lax.ppermute(send, everyone, pairs)
        matrix = jax.ShapeDtypeStruct((width, width), BF16)
        query, w_key, w_val, gate = call(
            functools.partial(query_kernel, layer),
            [
                jax.ShapeDtypeStruct((rows, width), BF16),
                matrix,
                matrix,
                jax.ShapeDtypeStruct((own, width), F32),
            ],
            xn,
            act,
            far=(tok_in,),
            scratch=[pltpu.VMEM((width, width), BF16)] * 2 + [pltpu.SemaphoreType.DMA((4,))],
            grant=48,
            flops=2 * rows * width * width,
            moved=8 * width * width,
        )
        if not layer:
            high = list(bias_of(1, weights))
            high[0], lower, *ready = lax.optimization_barrier(
                (high[0], lower, across[0][0], *packed)
            )
            across[0].append(lax.ppermute(lower, everyone, neighbour))
            beyond[0].append(lax.ppermute(ready[0], everyone, sibling))
            beside = [lax.ppermute(part, everyone, sibling) for part in ready[1:]]
        else:
            beyond[1].append(lax.ppermute(ready, everyone, sibling))
        message = call(
            attention_kernel,
            jax.ShapeDtypeStruct((rows, width + span), BF16),
            query,
            send,
            came,
            low[layer],
            high[layer],
            w_key,
            w_val,
            scalars=(token_mask,),
            grant=16,
            flops=10**9,
            moved=8 * 10**6,
        )
        message = lax.all_to_all(message.reshape(ncol, own, -1), "col", 0, 0)
        if not layer:
            message, ready = lax.optimization_barrier((message, packed[1]))
            across[1].append(lax.ppermute(ready, everyone, neighbour))
        act, xn2 = mix(layer, message, act, gate, tok_out, heads)
        came_rows = [lax.ppermute(xn2, everyone, shifts[d]) for d in range(1, peers)]
        if not layer:
            xn2, ready = lax.optimization_barrier((xn2, across[0][1]))
            beyond[0].append(lax.ppermute(ready, everyone, sibling))
        act, *parts = transition(
            act, xn2, came_rows, ([packed[layer]], [beside[layer]], across[layer], beyond[layer])
        )
        parts = [lax.ppermute(part, everyone, back[d]) for d, part in enumerate(parts, 1)]
        act, copies = close(act, parts, count if last else ncol, tok_atom if last else None)
        axes = everyone if last else "col"
        gathered = lax.all_to_all(copies, axes, 0, 0).reshape(copies.shape[0] * own, -1)
        if not last:
            xn = gathered

    return call(
        functools.partial(decoder_kernel, natom, rows),
        jax.ShapeDtypeStruct((pos_out.shape[0], atoms), F32),
        ext,
        feat,
        prev,
        after,
        gathered,
        dec_in,
        dec_out,
        pos_out,
        flops=10**8,
        moved=10**6,
    )


def solution(mesh):
    in_specs = (
        P(("row", "col"), None),
        P(("row", "col")),
        P(("row", "col")),
        P("row", None),
        P(),
        P("row", "col", None),
        P(),
        P(),
        P(),
        P(),
        P(),
        P(),
        P(None, None, None, "col"),
        P(None, "col", None),
        P(),
        P(),
        P(),
        P(),
    )
    out_specs = P(None, ("row", "col"))
    return jax.shard_map(body, mesh=mesh, in_specs=in_specs, out_specs=out_specs, check_vma=False)
```

```python
import functools
import math

import jax
import jax.numpy as jnp
from jax import lax
from jax.experimental import pallas as pl
from jax.experimental.pallas import tpu as pltpu
from jax.sharding import PartitionSpec as P

HA = 4
QB = 32
KW = 128
HALO = 64
BLOCKS = 2
EXTRA = 16
MIB = 1 << 20
F32 = jnp.float32
BF16 = jnp.bfloat16


def call(kernel, outs, *args, scalars=(), far=(), scratch=(), grant=8, flops=0, moved=0):
    smem = pl.BlockSpec(memory_space=pltpu.SMEM)
    vmem = pl.BlockSpec(memory_space=pltpu.VMEM)
    hbm = pl.BlockSpec(memory_space=pltpu.HBM)
    return pl.pallas_call(
        kernel,
        out_shape=outs,
        in_specs=[smem] * len(scalars) + [vmem] * len(args) + [hbm] * len(far),
        out_specs=jax.tree.map(lambda _: vmem, outs),
        scratch_shapes=list(scratch),
        compiler_params=pltpu.CompilerParams(vmem_limit_bytes=grant * MIB),
        cost_estimate=pl.CostEstimate(flops=flops, bytes_accessed=moved, transcendentals=0),
    )(*scalars, *args, *far)


def dot(a, b):
    return jnp.dot(a, b, preferred_element_type=F32)


def dot_nt(a, b):
    return lax.dot_general(a, b, (((1,), (1,)), ((), ())), preferred_element_type=F32)


def dot_tn(a, b):
    return lax.dot_general(a, b, (((0,), (0,)), ((), ())), preferred_element_type=F32)


def normed(x):
    x = x.astype(F32)
    cent = x - jnp.mean(x, -1, keepdims=True)
    var = jnp.mean(cent * cent, -1, keepdims=True)
    return cent * lax.rsqrt(var + 1e-05)


def iota(shape, dim):
    return lax.broadcasted_iota(jnp.int32, shape, dim)


def device():
    row, col = lax.axis_index("row"), lax.axis_index("col")
    return row, col, row * lax.axis_size("col") + col


def window_mask(shifts, first, natom, nkeys):
    shape = (len(shifts) * QB, nkeys)
    block = iota(shape, 0) // QB
    low = jnp.zeros(shape, jnp.int32)
    for i, shift in enumerate(shifts):
        low = jnp.where(block == i, shift + QB * i, low)
    key = iota(shape, 1)
    atom = key + first
    return (key >= low) & (key < low + KW) & (atom >= 0) & (atom < natom)


def attend(x, xn, gate, query, keys, vals, mask, w_out):
    width = x.shape[1]
    hsize = width // HA
    lane = iota((1, width), 1) // hsize
    outs = jnp.zeros(x.shape, F32)
    for h in range(HA):
        pick = (lane == h).astype(BF16)
        scores = dot_nt(query, keys * pick) * (1.0 / math.sqrt(hsize))
        scores = jnp.where(mask, scores, -1000000000.0)
        top = jnp.max(scores, -1, keepdims=True)
        expd = jnp.exp(scores - top)
        total = jnp.sum(expd, -1, keepdims=True)
        outs = outs + dot(expd.astype(BF16), vals * pick) / total
    gated = (jax.nn.sigmoid(gate) * outs).astype(BF16)
    return (x.astype(F32) + dot(gated, w_out)).astype(BF16)


def shifts_of(tail_ref, lanes):
    tail = tail_ref[tail_ref.shape[0] - EXTRA :, :].astype(F32)
    return [tail[1:2, k : k + 1].astype(jnp.int32) for k in lanes]


def encoder_kernel(natom, own_ref, prev_ref, next_ref, w_in, w_out, ext_ref, all_ref):
    rows = own_ref.shape[0] - EXTRA
    nblk = rows // QB
    half = HALO // QB
    x = jnp.concatenate([prev_ref[:rows], own_ref[:rows], next_ref[:rows]], 0)
    xn = normed(x).astype(BF16)
    keys = dot(xn, w_in[1]).astype(BF16)
    vals = dot(xn, w_in[2]).astype(BF16)
    qx, qn = x[HALO : 3 * rows - HALO], xn[HALO : 3 * rows - HALO]
    query = dot(qn, w_in[0]).astype(BF16)
    gate = dot(qn, w_in[3])
    shifts = (
        shifts_of(prev_ref, range(nblk - half, nblk))
        + shifts_of(own_ref, range(nblk))
        + shifts_of(next_ref, range(half))
    )
    first = device()[2] * rows - rows
    for part in range(2):
        mine = slice(part * rows, (part + 1) * rows)
        seen = slice(part * rows, (part + 2) * rows)
        mask = window_mask(
            shifts[part * nblk : (part + 1) * nblk], first + part * rows, natom, 2 * rows
        )
        ext_ref[mine] = attend(
            qx[mine], qn[mine], gate[mine], query[mine], keys[seen], vals[seen], mask, w_out[...]
        )
    new = ext_ref[HALO : HALO + rows]
    tail = own_ref[rows:]
    for j in range(all_ref.shape[0]):
        all_ref[j, :rows] = new
        all_ref[j, rows:] = tail


def pool_kernel(both_ref, weight, cond, act_ref, xn_ref, send_ref):
    count, rows = both_ref.shape[0], both_ref.shape[1] - EXTRA
    tokens = cond.shape[0]
    sums = jnp.zeros(cond.shape, F32)
    counts = jnp.zeros((tokens, 1), F32)
    step = 4 if count % 4 == 0 else 1
    for j in range(0, count, step):
        atoms = jnp.concatenate([both_ref[j + k, :rows] for k in range(step)], 0)
        feats = jnp.maximum(dot(atoms, weight[...]), 0.0).astype(BF16)
        spot = jnp.concatenate(
            [both_ref[j + k, rows:].astype(F32)[0:1] for k in range(step)], 1
        ).astype(jnp.int32)
        onehot = (iota((tokens, step * rows), 0) == spot).astype(F32)
        sums = sums + dot(onehot.astype(BF16), feats)
        counts = counts + jnp.sum(onehot, -1, keepdims=True)
    act = sums / counts + cond[...].astype(F32)
    xn = normed(act)
    xn_ref[...] = xn.astype(BF16)
    cols = send_ref.shape[0]
    part = xn[:cols]
    for k in range(1, tokens // cols):
        part = jnp.where(device()[1] % (tokens // cols) == k, xn[k * cols : (k + 1) * cols], part)
    send_ref[...] = part.astype(BF16)
    own = act_ref.shape[0]
    col = device()[1]
    mine = act[:own]
    for c in range(1, tokens // own):
        mine = jnp.where(col == c, act[c * own : (c + 1) * own], mine)
    act_ref[...] = mine


def decoder_kernel(
    natom, x1_ref, own_ref, prev_ref, next_ref, proj_ref, edge_ref, w_in, w_out, pos, out
):
    rows = own_ref.shape[0] - EXTRA
    proj = proj_ref[...].astype(F32)
    edge = edge_ref[...].astype(F32)
    tokens = proj.shape[0]
    _, col, me = device()
    rest = tokens - HALO
    below = jnp.where(col == 0, edge, proj[rest:])
    above = jnp.where(col == lax.axis_size("col") - 1, edge, proj[:HALO])
    tables = (
        jnp.concatenate([proj[:rest], below], 0),
        proj,
        jnp.concatenate([above, proj[HALO:]], 0),
    )
    spread = []
    for table, ref in zip(tables, (prev_ref, own_ref, next_ref)):
        spot = ref[rows:].astype(F32)[0:1].astype(jnp.int32)
        onehot = (iota((tokens, rows), 0) == spot).astype(F32).astype(BF16)
        spread.append(dot_tn(onehot, table.astype(BF16)))
    spread = jnp.concatenate([spread[0][rows - HALO :], spread[1], spread[2][:HALO]], 0)
    x = (x1_ref[...].astype(F32) + spread).astype(BF16)
    xn = normed(x).astype(BF16)
    keys = dot(xn, w_in[1]).astype(BF16)
    vals = dot(xn, w_in[2]).astype(BF16)
    qx, qn = x[HALO : HALO + rows], xn[HALO : HALO + rows]
    query = dot(qn, w_in[0]).astype(BF16)
    gate = dot(qn, w_in[3])
    shifts = shifts_of(own_ref, range(rows // QB))
    mask = window_mask(shifts, me * rows - HALO, natom, 2 * rows)
    third = attend(qx, qn, gate, query, keys, vals, mask, w_out[...])
    out[...] = dot_nt(pos[...], normed(third).astype(BF16))


def feat_kernel(row_tokens, starts, feat, token, own):
    rows, width = feat.shape
    row, _, me = device()
    nblk = starts.shape[0]
    lane = iota((EXTRA, width), 1)
    line = iota((EXTRA, width), 0)
    tail = jnp.where(line == 0, token[...] - row * row_tokens, 0)
    for k in range(nblk):
        shift = starts[k] - QB * (me * nblk + k) + HALO
        tail = jnp.where((line == 1) & (lane == k), shift, tail)
    own[:rows] = feat[...]
    own[rows:] = tail.astype(F32).astype(BF16)


def pack_kernel(first, second, upper, lower, *outs):
    hid = second.shape[1]
    part = upper.shape[0]
    for layer, out in enumerate(outs):
        out[:hid] = first[layer, 0]
        out[hid : 2 * hid] = first[layer, 1]
        out[2 * hid :] = second[layer]
    upper[...] = outs[0][:part]
    lower[...] = outs[0][part:]


def bias_kernel(pair_ref, weight, *outs):
    rows, cols, _ = pair_ref.shape
    _, heads, pad = outs[0].shape
    pad = pad - cols

    for q in range(rows):
        bias = dot_nt(weight[...], pair_ref[q])
        bias = jnp.concatenate([bias, jnp.zeros((bias.shape[0], pad), F32)], 1)
        for layer, out in enumerate(outs):
            out[q] = bias[layer * heads : (layer + 1) * heads]


def prepare(sources, targets, sems):
    return [
        pltpu.make_async_copy(source, target, sems.at[i])
        for i, (source, target) in enumerate(zip(sources, targets))
    ]


def query_kernel(
    layer, xn_ref, act_ref, w_in, query, w_key, w_val, gate, w_query, w_gate, sems
):
    fetches = prepare(
        [w_in.at[layer, k] for k in range(4)], [w_query, w_key, w_val, w_gate], sems
    )
    for k in (0, 3, 1, 2):
        fetches[k].start()
    fetches[0].wait()
    query[...] = dot(xn_ref[...], w_query[...]).astype(BF16)
    fetches[3].wait()
    gate[...] = jax.nn.sigmoid(dot(normed(act_ref[...]).astype(BF16), w_gate[...]))
    fetches[1].wait()
    fetches[2].wait()


def attention_kernel(mask_ref, query, here_ref, came_ref, low, high, w_key, w_val, out_ref):
    rows, width = query.shape
    cols = here_ref.shape[0]
    heads = low.shape[1]
    hsize = width // heads
    span = low.shape[2]
    row, col, _ = device()
    mine = col * cols // rows == row
    key_xn = jnp.where(mine, here_ref[...].astype(F32), came_ref[...].astype(F32))
    key_xn = jnp.concatenate([key_xn, jnp.zeros((span - cols, width), F32)], 0).astype(BF16)
    keys = dot(key_xn, w_key[...]).astype(BF16)
    vals = dot(key_xn, w_val[...]).astype(BF16)
    tokens = mask_ref.shape[0]
    count = jnp.int32(0)
    for bit in range(tokens.bit_length() - 1, -1, -1):
        longer = count + (1 << bit)
        inside = longer <= tokens
        last = mask_ref[jnp.where(inside, longer - 1, 0)]
        count = jnp.where(inside & (last == 1), longer, count)
    valid = iota((1, span), 1) + col * cols < count
    valid = valid & (iota((1, span), 1) < cols)
    group = heads // 2
    part = group * hsize
    lane = iota((1, part), 1) // hsize
    spot = iota((1, span), 1)
    levels = jnp.zeros((rows, span), F32)
    for g in range(2):
        wide = slice(g * part, (g + 1) * part)
        kg, vg = keys[:, wide], vals[:, wide]
        picks = [(lane == h).astype(BF16) for h in range(group)]
        stacked = jnp.concatenate([kg * p for p in picks], 0)
        scores = dot_nt(query[:, wide], stacked) * (1.0 / math.sqrt(hsize))
        probs = []
        for h in range(group):
            head = g * group + h
            bias = jnp.concatenate([low[:, head, :], high[:, head, :]], 0)
            score = scores[:, h * span : (h + 1) * span] + bias
            score = jnp.where(valid, score, -1000000000.0)
            top = jnp.max(score, -1, keepdims=True)
            expd = jnp.exp(score - top)
            total = jnp.sum(expd, -1, keepdims=True)
            probs.append((expd / total).astype(BF16))
            levels = jnp.where(spot % heads == head, top + jnp.log(total), levels)
        stacked = jnp.concatenate([vg * p for p in picks], 0)
        out_ref[:, wide] = dot(jnp.concatenate(probs, 1), stacked).astype(BF16)
    high = levels.astype(BF16).astype(F32)
    rest = levels - high
    middle = rest.astype(BF16).astype(F32)
    low = rest - middle
    packed = jnp.where(spot < heads, high, jnp.where(spot < 2 * heads, middle, low))
    out_ref[:, width:] = jnp.where(spot < 3 * heads, packed, 0.0).astype(BF16)


def mix_kernel(layer, heads, message, act_ref, gate, w_out, act_out, xn2_out, w_mix, sems):
    (copy,) = prepare([w_out.at[layer]], [w_mix], sems)
    copy.start()
    width = act_ref.shape[1]
    hsize = width // heads
    parts = [message[j, :, width:].astype(F32) for j in range(message.shape[0])]
    span = parts[0].shape[1]
    levels = [
        p + pltpu.roll(p, span - heads, 1) + pltpu.roll(p, span - 2 * heads, 1) for p in parts
    ]
    top = functools.reduce(jnp.maximum, levels)
    weights = [jnp.exp(level - top) for level in levels]
    whole = functools.reduce(jnp.add, weights)
    lane = iota((1, span), 1)
    row = iota((span, width), 0)
    expand = (row % heads == iota((span, width), 1) // hsize) & (row < 2 * heads)
    expand = expand.astype(F32).astype(BF16)
    packed = []
    for weight in weights:
        weight = weight / whole
        high = weight.astype(BF16).astype(F32)
        both = jnp.where(lane < heads, high, pltpu.roll(weight - high, heads, 1))
        packed.append(jnp.where(lane < 2 * heads, both, 0.0))
    spread = dot(jnp.concatenate(packed, 0).astype(BF16), expand)
    own = act_ref.shape[0]
    attn = jnp.zeros(act_ref.shape, F32)
    for j in range(message.shape[0]):
        attn = attn + spread[j * own : (j + 1) * own] * message[j, :, :width].astype(F32)
    gated = (gate[...] * attn).astype(BF16)
    copy.wait()
    act = act_ref[...] + dot(gated, w_mix[...])
    act_out[...] = act
    xn2_out[...] = normed(act).astype(BF16)


def mix(layer, message, act, gate, w_out, heads):
    own, width = act.shape
    return call(
        functools.partial(mix_kernel, layer, heads),
        [jax.ShapeDtypeStruct((own, width), F32), jax.ShapeDtypeStruct((own, width), BF16)],
        message,
        act,
        gate,
        far=(w_out,),
        scratch=[pltpu.VMEM((width, width), BF16), pltpu.SemaphoreType.DMA((1,))],
        grant=48,
        flops=4 * own * width * width,
        moved=4 * width * width,
    )


def transition_kernel(groups, pieces, act_ref, xn2, *refs):
    others, refs = refs[: groups - 1], refs[groups - 1 :]
    sources = []
    for number in pieces:
        sources.append(refs[:number])
        refs = refs[number:]
    outs, (w_first, w_second, sems) = refs[:groups], refs[groups:]
    count, hid = w_second.shape[:2]
    plan = []
    for wanted, target in (((0, 2 * hid), w_first), ((2 * hid, 3 * hid), w_second)):
        for j, source in enumerate(sources):
            begin = 0
            for ref in source:
                end = begin + ref.shape[0]
                low, high = max(begin, wanted[0]), min(end, wanted[1])
                if low < high:
                    near = target.at[j, pl.ds(low - wanted[0], high - low)]
                    plan.append((target is w_first, j, ref.at[pl.ds(low - begin, high - low)], near))
                begin = end
    fetches = prepare([item[2] for item in plan], [item[3] for item in plan], sems)
    for copy in fetches:
        copy.start()

    def arrived(first, j):
        for item, copy in zip(plan, fetches):
            if item[:2] == (first, j):
                copy.wait()

    own = act_ref.shape[0]
    rows = jnp.concatenate([ref[...].astype(F32) for ref in (xn2, *others)], 0).astype(BF16)
    total = jnp.zeros((rows.shape[0], rows.shape[1]), F32)
    hidden = []
    for j in range(count):
        arrived(True, j)
        both = dot_nt(rows, w_first[j])
        left, right = both[:, :hid], both[:, hid:]
        hidden.append((left * jax.nn.sigmoid(left) * right).astype(BF16))
    for j in range(count):
        arrived(False, j)
        total = total + dot(hidden[j], w_second[j])
    outs[0][...] = act_ref[...] + total[:own]
    for k, out in enumerate(outs[1:], 1):
        out[...] = total[k * own : (k + 1) * own].astype(BF16)


def transition(act, xn2, others, weights):
    own, width = act.shape
    blocks = len(weights)
    hid = sum(part.shape[0] for part in weights[0]) // 3
    parts = [part for source in weights for part in source]
    return call(
        functools.partial(transition_kernel, len(others) + 1, [len(source) for source in weights]),
        [jax.ShapeDtypeStruct((own, width), F32)]
        + [jax.ShapeDtypeStruct((own, width), BF16)] * len(others),
        act,
        xn2,
        *others,
        far=parts,
        scratch=[
            pltpu.VMEM((blocks, 2 * hid, width), BF16),
            pltpu.VMEM((blocks, hid, width), BF16),
            pltpu.SemaphoreType.DMA((2 * len(parts),)),
        ],
        grant=48,
        flops=12 * own * hid * width * blocks,
        moved=6 * hid * width * blocks,
    )


def close_kernel(project, act_ref, *refs):
    *refs, act_out, all_ref = refs
    if project:
        *refs, tok_atom = refs
    act = act_ref[...]
    for ref in refs:
        act = act + ref[...].astype(F32)
    act_out[...] = act
    normal = normed(act).astype(BF16)
    if project:
        normal = dot(normal, tok_atom[...]).astype(BF16)
    for j in range(all_ref.shape[0]):
        all_ref[j] = normal


def close(act, parts, copies, tok_atom):
    own, width = act.shape
    project = tok_atom is not None
    last = tok_atom.shape[1] if project else width
    return call(
        functools.partial(close_kernel, project),
        [
            jax.ShapeDtypeStruct((own, width), F32),
            jax.ShapeDtypeStruct((copies, own, last), BF16),
        ],
        act,
        *parts,
        *([tok_atom] if project else []),
        flops=10**7,
        moved=10**6,
    )


def key_source(rows, cols):
    nrow, ncol = lax.axis_size("row"), lax.axis_size("col")
    shares = rows // cols
    pairs = []
    for owner in range(nrow):
        free = [list(range(share, ncol, shares)) for share in range(shares)]
        for r in range(nrow):
            for share in range(shares):
                if r != owner:
                    spot = (2 * ((r + owner) % 2) + share) % (ncol // shares) * shares + share
                    source = spot if spot in free[share] else free[share][0]
                    free[share].remove(source)
                    pairs.append((owner * ncol + source, r * ncol + owner * shares + share))
    return pairs


def body(
    atom_feat,
    atom_token,
    window_start,
    token_cond,
    token_mask,
    pair,
    enc_in,
    enc_out,
    pool_weight,
    tok_in,
    tok_out,
    pair_weight,
    trans_in,
    trans_out,
    tok_atom,
    dec_in,
    dec_out,
    pos_out,
):
    nrow, ncol = lax.axis_size("row"), lax.axis_size("col")
    everyone = ("row", "col")
    count = nrow * ncol
    me_col = lax.axis_index("col")
    rows, width = token_cond.shape
    cols = pair.shape[1]
    heads = pair_weight.shape[2]
    own = rows // ncol
    atoms, afeat = atom_feat.shape
    natom = atoms * count
    nblk = atoms // QB

    hid = trans_out.shape[1]
    feat = call(
        functools.partial(feat_kernel, rows),
        jax.ShapeDtypeStruct((atoms + EXTRA, afeat), BF16),
        atom_feat,
        atom_token[None],
        scalars=(window_start,),
        grant=48,
        moved=10**5,
    )
    up = [(i, i + 1) for i in range(count - 1)]
    prev = lax.ppermute(feat, everyone, up)
    after = lax.ppermute(feat, everyone, [(b, a) for a, b in up])
    _, first_part, second_part = lax.optimization_barrier(
        (feat, jnp.swapaxes(trans_in, 2, 3), trans_out)
    )
    matrix = jax.ShapeDtypeStruct((3 * hid, width), BF16)
    upper, lower, *packed = call(
        pack_kernel,
        [jax.ShapeDtypeStruct((3 * hid // 2, width), BF16)] * 2
        + [matrix] * BLOCKS,
        first_part,
        second_part,
        grant=48,
        moved=12 * trans_out.size,
    )
    prev, after, upper = lax.optimization_barrier((prev, after, upper))
    neighbour = [(i, i ^ 2) for i in range(count)]
    sibling = [(i, i ^ 1) for i in range(count)]
    across = [[lax.ppermute(upper, everyone, neighbour)], []]

    ext, copies = call(
        functools.partial(encoder_kernel, natom),
        [
            jax.ShapeDtypeStruct((atoms + 2 * HALO, afeat), BF16),
            jax.ShapeDtypeStruct((ncol, atoms + EXTRA, afeat), BF16),
        ],
        feat,
        prev,
        after,
        enc_in,
        enc_out,
        flops=10**8,
        moved=10**6,
    )
    span = -(-cols // 128) * 128
    half = rows // 2
    step = 24

    def bias_of(part, weights):
        return pl.pallas_call(
            bias_kernel,
            grid=(half // step,),
            out_shape=[jax.ShapeDtypeStruct((half, heads, span), F32)] * BLOCKS,
            in_specs=[
                pl.BlockSpec(
                    (step, cols, pair.shape[2]), lambda i: (i + part * (half // step), 0, 0)
                ),
                pl.BlockSpec(weights.shape, lambda i: (0, 0)),
            ],
            out_specs=[pl.BlockSpec((step, heads, span), lambda i: (i, 0, 0))] * BLOCKS,
            compiler_params=pltpu.CompilerParams(vmem_limit_bytes=(52 if part else 60) * MIB),
            cost_estimate=pl.CostEstimate(
                flops=2 * 10**9, bytes_accessed=4 * 10**6, transcendentals=0
            ),
        )(pair, weights)

    weights = jnp.swapaxes(pair_weight, 1, 2).reshape(BLOCKS * heads, -1)
    copies, first_weights = lax.optimization_barrier((copies, weights))
    low = bias_of(0, first_weights)
    both = lax.all_to_all(copies, "col", 0, 0)
    both, low, across[0][0] = lax.optimization_barrier((both, low, across[0][0]))

    act, xn, send = call(
        pool_kernel,
        [
            jax.ShapeDtypeStruct((own, width), F32),
            jax.ShapeDtypeStruct((rows, width), BF16),
            jax.ShapeDtypeStruct((cols, width), BF16),
        ],
        both,
        pool_weight,
        token_cond,
        flops=10**9,
        moved=10**6,
    )

    pairs = key_source(rows, cols)
    share = me_col % (rows // cols)
    peers = ncol // 4
    shifts = [
        [(r * ncol + c, r * ncol + (c + 4 * d) % ncol) for r in range(nrow) for c in range(ncol)]
        for d in range(peers)
    ]
    back = [[(b, a) for a, b in pairs_of] for pairs_of in shifts]
    xn, weights = lax.optimization_barrier((xn, weights))
    beside, beyond = [], [[], []]
    for layer in range(BLOCKS):
        last = layer == BLOCKS - 1
        if layer:
            send = lax.dynamic_slice_in_dim(xn, share * cols, cols, 0)
            send, xn, ready = lax.optimization_barrier((send, xn, across[1][0]))
        came = lax.ppermute(send, everyone, pairs)
        matrix = jax.ShapeDtypeStruct((width, width), BF16)
        query, w_key, w_val, gate = call(
            functools.partial(query_kernel, layer),
            [
                jax.ShapeDtypeStruct((rows, width), BF16),
                matrix,
                matrix,
                jax.ShapeDtypeStruct((own, width), F32),
            ],
            xn,
            act,
            far=(tok_in,),
            scratch=[pltpu.VMEM((width, width), BF16)] * 2 + [pltpu.SemaphoreType.DMA((4,))],
            grant=48,
            flops=2 * rows * width * width,
            moved=8 * width * width,
        )
        if not layer:
            high = list(bias_of(1, weights))
            high[0], lower, *ready = lax.optimization_barrier(
                (high[0], lower, across[0][0], *packed)
            )
            across[0].append(lax.ppermute(lower, everyone, neighbour))
            beyond[0].append(lax.ppermute(ready[0], everyone, sibling))
            beside = [lax.ppermute(part, everyone, sibling) for part in ready[1:]]
        else:
            beyond[1].append(lax.ppermute(ready, everyone, sibling))
        message = call(
            attention_kernel,
            jax.ShapeDtypeStruct((rows, width + span), BF16),
            query,
            send,
            came,
            low[layer],
            high[layer],
            w_key,
            w_val,
            scalars=(token_mask,),
            grant=16,
            flops=10**9,
            moved=8 * 10**6,
        )
        message = lax.all_to_all(message.reshape(ncol, own, -1), "col", 0, 0)
        if not layer:
            message, ready = lax.optimization_barrier((message, packed[1]))
            across[1].append(lax.ppermute(ready, everyone, neighbour))
        act, xn2 = mix(layer, message, act, gate, tok_out, heads)
        came_rows = [lax.ppermute(xn2, everyone, shifts[d]) for d in range(1, peers)]
        if not layer:
            xn2, ready = lax.optimization_barrier((xn2, across[0][1]))
            beyond[0].append(lax.ppermute(ready, everyone, sibling))
        act, *parts = transition(
            act, xn2, came_rows, ([packed[layer]], [beside[layer]], across[layer], beyond[layer])
        )
        parts = [lax.ppermute(part, everyone, back[d]) for d, part in enumerate(parts, 1)]
        act, copies = close(act, parts, ncol, tok_atom if last else None)
        gathered = lax.all_to_all(copies, "col", 0, 0).reshape(rows, -1)
        if not last:
            xn = gathered

    bounds = [(r * ncol - 1, r * ncol) for r in range(1, nrow)]
    bounds += [(b, a) for a, b in bounds]
    edge = jnp.where(me_col == 0, gathered[:HALO], gathered[rows - HALO :])
    edge = lax.ppermute(edge, everyone, bounds)

    return call(
        functools.partial(decoder_kernel, natom),
        jax.ShapeDtypeStruct((pos_out.shape[0], atoms), F32),
        ext,
        feat,
        prev,
        after,
        gathered,
        edge,
        dec_in,
        dec_out,
        pos_out,
        flops=10**8,
        moved=10**6,
    )


def solution(mesh):
    in_specs = (
        P(("row", "col"), None),
        P(("row", "col")),
        P(("row", "col")),
        P("row", None),
        P(),
        P("row", "col", None),
        P(),
        P(),
        P(),
        P(),
        P(),
        P(),
        P(None, None, None, "col"),
        P(None, "col", None),
        P(),
        P(),
        P(),
        P(),
    )
    out_specs = P(None, ("row", "col"))
    return jax.shard_map(body, mesh=mesh, in_specs=in_specs, out_specs=out_specs, check_vma=False)
```

```python
import functools
import math

import jax
import jax.numpy as jnp
from jax import lax
from jax.experimental import pallas as pl
from jax.experimental.pallas import tpu as pltpu
from jax.sharding import PartitionSpec as P

HA = 4
QB = 32
KW = 128
HALO = 64
BLOCKS = 2
EXTRA = 16
MIB = 1 << 20
F32 = jnp.float32
BF16 = jnp.bfloat16


def call(kernel, outs, *args, scalars=(), far=(), scratch=(), grant=8, flops=0, moved=0):
    smem = pl.BlockSpec(memory_space=pltpu.SMEM)
    vmem = pl.BlockSpec(memory_space=pltpu.VMEM)
    hbm = pl.BlockSpec(memory_space=pltpu.HBM)
    return pl.pallas_call(
        kernel,
        out_shape=outs,
        in_specs=[smem] * len(scalars) + [vmem] * len(args) + [hbm] * len(far),
        out_specs=jax.tree.map(lambda _: vmem, outs),
        scratch_shapes=list(scratch),
        compiler_params=pltpu.CompilerParams(vmem_limit_bytes=grant * MIB),
        cost_estimate=pl.CostEstimate(flops=flops, bytes_accessed=moved, transcendentals=0),
    )(*scalars, *args, *far)


def dot(a, b):
    return jnp.dot(a, b, preferred_element_type=F32)


def dot_nt(a, b):
    return lax.dot_general(a, b, (((1,), (1,)), ((), ())), preferred_element_type=F32)


def dot_tn(a, b):
    return lax.dot_general(a, b, (((0,), (0,)), ((), ())), preferred_element_type=F32)


def normed(x):
    x = x.astype(F32)
    cent = x - jnp.mean(x, -1, keepdims=True)
    var = jnp.mean(cent * cent, -1, keepdims=True)
    return cent * lax.rsqrt(var + 1e-05)


def iota(shape, dim):
    return lax.broadcasted_iota(jnp.int32, shape, dim)


def device():
    row, col = lax.axis_index("row"), lax.axis_index("col")
    return row, col, row * lax.axis_size("col") + col


def window_mask(shifts, first, natom, nkeys):
    shape = (len(shifts) * QB, nkeys)
    block = iota(shape, 0) // QB
    low = jnp.zeros(shape, jnp.int32)
    for i, shift in enumerate(shifts):
        low = jnp.where(block == i, shift + QB * i, low)
    key = iota(shape, 1)
    atom = key + first
    return (key >= low) & (key < low + KW) & (atom >= 0) & (atom < natom)


def attend(x, xn, gate, query, keys, vals, mask, w_out):
    width = x.shape[1]
    hsize = width // HA
    lane = iota((1, width), 1) // hsize
    outs = jnp.zeros(x.shape, F32)
    for h in range(HA):
        pick = (lane == h).astype(BF16)
        scores = dot_nt(query, keys * pick) * (1.0 / math.sqrt(hsize))
        scores = jnp.where(mask, scores, -1000000000.0)
        top = jnp.max(scores, -1, keepdims=True)
        expd = jnp.exp(scores - top)
        total = jnp.sum(expd, -1, keepdims=True)
        outs = outs + dot(expd.astype(BF16), vals * pick) / total
    gated = (jax.nn.sigmoid(gate) * outs).astype(BF16)
    return (x.astype(F32) + dot(gated, w_out)).astype(BF16)


def shifts_of(tail_ref, lanes):
    tail = tail_ref[tail_ref.shape[0] - EXTRA :, :].astype(F32)
    return [tail[1:2, k : k + 1].astype(jnp.int32) for k in lanes]


def encoder_kernel(natom, own_ref, prev_ref, next_ref, w_in, w_out, ext_ref, all_ref):
    rows = own_ref.shape[0] - EXTRA
    nblk = rows // QB
    half = HALO // QB
    x = jnp.concatenate([prev_ref[:rows], own_ref[:rows], next_ref[:rows]], 0)
    xn = normed(x).astype(BF16)
    keys = dot(xn, w_in[1]).astype(BF16)
    vals = dot(xn, w_in[2]).astype(BF16)
    qx, qn = x[HALO : 3 * rows - HALO], xn[HALO : 3 * rows - HALO]
    query = dot(qn, w_in[0]).astype(BF16)
    gate = dot(qn, w_in[3])
    shifts = (
        shifts_of(prev_ref, range(nblk - half, nblk))
        + shifts_of(own_ref, range(nblk))
        + shifts_of(next_ref, range(half))
    )
    first = device()[2] * rows - rows
    for part in range(2):
        mine = slice(part * rows, (part + 1) * rows)
        seen = slice(part * rows, (part + 2) * rows)
        mask = window_mask(
            shifts[part * nblk : (part + 1) * nblk], first + part * rows, natom, 2 * rows
        )
        ext_ref[mine] = attend(
            qx[mine], qn[mine], gate[mine], query[mine], keys[seen], vals[seen], mask, w_out[...]
        )
    new = ext_ref[HALO : HALO + rows]
    tail = own_ref[rows:]
    for j in range(all_ref.shape[0]):
        all_ref[j, :rows] = new
        all_ref[j, rows:] = tail


def pool_kernel(both_ref, weight, cond, act_ref, xn_ref, send_ref):
    count, rows = both_ref.shape[0], both_ref.shape[1] - EXTRA
    tokens = cond.shape[0]
    sums = jnp.zeros(cond.shape, F32)
    counts = jnp.zeros((tokens, 1), F32)
    step = 4 if count % 4 == 0 else 1
    for j in range(0, count, step):
        atoms = jnp.concatenate([both_ref[j + k, :rows] for k in range(step)], 0)
        feats = jnp.maximum(dot(atoms, weight[...]), 0.0).astype(BF16)
        spot = jnp.concatenate(
            [both_ref[j + k, rows:].astype(F32)[0:1] for k in range(step)], 1
        ).astype(jnp.int32)
        onehot = (iota((tokens, step * rows), 0) == spot).astype(F32)
        sums = sums + dot(onehot.astype(BF16), feats)
        counts = counts + jnp.sum(onehot, -1, keepdims=True)
    act = sums / counts + cond[...].astype(F32)
    xn = normed(act)
    xn_ref[...] = xn.astype(BF16)
    cols = send_ref.shape[0]
    part = xn[:cols]
    for k in range(1, tokens // cols):
        part = jnp.where(device()[1] % (tokens // cols) == k, xn[k * cols : (k + 1) * cols], part)
    send_ref[...] = part.astype(BF16)
    own = act_ref.shape[0]
    col = device()[1]
    mine = act[:own]
    for c in range(1, tokens // own):
        mine = jnp.where(col == c, act[c * own : (c + 1) * own], mine)
    act_ref[...] = mine


def decoder_kernel(
    natom, x1_ref, own_ref, prev_ref, next_ref, proj_ref, edge_ref, w_in, w_out, pos, out
):
    rows = own_ref.shape[0] - EXTRA
    proj = proj_ref[...].astype(F32)
    edge = edge_ref[...].astype(F32)
    tokens = proj.shape[0]
    _, col, me = device()
    rest = tokens - HALO
    below = jnp.where(col == 0, edge, proj[rest:])
    above = jnp.where(col == lax.axis_size("col") - 1, edge, proj[:HALO])
    tables = (
        jnp.concatenate([proj[:rest], below], 0),
        proj,
        jnp.concatenate([above, proj[HALO:]], 0),
    )
    spread = []
    for table, ref in zip(tables, (prev_ref, own_ref, next_ref)):
        spot = ref[rows:].astype(F32)[0:1].astype(jnp.int32)
        onehot = (iota((tokens, rows), 0) == spot).astype(F32).astype(BF16)
        spread.append(dot_tn(onehot, table.astype(BF16)))
    spread = jnp.concatenate([spread[0][rows - HALO :], spread[1], spread[2][:HALO]], 0)
    x = (x1_ref[...].astype(F32) + spread).astype(BF16)
    xn = normed(x).astype(BF16)
    keys = dot(xn, w_in[1]).astype(BF16)
    vals = dot(xn, w_in[2]).astype(BF16)
    qx, qn = x[HALO : HALO + rows], xn[HALO : HALO + rows]
    query = dot(qn, w_in[0]).astype(BF16)
    gate = dot(qn, w_in[3])
    shifts = shifts_of(own_ref, range(rows // QB))
    mask = window_mask(shifts, me * rows - HALO, natom, 2 * rows)
    third = attend(qx, qn, gate, query, keys, vals, mask, w_out[...])
    out[...] = dot_nt(pos[...], normed(third).astype(BF16))


def feat_kernel(row_tokens, starts, feat, token, own):
    rows, width = feat.shape
    row, _, me = device()
    nblk = starts.shape[0]
    lane = iota((EXTRA, width), 1)
    line = iota((EXTRA, width), 0)
    tail = jnp.where(line == 0, token[...] - row * row_tokens, 0)
    for k in range(nblk):
        shift = starts[k] - QB * (me * nblk + k) + HALO
        tail = jnp.where((line == 1) & (lane == k), shift, tail)
    own[:rows] = feat[...]
    own[rows:] = tail.astype(F32).astype(BF16)


def pack_kernel(first, second, *outs):
    hid = second.shape[1]
    part = 3 * hid // 2
    for layer in range(BLOCKS):
        whole, upper, lower = outs[3 * layer : 3 * layer + 3]
        whole[:hid] = first[layer, 0]
        whole[hid : 2 * hid] = first[layer, 1]
        whole[2 * hid :] = second[layer]
        upper[...] = whole[:part]
        lower[...] = whole[part:]


def bias_kernel(pair_ref, weight, *outs):
    rows, cols, _ = pair_ref.shape
    _, heads, pad = outs[0].shape
    pad = pad - cols

    for q in range(rows):
        bias = dot_nt(weight[...], pair_ref[q])
        bias = jnp.concatenate([bias, jnp.zeros((bias.shape[0], pad), F32)], 1)
        for layer, out in enumerate(outs):
            out[q] = bias[layer * heads : (layer + 1) * heads]


def prepare(sources, targets, sems):
    return [
        pltpu.make_async_copy(source, target, sems.at[i])
        for i, (source, target) in enumerate(zip(sources, targets))
    ]


def query_kernel(
    layer, xn_ref, act_ref, w_in, query, w_key, w_val, gate, w_query, w_gate, sems
):
    fetches = prepare(
        [w_in.at[layer, k] for k in range(4)], [w_query, w_key, w_val, w_gate], sems
    )
    for k in (0, 3, 1, 2):
        fetches[k].start()
    fetches[0].wait()
    query[...] = dot(xn_ref[...], w_query[...]).astype(BF16)
    fetches[3].wait()
    gate[...] = jax.nn.sigmoid(dot(normed(act_ref[...]).astype(BF16), w_gate[...]))
    fetches[1].wait()
    fetches[2].wait()


def attention_kernel(mask_ref, query, here_ref, came_ref, low, high, w_key, w_val, out_ref):
    rows, width = query.shape
    cols = here_ref.shape[0]
    heads = low.shape[1]
    hsize = width // heads
    span = low.shape[2]
    row, col, _ = device()
    mine = col * cols // rows == row
    key_xn = jnp.where(mine, here_ref[...].astype(F32), came_ref[...].astype(F32))
    key_xn = jnp.concatenate([key_xn, jnp.zeros((span - cols, width), F32)], 0).astype(BF16)
    keys = dot(key_xn, w_key[...]).astype(BF16)
    vals = dot(key_xn, w_val[...]).astype(BF16)
    tokens = mask_ref.shape[0]
    count = jnp.int32(0)
    for bit in range(tokens.bit_length() - 1, -1, -1):
        longer = count + (1 << bit)
        inside = longer <= tokens
        last = mask_ref[jnp.where(inside, longer - 1, 0)]
        count = jnp.where(inside & (last == 1), longer, count)
    valid = iota((1, span), 1) + col * cols < count
    valid = valid & (iota((1, span), 1) < cols)
    group = heads // 2
    part = group * hsize
    lane = iota((1, part), 1) // hsize
    spot = iota((1, span), 1)
    levels = jnp.zeros((rows, span), F32)
    for g in range(2):
        wide = slice(g * part, (g + 1) * part)
        kg, vg = keys[:, wide], vals[:, wide]
        picks = [(lane == h).astype(BF16) for h in range(group)]
        stacked = jnp.concatenate([kg * p for p in picks], 0)
        scores = dot_nt(query[:, wide], stacked) * (1.0 / math.sqrt(hsize))
        probs = []
        for h in range(group):
            head = g * group + h
            bias = jnp.concatenate([low[:, head, :], high[:, head, :]], 0)
            score = scores[:, h * span : (h + 1) * span] + bias
            score = jnp.where(valid, score, -1000000000.0)
            top = jnp.max(score, -1, keepdims=True)
            expd = jnp.exp(score - top)
            total = jnp.sum(expd, -1, keepdims=True)
            probs.append((expd / total).astype(BF16))
            levels = jnp.where(spot % heads == head, top + jnp.log(total), levels)
        stacked = jnp.concatenate([vg * p for p in picks], 0)
        out_ref[:, wide] = dot(jnp.concatenate(probs, 1), stacked).astype(BF16)
    high = levels.astype(BF16).astype(F32)
    rest = levels - high
    middle = rest.astype(BF16).astype(F32)
    low = rest - middle
    packed = jnp.where(spot < heads, high, jnp.where(spot < 2 * heads, middle, low))
    out_ref[:, width:] = jnp.where(spot < 3 * heads, packed, 0.0).astype(BF16)


def mix_kernel(layer, heads, message, act_ref, gate, w_out, act_out, w_mix, sems):
    (copy,) = prepare([w_out.at[layer]], [w_mix], sems)
    copy.start()
    width = act_ref.shape[1]
    hsize = width // heads
    parts = [message[j, :, width:].astype(F32) for j in range(message.shape[0])]
    span = parts[0].shape[1]
    levels = [
        p + pltpu.roll(p, span - heads, 1) + pltpu.roll(p, span - 2 * heads, 1) for p in parts
    ]
    top = functools.reduce(jnp.maximum, levels)
    weights = [jnp.exp(level - top) for level in levels]
    whole = functools.reduce(jnp.add, weights)
    lane = iota((1, span), 1)
    row = iota((span, width), 0)
    expand = (row % heads == iota((span, width), 1) // hsize) & (row < 2 * heads)
    expand = expand.astype(F32).astype(BF16)
    packed = []
    for weight in weights:
        weight = weight / whole
        high = weight.astype(BF16).astype(F32)
        both = jnp.where(lane < heads, high, pltpu.roll(weight - high, heads, 1))
        packed.append(jnp.where(lane < 2 * heads, both, 0.0))
    spread = dot(jnp.concatenate(packed, 0).astype(BF16), expand)
    own = act_ref.shape[0]
    attn = jnp.zeros(act_ref.shape, F32)
    for j in range(message.shape[0]):
        attn = attn + spread[j * own : (j + 1) * own] * message[j, :, :width].astype(F32)
    gated = (gate[...] * attn).astype(BF16)
    copy.wait()
    act_out[...] = act_ref[...] + dot(gated, w_mix[...])


def mix(layer, message, act, gate, w_out, heads):
    own, width = act.shape
    return call(
        functools.partial(mix_kernel, layer, heads),
        jax.ShapeDtypeStruct((own, width), F32),
        message,
        act,
        gate,
        far=(w_out,),
        scratch=[pltpu.VMEM((width, width), BF16), pltpu.SemaphoreType.DMA((1,))],
        grant=48,
        flops=4 * own * width * width,
        moved=4 * width * width,
    )


def transition_kernel(groups, pieces, act_ref, *refs):
    others, refs = refs[: groups - 1], refs[groups - 1 :]
    sources = []
    for number in pieces:
        sources.append(refs[:number])
        refs = refs[number:]
    base, send, w_first, w_second, sems = refs
    count, hid = w_second.shape[:2]
    plan = []
    for wanted, target in (((0, 2 * hid), w_first), ((2 * hid, 3 * hid), w_second)):
        for j, source in enumerate(sources):
            begin = 0
            for ref in source:
                end = begin + ref.shape[0]
                low, high = max(begin, wanted[0]), min(end, wanted[1])
                if low < high:
                    near = target.at[j, pl.ds(low - wanted[0], high - low)]
                    plan.append((target is w_first, j, ref.at[pl.ds(low - begin, high - low)], near))
                begin = end
    fetches = prepare([item[2] for item in plan], [item[3] for item in plan], sems)
    for copy in fetches:
        copy.start()

    def arrived(first, j):
        for item, copy in zip(plan, fetches):
            if item[:2] == (first, j):
                copy.wait()

    group = device()[1] // 4
    came = [ref[...] for ref in (act_ref, *others)]
    ordered = []
    for place in range(groups):
        rows = came[0]
        for d in range(1, groups):
            rows = jnp.where((group - place + groups) % groups == d, came[d], rows)
        ordered.append(rows)
    act = jnp.concatenate(ordered, 0)
    rows = normed(act).astype(BF16)
    total = jnp.zeros(act.shape, F32)
    hidden = []
    for j in range(count):
        arrived(True, j)
        both = dot_nt(rows, w_first[j])
        left, right = both[:, :hid], both[:, hid:]
        hidden.append((left * jax.nn.sigmoid(left) * right).astype(BF16))
    for j in range(count):
        arrived(False, j)
        total = total + dot(hidden[j], w_second[j])
    base[...] = act + total
    send[...] = total.astype(BF16)


def transition(act, others, weights):
    own, width = act.shape
    blocks = len(weights)
    hid = sum(part.shape[0] for part in weights[0]) // 3
    parts = [part for source in weights for part in source]
    return call(
        functools.partial(transition_kernel, len(others) + 1, [len(source) for source in weights]),
        [jax.ShapeDtypeStruct(((len(others) + 1) * own, width), kind) for kind in (F32, BF16)],
        act,
        *others,
        far=parts,
        scratch=[
            pltpu.VMEM((blocks, 2 * hid, width), BF16),
            pltpu.VMEM((blocks, hid, width), BF16),
            pltpu.SemaphoreType.DMA((2 * len(parts),)),
        ],
        grant=48,
        flops=12 * own * hid * width * blocks,
        moved=6 * hid * width * blocks,
    )


def close_kernel(project, act_ref, *refs):
    *refs, act_out, out = refs
    if project:
        *refs, tok_atom = refs
    act = act_ref[...]
    for ref in refs:
        act = act + ref[...].astype(F32)
    own = act_out.shape[0]
    mine = act[:own]
    for k in range(1, act.shape[0] // own):
        mine = jnp.where(device()[1] // 4 == k, act[k * own : (k + 1) * own], mine)
    act_out[...] = mine
    normal = normed(act).astype(BF16)
    if project:
        normal = dot(normal, tok_atom[...]).astype(BF16)
    out[...] = normal


def close(own, act, parts, tok_atom):
    rows, width = act.shape
    project = tok_atom is not None
    last = tok_atom.shape[1] if project else width
    return call(
        functools.partial(close_kernel, project),
        [jax.ShapeDtypeStruct((own, width), F32), jax.ShapeDtypeStruct((rows, last), BF16)],
        act,
        *parts,
        *([tok_atom] if project else []),
        flops=10**7,
        moved=10**6,
    )


def row_of(mine, own):
    nrow, ncol = lax.axis_size("row"), lax.axis_size("col")
    parts = [mine]
    for flip in range(1, 4):
        parts.append(
            lax.ppermute(mine, ("row", "col"), [(i, i ^ flip) for i in range(nrow * ncol)])
        )
    low = lax.axis_index("col") % 4
    ordered = []
    for place in range(4):
        rows = parts[place]
        for flip in range(1, 4):
            rows = jnp.where(low == flip, parts[place ^ flip], rows)
        ordered.append(rows.reshape(-1, 1, own, mine.shape[1]))
    return jnp.concatenate(ordered, 1).reshape(-1, mine.shape[1])


def key_source(rows, cols):
    nrow, ncol = lax.axis_size("row"), lax.axis_size("col")
    shares = rows // cols
    pairs = []
    for owner in range(nrow):
        free = [list(range(share, ncol, shares)) for share in range(shares)]
        for r in range(nrow):
            for share in range(shares):
                if r != owner:
                    spot = (2 * ((r + owner) % 2) + share) % (ncol // shares) * shares + share
                    source = spot if spot in free[share] else free[share][0]
                    free[share].remove(source)
                    pairs.append((owner * ncol + source, r * ncol + owner * shares + share))
    return pairs


def body(
    atom_feat,
    atom_token,
    window_start,
    token_cond,
    token_mask,
    pair,
    enc_in,
    enc_out,
    pool_weight,
    tok_in,
    tok_out,
    pair_weight,
    trans_in,
    trans_out,
    tok_atom,
    dec_in,
    dec_out,
    pos_out,
):
    nrow, ncol = lax.axis_size("row"), lax.axis_size("col")
    everyone = ("row", "col")
    count = nrow * ncol
    me_col = lax.axis_index("col")
    rows, width = token_cond.shape
    cols = pair.shape[1]
    heads = pair_weight.shape[2]
    own = rows // ncol
    atoms, afeat = atom_feat.shape
    natom = atoms * count
    nblk = atoms // QB

    hid = trans_out.shape[1]
    feat = call(
        functools.partial(feat_kernel, rows),
        jax.ShapeDtypeStruct((atoms + EXTRA, afeat), BF16),
        atom_feat,
        atom_token[None],
        scalars=(window_start,),
        grant=48,
        moved=10**5,
    )
    up = [(i, i + 1) for i in range(count - 1)]
    prev = lax.ppermute(feat, everyone, up)
    after = lax.ppermute(feat, everyone, [(b, a) for a, b in up])
    _, first_part, second_part = lax.optimization_barrier(
        (feat, jnp.swapaxes(trans_in, 2, 3), trans_out)
    )
    matrix = jax.ShapeDtypeStruct((3 * hid, width), BF16)
    half = jax.ShapeDtypeStruct((3 * hid // 2, width), BF16)
    pieces = call(
        pack_kernel,
        [matrix, half, half] * BLOCKS,
        first_part,
        second_part,
        grant=48,
        moved=12 * trans_out.size,
    )
    packed, upper, lower = pieces[::3], pieces[1::3], pieces[2::3]
    prev, after, early = lax.optimization_barrier((prev, after, upper[0]))
    neighbour = [(i, i ^ 2) for i in range(count)]
    sibling = [(i, i ^ 1) for i in range(count)]
    across = [[lax.ppermute(early, everyone, neighbour)], []]

    ext, copies = call(
        functools.partial(encoder_kernel, natom),
        [
            jax.ShapeDtypeStruct((atoms + 2 * HALO, afeat), BF16),
            jax.ShapeDtypeStruct((ncol, atoms + EXTRA, afeat), BF16),
        ],
        feat,
        prev,
        after,
        enc_in,
        enc_out,
        flops=10**8,
        moved=10**6,
    )
    span = -(-cols // 128) * 128
    half = rows // 2
    step = 24

    def bias_of(part, weights):
        return pl.pallas_call(
            bias_kernel,
            grid=(half // step,),
            out_shape=[jax.ShapeDtypeStruct((half, heads, span), F32)] * BLOCKS,
            in_specs=[
                pl.BlockSpec(
                    (step, cols, pair.shape[2]), lambda i: (i + part * (half // step), 0, 0)
                ),
                pl.BlockSpec(weights.shape, lambda i: (0, 0)),
            ],
            out_specs=[pl.BlockSpec((step, heads, span), lambda i: (i, 0, 0))] * BLOCKS,
            compiler_params=pltpu.CompilerParams(vmem_limit_bytes=(52 if part else 60) * MIB),
            cost_estimate=pl.CostEstimate(
                flops=2 * 10**9, bytes_accessed=4 * 10**6, transcendentals=0
            ),
        )(pair, weights)

    weights = jnp.swapaxes(pair_weight, 1, 2).reshape(BLOCKS * heads, -1)
    copies, first_weights = lax.optimization_barrier((copies, weights))
    low = bias_of(0, first_weights)
    both = lax.all_to_all(copies, "col", 0, 0)
    both, low, across[0][0] = lax.optimization_barrier((both, low, across[0][0]))

    act, xn, send = call(
        pool_kernel,
        [
            jax.ShapeDtypeStruct((own, width), F32),
            jax.ShapeDtypeStruct((rows, width), BF16),
            jax.ShapeDtypeStruct((cols, width), BF16),
        ],
        both,
        pool_weight,
        token_cond,
        flops=10**9,
        moved=10**6,
    )

    pairs = key_source(rows, cols)
    share = me_col % (rows // cols)
    peers = ncol // 4
    shifts = [
        [(r * ncol + c, r * ncol + (c + 4 * d) % ncol) for r in range(nrow) for c in range(ncol)]
        for d in range(peers)
    ]
    xn, weights = lax.optimization_barrier((xn, weights))
    beside, beyond = [], [[], []]
    for layer in range(BLOCKS):
        last = layer == BLOCKS - 1
        if layer:
            send = lax.dynamic_slice_in_dim(xn, share * cols, cols, 0)
            send, xn = lax.optimization_barrier((send, xn))
        came = lax.ppermute(send, everyone, pairs)
        matrix = jax.ShapeDtypeStruct((width, width), BF16)
        query, w_key, w_val, gate = call(
            functools.partial(query_kernel, layer),
            [
                jax.ShapeDtypeStruct((rows, width), BF16),
                matrix,
                matrix,
                jax.ShapeDtypeStruct((own, width), F32),
            ],
            xn,
            act,
            far=(tok_in,),
            scratch=[pltpu.VMEM((width, width), BF16)] * 2 + [pltpu.SemaphoreType.DMA((4,))],
            grant=48,
            flops=2 * rows * width * width,
            moved=8 * width * width,
        )
        if not layer:
            high = list(bias_of(1, weights))
            high[0], late, *ready = lax.optimization_barrier(
                (high[0], lower[0], across[0][0], *packed)
            )
            across[0].append(lax.ppermute(late, everyone, neighbour))
            beyond[0].append(lax.ppermute(ready[0], everyone, sibling))
            beside = [lax.ppermute(part, everyone, sibling) for part in ready[1:]]
        else:
            beyond[1].append(lax.ppermute(ready, everyone, sibling))
            query, late = lax.optimization_barrier((query, lower[1]))
            across[1].append(lax.ppermute(late, everyone, neighbour))
        message = call(
            attention_kernel,
            jax.ShapeDtypeStruct((rows, width + span), BF16),
            query,
            send,
            came,
            low[layer],
            high[layer],
            w_key,
            w_val,
            scalars=(token_mask,),
            grant=16,
            flops=10**9,
            moved=8 * 10**6,
        )
        message = lax.all_to_all(message.reshape(ncol, own, -1), "col", 0, 0)
        if not layer:
            message, ready = lax.optimization_barrier((message, upper[1]))
            across[1].append(lax.ppermute(ready, everyone, neighbour))
        act = mix(layer, message, act, gate, tok_out, heads)
        came_rows = [lax.ppermute(act, everyone, shifts[d]) for d in range(1, peers)]
        act, ready = lax.optimization_barrier((act, across[layer][1]))
        beyond[layer].append(lax.ppermute(ready, everyone, sibling))
        act, part = transition(
            act, came_rows, ([packed[layer]], [beside[layer]], across[layer], beyond[layer])
        )
        parts = [lax.ppermute(part, everyone, shifts[d]) for d in range(1, peers)]
        act, mine = close(own, act, parts, tok_atom if last else None)
        if not last:
            mine, ready = lax.optimization_barrier((mine, across[1][0]))
        gathered = row_of(mine, own)
        if not last:
            xn = gathered

    bounds = [(r * ncol - 1, r * ncol) for r in range(1, nrow)]
    bounds += [(b, a) for a, b in bounds]
    edge = jnp.where(me_col == 0, gathered[:HALO], gathered[rows - HALO :])
    edge = lax.ppermute(edge, everyone, bounds)

    return call(
        functools.partial(decoder_kernel, natom),
        jax.ShapeDtypeStruct((pos_out.shape[0], atoms), F32),
        ext,
        feat,
        prev,
        after,
        gathered,
        edge,
        dec_in,
        dec_out,
        pos_out,
        flops=10**8,
        moved=10**6,
    )


def solution(mesh):
    in_specs = (
        P(("row", "col"), None),
        P(("row", "col")),
        P(("row", "col")),
        P("row", None),
        P(),
        P("row", "col", None),
        P(),
        P(),
        P(),
        P(),
        P(),
        P(),
        P(None, None, None, "col"),
        P(None, "col", None),
        P(),
        P(),
        P(),
        P(),
    )
    out_specs = P(None, ("row", "col"))
    return jax.shard_map(body, mesh=mesh, in_specs=in_specs, out_specs=out_specs, check_vma=False)
```

```python
import functools
import math

import jax
import jax.numpy as jnp
from jax import lax
from jax.experimental import pallas as pl
from jax.experimental.pallas import tpu as pltpu
from jax.sharding import PartitionSpec as P

HA = 4
QB = 32
KW = 128
HALO = 64
BLOCKS = 2
EXTRA = 16
MIB = 1 << 20
F32 = jnp.float32
BF16 = jnp.bfloat16


def call(kernel, outs, *args, scalars=(), far=(), scratch=(), grant=8, flops=0, moved=0):
    smem = pl.BlockSpec(memory_space=pltpu.SMEM)
    vmem = pl.BlockSpec(memory_space=pltpu.VMEM)
    hbm = pl.BlockSpec(memory_space=pltpu.HBM)
    return pl.pallas_call(
        kernel,
        out_shape=outs,
        in_specs=[smem] * len(scalars) + [vmem] * len(args) + [hbm] * len(far),
        out_specs=jax.tree.map(lambda _: vmem, outs),
        scratch_shapes=list(scratch),
        compiler_params=pltpu.CompilerParams(vmem_limit_bytes=grant * MIB),
        cost_estimate=pl.CostEstimate(flops=flops, bytes_accessed=moved, transcendentals=0),
    )(*scalars, *args, *far)


def dot(a, b):
    return jnp.dot(a, b, preferred_element_type=F32)


def dot_nt(a, b):
    return lax.dot_general(a, b, (((1,), (1,)), ((), ())), preferred_element_type=F32)


def dot_tn(a, b):
    return lax.dot_general(a, b, (((0,), (0,)), ((), ())), preferred_element_type=F32)


def normed(x):
    x = x.astype(F32)
    cent = x - jnp.mean(x, -1, keepdims=True)
    var = jnp.mean(cent * cent, -1, keepdims=True)
    return cent * lax.rsqrt(var + 1e-05)


def iota(shape, dim):
    return lax.broadcasted_iota(jnp.int32, shape, dim)


def device():
    row, col = lax.axis_index("row"), lax.axis_index("col")
    return row, col, row * lax.axis_size("col") + col


def window_mask(shifts, first, natom, nkeys):
    shape = (len(shifts) * QB, nkeys)
    block = iota(shape, 0) // QB
    low = jnp.zeros(shape, jnp.int32)
    for i, shift in enumerate(shifts):
        low = jnp.where(block == i, shift + QB * i, low)
    key = iota(shape, 1)
    atom = key + first
    return (key >= low) & (key < low + KW) & (atom >= 0) & (atom < natom)


def attend(x, xn, gate, query, keys, vals, mask, w_out):
    width = x.shape[1]
    hsize = width // HA
    lane = iota((1, width), 1) // hsize
    outs = jnp.zeros(x.shape, F32)
    for h in range(HA):
        pick = (lane == h).astype(BF16)
        scores = dot_nt(query, keys * pick) * (1.0 / math.sqrt(hsize))
        scores = jnp.where(mask, scores, -1000000000.0)
        top = jnp.max(scores, -1, keepdims=True)
        expd = jnp.exp(scores - top)
        total = jnp.sum(expd, -1, keepdims=True)
        outs = outs + dot(expd.astype(BF16), vals * pick) / total
    gated = (jax.nn.sigmoid(gate) * outs).astype(BF16)
    return (x.astype(F32) + dot(gated, w_out)).astype(BF16)


def shifts_of(tail_ref, lanes):
    tail = tail_ref[tail_ref.shape[0] - EXTRA :, :].astype(F32)
    return [tail[1:2, k : k + 1].astype(jnp.int32) for k in lanes]


def encoder_kernel(natom, own_ref, prev_ref, next_ref, w_in, w_out, ext_ref, all_ref):
    rows = own_ref.shape[0] - EXTRA
    nblk = rows // QB
    half = HALO // QB
    x = jnp.concatenate([prev_ref[:rows], own_ref[:rows], next_ref[:rows]], 0)
    xn = normed(x).astype(BF16)
    keys = dot(xn, w_in[1]).astype(BF16)
    vals = dot(xn, w_in[2]).astype(BF16)
    qx, qn = x[HALO : 3 * rows - HALO], xn[HALO : 3 * rows - HALO]
    query = dot(qn, w_in[0]).astype(BF16)
    gate = dot(qn, w_in[3])
    shifts = (
        shifts_of(prev_ref, range(nblk - half, nblk))
        + shifts_of(own_ref, range(nblk))
        + shifts_of(next_ref, range(half))
    )
    first = device()[2] * rows - rows
    for part in range(2):
        mine = slice(part * rows, (part + 1) * rows)
        seen = slice(part * rows, (part + 2) * rows)
        mask = window_mask(
            shifts[part * nblk : (part + 1) * nblk], first + part * rows, natom, 2 * rows
        )
        ext_ref[mine] = attend(
            qx[mine], qn[mine], gate[mine], query[mine], keys[seen], vals[seen], mask, w_out[...]
        )
    new = ext_ref[HALO : HALO + rows]
    tail = own_ref[rows:]
    for j in range(all_ref.shape[0]):
        all_ref[j, :rows] = new
        all_ref[j, rows:] = tail


def pool_kernel(both_ref, weight, cond, act_ref, xn_ref, send_ref):
    count, rows = both_ref.shape[0], both_ref.shape[1] - EXTRA
    tokens = cond.shape[0]
    sums = jnp.zeros(cond.shape, F32)
    counts = jnp.zeros((tokens, 1), F32)
    step = 4 if count % 4 == 0 else 1
    for j in range(0, count, step):
        atoms = jnp.concatenate([both_ref[j + k, :rows] for k in range(step)], 0)
        feats = jnp.maximum(dot(atoms, weight[...]), 0.0).astype(BF16)
        spot = jnp.concatenate(
            [both_ref[j + k, rows:].astype(F32)[0:1] for k in range(step)], 1
        ).astype(jnp.int32)
        onehot = (iota((tokens, step * rows), 0) == spot).astype(F32)
        sums = sums + dot(onehot.astype(BF16), feats)
        counts = counts + jnp.sum(onehot, -1, keepdims=True)
    act = sums / counts + cond[...].astype(F32)
    xn = normed(act)
    xn_ref[...] = xn.astype(BF16)
    cols = send_ref.shape[0]
    part = xn[:cols]
    for k in range(1, tokens // cols):
        part = jnp.where(device()[1] % (tokens // cols) == k, xn[k * cols : (k + 1) * cols], part)
    send_ref[...] = part.astype(BF16)
    own = act_ref.shape[0]
    col = device()[1]
    mine = act[:own]
    for c in range(1, tokens // own):
        mine = jnp.where(col == c, act[c * own : (c + 1) * own], mine)
    act_ref[...] = mine


def decoder_kernel(
    natom, x1_ref, own_ref, prev_ref, next_ref, proj_ref, edge_ref, w_in, w_out, pos, out
):
    rows = own_ref.shape[0] - EXTRA
    proj = proj_ref[...].astype(F32)
    edge = edge_ref[...].astype(F32)
    tokens = proj.shape[0]
    _, col, me = device()
    rest = tokens - HALO
    below = jnp.where(col == 0, edge, proj[rest:])
    above = jnp.where(col == lax.axis_size("col") - 1, edge, proj[:HALO])
    tables = (
        jnp.concatenate([proj[:rest], below], 0),
        proj,
        jnp.concatenate([above, proj[HALO:]], 0),
    )
    spread = []
    for table, ref in zip(tables, (prev_ref, own_ref, next_ref)):
        spot = ref[rows:].astype(F32)[0:1].astype(jnp.int32)
        onehot = (iota((tokens, rows), 0) == spot).astype(F32).astype(BF16)
        spread.append(dot_tn(onehot, table.astype(BF16)))
    spread = jnp.concatenate([spread[0][rows - HALO :], spread[1], spread[2][:HALO]], 0)
    x = (x1_ref[...].astype(F32) + spread).astype(BF16)
    xn = normed(x).astype(BF16)
    keys = dot(xn, w_in[1]).astype(BF16)
    vals = dot(xn, w_in[2]).astype(BF16)
    qx, qn = x[HALO : HALO + rows], xn[HALO : HALO + rows]
    query = dot(qn, w_in[0]).astype(BF16)
    gate = dot(qn, w_in[3])
    shifts = shifts_of(own_ref, range(rows // QB))
    mask = window_mask(shifts, me * rows - HALO, natom, 2 * rows)
    third = attend(qx, qn, gate, query, keys, vals, mask, w_out[...])
    out[...] = dot_nt(pos[...], normed(third).astype(BF16))


def feat_kernel(row_tokens, starts, feat, token, own):
    rows, width = feat.shape
    row, _, me = device()
    nblk = starts.shape[0]
    lane = iota((EXTRA, width), 1)
    line = iota((EXTRA, width), 0)
    tail = jnp.where(line == 0, token[...] - row * row_tokens, 0)
    for k in range(nblk):
        shift = starts[k] - QB * (me * nblk + k) + HALO
        tail = jnp.where((line == 1) & (lane == k), shift, tail)
    own[:rows] = feat[...]
    own[rows:] = tail.astype(F32).astype(BF16)


def pack_kernel(first, second, *outs):
    hid = second.shape[1]
    part = 3 * hid // 2
    for layer in range(BLOCKS):
        whole, upper, lower = outs[3 * layer : 3 * layer + 3]
        whole[:hid] = first[layer, 0]
        whole[hid : 2 * hid] = first[layer, 1]
        whole[2 * hid :] = second[layer]
        upper[...] = whole[:part]
        lower[...] = whole[part:]


def bias_kernel(pair_ref, weight, *outs):
    rows, cols, _ = pair_ref.shape
    _, heads, pad = outs[0].shape
    pad = pad - cols

    for q in range(rows):
        bias = dot_nt(weight[...], pair_ref[q])
        bias = jnp.concatenate([bias, jnp.zeros((bias.shape[0], pad), F32)], 1)
        for layer, out in enumerate(outs):
            out[q] = bias[layer * heads : (layer + 1) * heads]


def prepare(sources, targets, sems):
    return [
        pltpu.make_async_copy(source, target, sems.at[i])
        for i, (source, target) in enumerate(zip(sources, targets))
    ]


def query_kernel(
    layer, xn_ref, act_ref, w_in, query, w_key, w_val, gate, w_query, w_gate, sems
):
    fetches = prepare(
        [w_in.at[layer, k] for k in range(4)], [w_query, w_key, w_val, w_gate], sems
    )
    for k in (0, 3, 1, 2):
        fetches[k].start()
    fetches[0].wait()
    query[...] = dot(xn_ref[...], w_query[...]).astype(BF16)
    fetches[3].wait()
    gate[...] = jax.nn.sigmoid(dot(normed(act_ref[...]).astype(BF16), w_gate[...]))
    fetches[1].wait()
    fetches[2].wait()


def attention_kernel(mask_ref, query, here_ref, came_ref, low, high, w_key, w_val, out_ref):
    rows, width = query.shape
    cols = here_ref.shape[0]
    heads = low.shape[1]
    hsize = width // heads
    span = low.shape[2]
    row, col, _ = device()
    mine = col * cols // rows == row
    key_xn = jnp.where(mine, here_ref[...].astype(F32), came_ref[...].astype(F32))
    key_xn = jnp.concatenate([key_xn, jnp.zeros((span - cols, width), F32)], 0).astype(BF16)
    keys = dot(key_xn, w_key[...]).astype(BF16)
    vals = dot(key_xn, w_val[...]).astype(BF16)
    tokens = mask_ref.shape[0]
    count = jnp.int32(0)
    for bit in range(tokens.bit_length() - 1, -1, -1):
        longer = count + (1 << bit)
        inside = longer <= tokens
        last = mask_ref[jnp.where(inside, longer - 1, 0)]
        count = jnp.where(inside & (last == 1), longer, count)
    valid = iota((1, span), 1) + col * cols < count
    valid = valid & (iota((1, span), 1) < cols)
    group = heads // 2
    part = group * hsize
    lane = iota((1, part), 1) // hsize
    spot = iota((1, span), 1)
    levels = jnp.zeros((rows, span), F32)
    for g in range(2):
        wide = slice(g * part, (g + 1) * part)
        kg, vg = keys[:, wide], vals[:, wide]
        picks = [(lane == h).astype(BF16) for h in range(group)]
        stacked = jnp.concatenate([kg * p for p in picks], 0)
        scores = dot_nt(query[:, wide], stacked) * (1.0 / math.sqrt(hsize))
        probs = []
        for h in range(group):
            head = g * group + h
            bias = jnp.concatenate([low[:, head, :], high[:, head, :]], 0)
            score = scores[:, h * span : (h + 1) * span] + bias
            score = jnp.where(valid, score, -1000000000.0)
            top = jnp.max(score, -1, keepdims=True)
            expd = jnp.exp(score - top)
            total = jnp.sum(expd, -1, keepdims=True)
            probs.append((expd / total).astype(BF16))
            levels = jnp.where(spot % heads == head, top + jnp.log(total), levels)
        stacked = jnp.concatenate([vg * p for p in picks], 0)
        out_ref[:, wide] = dot(jnp.concatenate(probs, 1), stacked).astype(BF16)
    high = levels.astype(BF16).astype(F32)
    rest = levels - high
    middle = rest.astype(BF16).astype(F32)
    low = rest - middle
    packed = jnp.where(spot < heads, high, jnp.where(spot < 2 * heads, middle, low))
    out_ref[:, width:] = jnp.where(spot < 3 * heads, packed, 0.0).astype(BF16)


def mix_kernel(layer, heads, message, act_ref, gate, w_out, act_out, w_mix, sems):
    (copy,) = prepare([w_out.at[layer]], [w_mix], sems)
    copy.start()
    width = act_ref.shape[1]
    hsize = width // heads
    parts = [message[j, :, width:].astype(F32) for j in range(message.shape[0])]
    span = parts[0].shape[1]
    levels = [
        p + pltpu.roll(p, span - heads, 1) + pltpu.roll(p, span - 2 * heads, 1) for p in parts
    ]
    top = functools.reduce(jnp.maximum, levels)
    weights = [jnp.exp(level - top) for level in levels]
    whole = functools.reduce(jnp.add, weights)
    lane = iota((1, span), 1)
    row = iota((span, width), 0)
    expand = (row % heads == iota((span, width), 1) // hsize) & (row < 2 * heads)
    expand = expand.astype(F32).astype(BF16)
    packed = []
    for weight in weights:
        weight = weight / whole
        high = weight.astype(BF16).astype(F32)
        both = jnp.where(lane < heads, high, pltpu.roll(weight - high, heads, 1))
        packed.append(jnp.where(lane < 2 * heads, both, 0.0))
    spread = dot(jnp.concatenate(packed, 0).astype(BF16), expand)
    own = act_ref.shape[0]
    attn = jnp.zeros(act_ref.shape, F32)
    for j in range(message.shape[0]):
        attn = attn + spread[j * own : (j + 1) * own] * message[j, :, :width].astype(F32)
    gated = (gate[...] * attn).astype(BF16)
    copy.wait()
    act_out[...] = act_ref[...] + dot(gated, w_mix[...])


def mix(layer, message, act, gate, w_out, heads):
    own, width = act.shape
    return call(
        functools.partial(mix_kernel, layer, heads),
        jax.ShapeDtypeStruct((own, width), F32),
        message,
        act,
        gate,
        far=(w_out,),
        scratch=[pltpu.VMEM((width, width), BF16), pltpu.SemaphoreType.DMA((1,))],
        grant=48,
        flops=4 * own * width * width,
        moved=4 * width * width,
    )


def transition_kernel(groups, pieces, act_ref, *refs):
    others, refs = refs[: groups - 1], refs[groups - 1 :]
    sources = []
    for number in pieces:
        sources.append(refs[:number])
        refs = refs[number:]
    base, send, w_first, w_second, sems = refs
    count, hid = w_second.shape[:2]
    plan = []
    for wanted, target in (((0, 2 * hid), w_first), ((2 * hid, 3 * hid), w_second)):
        for j, source in enumerate(sources):
            begin = 0
            for ref in source:
                end = begin + ref.shape[0]
                low, high = max(begin, wanted[0]), min(end, wanted[1])
                if low < high:
                    near = target.at[j, pl.ds(low - wanted[0], high - low)]
                    plan.append((target is w_first, j, ref.at[pl.ds(low - begin, high - low)], near))
                begin = end
    fetches = prepare([item[2] for item in plan], [item[3] for item in plan], sems)
    for copy in fetches:
        copy.start()

    def arrived(first, j):
        for item, copy in zip(plan, fetches):
            if item[:2] == (first, j):
                copy.wait()

    group = device()[1] // 4
    came = [ref[...] for ref in (act_ref, *others)]
    ordered = []
    for place in range(groups):
        rows = came[0]
        for d in range(1, groups):
            rows = jnp.where((group - place + groups) % groups == d, came[d], rows)
        ordered.append(rows)
    act = jnp.concatenate(ordered, 0)
    rows = normed(act).astype(BF16)
    total = jnp.zeros(act.shape, F32)
    hidden = []
    for j in range(count):
        arrived(True, j)
        both = dot_nt(rows, w_first[j])
        left, right = both[:, :hid], both[:, hid:]
        hidden.append((left * jax.nn.sigmoid(left) * right).astype(BF16))
    for j in range(count):
        arrived(False, j)
        total = total + dot(hidden[j], w_second[j])
    base[...] = act + total
    send[...] = total.astype(BF16)


def transition(act, others, weights):
    own, width = act.shape
    blocks = len(weights)
    hid = sum(part.shape[0] for part in weights[0]) // 3
    parts = [part for source in weights for part in source]
    return call(
        functools.partial(transition_kernel, len(others) + 1, [len(source) for source in weights]),
        [jax.ShapeDtypeStruct(((len(others) + 1) * own, width), kind) for kind in (F32, BF16)],
        act,
        *others,
        far=parts,
        scratch=[
            pltpu.VMEM((blocks, 2 * hid, width), BF16),
            pltpu.VMEM((blocks, hid, width), BF16),
            pltpu.SemaphoreType.DMA((2 * len(parts),)),
        ],
        grant=48,
        flops=12 * own * hid * width * blocks,
        moved=6 * hid * width * blocks,
    )


def close_kernel(project, act_ref, *refs):
    *refs, act_out, out = refs
    if project:
        *refs, tok_atom = refs
    act = act_ref[...]
    for ref in refs:
        act = act + ref[...].astype(F32)
    own = act_out.shape[0]
    mine = act[:own]
    for k in range(1, act.shape[0] // own):
        mine = jnp.where(device()[1] // 4 == k, act[k * own : (k + 1) * own], mine)
    act_out[...] = mine
    normal = normed(act).astype(BF16)
    if project:
        normal = dot(normal, tok_atom[...]).astype(BF16)
    out[...] = normal


def close(own, act, parts, tok_atom):
    rows, width = act.shape
    project = tok_atom is not None
    last = tok_atom.shape[1] if project else width
    return call(
        functools.partial(close_kernel, project),
        [jax.ShapeDtypeStruct((own, width), F32), jax.ShapeDtypeStruct((rows, last), BF16)],
        act,
        *parts,
        *([tok_atom] if project else []),
        flops=10**7,
        moved=10**6,
    )


def row_of(mine, own):
    nrow, ncol = lax.axis_size("row"), lax.axis_size("col")
    parts = [mine]
    for flip in range(1, 4):
        parts.append(
            lax.ppermute(mine, ("row", "col"), [(i, i ^ flip) for i in range(nrow * ncol)])
        )
    low = lax.axis_index("col") % 4
    ordered = []
    for place in range(4):
        rows = parts[place]
        for flip in range(1, 4):
            rows = jnp.where(low == flip, parts[place ^ flip], rows)
        ordered.append(rows.reshape(-1, 1, own, mine.shape[1]))
    return jnp.concatenate(ordered, 1).reshape(-1, mine.shape[1])


def key_source(rows, cols):
    nrow, ncol = lax.axis_size("row"), lax.axis_size("col")
    shares = rows // cols
    pairs = []
    for owner in range(nrow):
        free = [list(range(share, ncol, shares)) for share in range(shares)]
        for r in range(nrow):
            for share in range(shares):
                if r != owner:
                    spot = (2 * ((r + owner) % 2) + share) % (ncol // shares) * shares + share
                    source = spot if spot in free[share] else free[share][0]
                    free[share].remove(source)
                    pairs.append((owner * ncol + source, r * ncol + owner * shares + share))
    return pairs


def body(
    atom_feat,
    atom_token,
    window_start,
    token_cond,
    token_mask,
    pair,
    enc_in,
    enc_out,
    pool_weight,
    tok_in,
    tok_out,
    pair_weight,
    trans_in,
    trans_out,
    tok_atom,
    dec_in,
    dec_out,
    pos_out,
):
    nrow, ncol = lax.axis_size("row"), lax.axis_size("col")
    everyone = ("row", "col")
    count = nrow * ncol
    me_col = lax.axis_index("col")
    rows, width = token_cond.shape
    cols = pair.shape[1]
    heads = pair_weight.shape[2]
    own = rows // ncol
    atoms, afeat = atom_feat.shape
    natom = atoms * count
    nblk = atoms // QB

    hid = trans_out.shape[1]
    feat = call(
        functools.partial(feat_kernel, rows),
        jax.ShapeDtypeStruct((atoms + EXTRA, afeat), BF16),
        atom_feat,
        atom_token[None],
        scalars=(window_start,),
        grant=48,
        moved=10**5,
    )
    up = [(i, i + 1) for i in range(count - 1)]
    prev = lax.ppermute(feat, everyone, up)
    after = lax.ppermute(feat, everyone, [(b, a) for a, b in up])
    _, first_part, second_part = lax.optimization_barrier(
        (feat, jnp.swapaxes(trans_in, 2, 3), trans_out)
    )
    matrix = jax.ShapeDtypeStruct((3 * hid, width), BF16)
    half = jax.ShapeDtypeStruct((3 * hid // 2, width), BF16)
    pieces = call(
        pack_kernel,
        [matrix, half, half] * BLOCKS,
        first_part,
        second_part,
        grant=48,
        moved=12 * trans_out.size,
    )
    packed, upper, lower = pieces[::3], pieces[1::3], pieces[2::3]
    prev, after, early = lax.optimization_barrier((prev, after, upper[0]))
    neighbour = [(i, i ^ 2) for i in range(count)]
    sibling = [(i, i ^ 1) for i in range(count)]
    across = [[lax.ppermute(early, everyone, neighbour)], []]

    ext, copies = call(
        functools.partial(encoder_kernel, natom),
        [
            jax.ShapeDtypeStruct((atoms + 2 * HALO, afeat), BF16),
            jax.ShapeDtypeStruct((ncol, atoms + EXTRA, afeat), BF16),
        ],
        feat,
        prev,
        after,
        enc_in,
        enc_out,
        flops=10**8,
        moved=10**6,
    )
    span = -(-cols // 128) * 128
    half = rows // 2
    step = 24

    def bias_of(part, weights):
        return pl.pallas_call(
            bias_kernel,
            grid=(half // step,),
            out_shape=[jax.ShapeDtypeStruct((half, heads, span), F32)] * BLOCKS,
            in_specs=[
                pl.BlockSpec(
                    (step, cols, pair.shape[2]), lambda i: (i + part * (half // step), 0, 0)
                ),
                pl.BlockSpec(weights.shape, lambda i: (0, 0)),
            ],
            out_specs=[pl.BlockSpec((step, heads, span), lambda i: (i, 0, 0))] * BLOCKS,
            compiler_params=pltpu.CompilerParams(vmem_limit_bytes=(52 if part else 60) * MIB),
            cost_estimate=pl.CostEstimate(
                flops=2 * 10**9, bytes_accessed=4 * 10**6, transcendentals=0
            ),
        )(pair, weights)

    weights = jnp.swapaxes(pair_weight, 1, 2).reshape(BLOCKS * heads, -1)
    copies, first_weights = lax.optimization_barrier((copies, weights))
    low = bias_of(0, first_weights)
    both = lax.all_to_all(copies, "col", 0, 0)
    both, low, across[0][0] = lax.optimization_barrier((both, low, across[0][0]))

    act, xn, send = call(
        pool_kernel,
        [
            jax.ShapeDtypeStruct((own, width), F32),
            jax.ShapeDtypeStruct((rows, width), BF16),
            jax.ShapeDtypeStruct((cols, width), BF16),
        ],
        both,
        pool_weight,
        token_cond,
        flops=10**9,
        moved=10**6,
    )

    pairs = key_source(rows, cols)
    share = me_col % (rows // cols)
    peers = ncol // 4
    shifts = [
        [(r * ncol + c, r * ncol + (c + 4 * d) % ncol) for r in range(nrow) for c in range(ncol)]
        for d in range(peers)
    ]
    xn, weights = lax.optimization_barrier((xn, weights))
    beside, beyond = [], [[], []]
    for layer in range(BLOCKS):
        last = layer == BLOCKS - 1
        if layer:
            send = lax.dynamic_slice_in_dim(xn, share * cols, cols, 0)
            send, xn = lax.optimization_barrier((send, xn))
        came = lax.ppermute(send, everyone, pairs)
        matrix = jax.ShapeDtypeStruct((width, width), BF16)
        query, w_key, w_val, gate = call(
            functools.partial(query_kernel, layer),
            [
                jax.ShapeDtypeStruct((rows, width), BF16),
                matrix,
                matrix,
                jax.ShapeDtypeStruct((own, width), F32),
            ],
            xn,
            act,
            far=(tok_in,),
            scratch=[pltpu.VMEM((width, width), BF16)] * 2 + [pltpu.SemaphoreType.DMA((4,))],
            grant=48,
            flops=2 * rows * width * width,
            moved=8 * width * width,
        )
        if not layer:
            high = list(bias_of(1, weights))
            high[0], late, *ready = lax.optimization_barrier(
                (high[0], lower[0], *packed)
            )
            across[0].append(lax.ppermute(late, everyone, neighbour))
            beside = [lax.ppermute(part, everyone, sibling) for part in ready]
        else:
            query, late = lax.optimization_barrier((query, lower[1]))
            across[1].append(lax.ppermute(late, everyone, neighbour))
        message = call(
            attention_kernel,
            jax.ShapeDtypeStruct((rows, width + span), BF16),
            query,
            send,
            came,
            low[layer],
            high[layer],
            w_key,
            w_val,
            scalars=(token_mask,),
            grant=16,
            flops=10**9,
            moved=8 * 10**6,
        )
        message = lax.all_to_all(message.reshape(ncol, own, -1), "col", 0, 0)
        if not layer:
            message, ready = lax.optimization_barrier((message, upper[1]))
            across[1].append(lax.ppermute(ready, everyone, neighbour))
        act = mix(layer, message, act, gate, tok_out, heads)
        came_rows = [lax.ppermute(act, everyone, shifts[d]) for d in range(1, peers)]
        act, *ready = lax.optimization_barrier((act, *across[layer]))
        beyond[layer] = [lax.ppermute(part, everyone, sibling) for part in ready]
        act, part = transition(
            act, came_rows, ([packed[layer]], [beside[layer]], across[layer], beyond[layer])
        )
        parts = [lax.ppermute(part, everyone, shifts[d]) for d in range(1, peers)]
        act, mine = close(own, act, parts, tok_atom if last else None)
        if not last:
            mine, across[1][0] = lax.optimization_barrier((mine, across[1][0]))
        gathered = row_of(mine, own)
        if not last:
            xn = gathered

    bounds = [(r * ncol - 1, r * ncol) for r in range(1, nrow)]
    bounds += [(b, a) for a, b in bounds]
    edge = jnp.where(me_col == 0, gathered[:HALO], gathered[rows - HALO :])
    edge = lax.ppermute(edge, everyone, bounds)

    return call(
        functools.partial(decoder_kernel, natom),
        jax.ShapeDtypeStruct((pos_out.shape[0], atoms), F32),
        ext,
        feat,
        prev,
        after,
        gathered,
        edge,
        dec_in,
        dec_out,
        pos_out,
        flops=10**8,
        moved=10**6,
    )


def solution(mesh):
    in_specs = (
        P(("row", "col"), None),
        P(("row", "col")),
        P(("row", "col")),
        P("row", None),
        P(),
        P("row", "col", None),
        P(),
        P(),
        P(),
        P(),
        P(),
        P(),
        P(None, None, None, "col"),
        P(None, "col", None),
        P(),
        P(),
        P(),
        P(),
    )
    out_specs = P(None, ("row", "col"))
    return jax.shard_map(body, mesh=mesh, in_specs=in_specs, out_specs=out_specs, check_vma=False)
```

```python
import functools
import math

import jax
import jax.numpy as jnp
from jax import lax
from jax.experimental import pallas as pl
from jax.experimental.pallas import tpu as pltpu
from jax.sharding import PartitionSpec as P

HA = 4
QB = 32
KW = 128
HALO = 64
BLOCKS = 2
EXTRA = 16
MIB = 1 << 20
F32 = jnp.float32
BF16 = jnp.bfloat16


def call(kernel, outs, *args, scalars=(), far=(), scratch=(), grant=8, flops=0, moved=0):
    smem = pl.BlockSpec(memory_space=pltpu.SMEM)
    vmem = pl.BlockSpec(memory_space=pltpu.VMEM)
    hbm = pl.BlockSpec(memory_space=pltpu.HBM)
    return pl.pallas_call(
        kernel,
        out_shape=outs,
        in_specs=[smem] * len(scalars) + [vmem] * len(args) + [hbm] * len(far),
        out_specs=jax.tree.map(lambda _: vmem, outs),
        scratch_shapes=list(scratch),
        compiler_params=pltpu.CompilerParams(vmem_limit_bytes=grant * MIB),
        cost_estimate=pl.CostEstimate(flops=flops, bytes_accessed=moved, transcendentals=0),
    )(*scalars, *args, *far)


def dot(a, b):
    return jnp.dot(a, b, preferred_element_type=F32)


def dot_nt(a, b):
    return lax.dot_general(a, b, (((1,), (1,)), ((), ())), preferred_element_type=F32)


def dot_tn(a, b):
    return lax.dot_general(a, b, (((0,), (0,)), ((), ())), preferred_element_type=F32)


def normed(x):
    x = x.astype(F32)
    cent = x - jnp.mean(x, -1, keepdims=True)
    var = jnp.mean(cent * cent, -1, keepdims=True)
    return cent * lax.rsqrt(var + 1e-05)


def iota(shape, dim):
    return lax.broadcasted_iota(jnp.int32, shape, dim)


def device():
    row, col = lax.axis_index("row"), lax.axis_index("col")
    return row, col, row * lax.axis_size("col") + col


def window_mask(shifts, first, natom, nkeys):
    shape = (len(shifts) * QB, nkeys)
    block = iota(shape, 0) // QB
    low = jnp.zeros(shape, jnp.int32)
    for i, shift in enumerate(shifts):
        low = jnp.where(block == i, shift + QB * i, low)
    key = iota(shape, 1)
    atom = key + first
    return (key >= low) & (key < low + KW) & (atom >= 0) & (atom < natom)


def attend(x, xn, gate, query, keys, vals, mask, w_out):
    width = x.shape[1]
    hsize = width // HA
    lane = iota((1, width), 1) // hsize
    outs = jnp.zeros(x.shape, F32)
    for h in range(HA):
        pick = (lane == h).astype(BF16)
        scores = dot_nt(query, keys * pick) * (1.0 / math.sqrt(hsize))
        scores = jnp.where(mask, scores, -1000000000.0)
        top = jnp.max(scores, -1, keepdims=True)
        expd = jnp.exp(scores - top)
        total = jnp.sum(expd, -1, keepdims=True)
        outs = outs + dot(expd.astype(BF16), vals * pick) / total
    gated = (jax.nn.sigmoid(gate) * outs).astype(BF16)
    return (x.astype(F32) + dot(gated, w_out)).astype(BF16)


def shifts_of(tail_ref, lanes):
    tail = tail_ref[tail_ref.shape[0] - EXTRA :, :].astype(F32)
    return [tail[1:2, k : k + 1].astype(jnp.int32) for k in lanes]


def encoder_kernel(natom, own_ref, prev_ref, next_ref, w_in, w_out, ext_ref, all_ref):
    rows = own_ref.shape[0] - EXTRA
    nblk = rows // QB
    half = HALO // QB
    x = jnp.concatenate([prev_ref[:rows], own_ref[:rows], next_ref[:rows]], 0)
    xn = normed(x).astype(BF16)
    keys = dot(xn, w_in[1]).astype(BF16)
    vals = dot(xn, w_in[2]).astype(BF16)
    qx, qn = x[HALO : 3 * rows - HALO], xn[HALO : 3 * rows - HALO]
    query = dot(qn, w_in[0]).astype(BF16)
    gate = dot(qn, w_in[3])
    shifts = (
        shifts_of(prev_ref, range(nblk - half, nblk))
        + shifts_of(own_ref, range(nblk))
        + shifts_of(next_ref, range(half))
    )
    first = device()[2] * rows - rows
    for part in range(2):
        mine = slice(part * rows, (part + 1) * rows)
        seen = slice(part * rows, (part + 2) * rows)
        mask = window_mask(
            shifts[part * nblk : (part + 1) * nblk], first + part * rows, natom, 2 * rows
        )
        ext_ref[mine] = attend(
            qx[mine], qn[mine], gate[mine], query[mine], keys[seen], vals[seen], mask, w_out[...]
        )
    new = ext_ref[HALO : HALO + rows]
    tail = own_ref[rows:]
    for j in range(all_ref.shape[0]):
        all_ref[j, :rows] = new
        all_ref[j, rows:] = tail


def pool_kernel(both_ref, weight, cond, act_ref, xn_ref, send_ref):
    count, rows = both_ref.shape[0], both_ref.shape[1] - EXTRA
    tokens = cond.shape[0]
    sums = jnp.zeros(cond.shape, F32)
    counts = jnp.zeros((tokens, 1), F32)
    step = 4 if count % 4 == 0 else 1
    for j in range(0, count, step):
        atoms = jnp.concatenate([both_ref[j + k, :rows] for k in range(step)], 0)
        feats = jnp.maximum(dot(atoms, weight[...]), 0.0).astype(BF16)
        spot = jnp.concatenate(
            [both_ref[j + k, rows:].astype(F32)[0:1] for k in range(step)], 1
        ).astype(jnp.int32)
        onehot = (iota((tokens, step * rows), 0) == spot).astype(F32)
        sums = sums + dot(onehot.astype(BF16), feats)
        counts = counts + jnp.sum(onehot, -1, keepdims=True)
    act = sums / counts + cond[...].astype(F32)
    xn = normed(act)
    xn_ref[...] = xn.astype(BF16)
    cols = send_ref.shape[0]
    part = xn[:cols]
    for k in range(1, tokens // cols):
        part = jnp.where(device()[1] % (tokens // cols) == k, xn[k * cols : (k + 1) * cols], part)
    send_ref[...] = part.astype(BF16)
    own = act_ref.shape[0]
    col = device()[1]
    mine = act[:own]
    for c in range(1, tokens // own):
        mine = jnp.where(col == c, act[c * own : (c + 1) * own], mine)
    act_ref[...] = mine


def decoder_kernel(
    natom, x1_ref, own_ref, prev_ref, next_ref, proj_ref, edge_ref, w_in, w_out, pos, out
):
    rows = own_ref.shape[0] - EXTRA
    proj = proj_ref[...].astype(F32)
    edge = edge_ref[...].astype(F32)
    tokens = proj.shape[0]
    _, col, me = device()
    rest = tokens - HALO
    below = jnp.where(col == 0, edge, proj[rest:])
    above = jnp.where(col == lax.axis_size("col") - 1, edge, proj[:HALO])
    tables = (
        jnp.concatenate([proj[:rest], below], 0),
        proj,
        jnp.concatenate([above, proj[HALO:]], 0),
    )
    spread = []
    for table, ref in zip(tables, (prev_ref, own_ref, next_ref)):
        spot = ref[rows:].astype(F32)[0:1].astype(jnp.int32)
        onehot = (iota((tokens, rows), 0) == spot).astype(F32).astype(BF16)
        spread.append(dot_tn(onehot, table.astype(BF16)))
    spread = jnp.concatenate([spread[0][rows - HALO :], spread[1], spread[2][:HALO]], 0)
    x = (x1_ref[...].astype(F32) + spread).astype(BF16)
    xn = normed(x).astype(BF16)
    keys = dot(xn, w_in[1]).astype(BF16)
    vals = dot(xn, w_in[2]).astype(BF16)
    qx, qn = x[HALO : HALO + rows], xn[HALO : HALO + rows]
    query = dot(qn, w_in[0]).astype(BF16)
    gate = dot(qn, w_in[3])
    shifts = shifts_of(own_ref, range(rows // QB))
    mask = window_mask(shifts, me * rows - HALO, natom, 2 * rows)
    third = attend(qx, qn, gate, query, keys, vals, mask, w_out[...])
    out[...] = dot_nt(pos[...], normed(third).astype(BF16))


def feat_kernel(row_tokens, starts, feat, token, own):
    rows, width = feat.shape
    row, _, me = device()
    nblk = starts.shape[0]
    lane = iota((EXTRA, width), 1)
    line = iota((EXTRA, width), 0)
    tail = jnp.where(line == 0, token[...] - row * row_tokens, 0)
    for k in range(nblk):
        shift = starts[k] - QB * (me * nblk + k) + HALO
        tail = jnp.where((line == 1) & (lane == k), shift, tail)
    own[:rows] = feat[...]
    own[rows:] = tail.astype(F32).astype(BF16)


def pack_kernel(first, second, *outs):
    hid = second.shape[1]
    part = 3 * hid // 2
    for layer in range(BLOCKS):
        whole, upper, lower = outs[3 * layer : 3 * layer + 3]
        whole[:hid] = first[layer, 0]
        whole[hid : 2 * hid] = first[layer, 1]
        whole[2 * hid :] = second[layer]
        upper[...] = whole[:part]
        lower[...] = whole[part:]


def bias_kernel(pair_ref, weight, *outs):
    rows, cols, _ = pair_ref.shape
    _, heads, pad = outs[0].shape
    pad = pad - cols

    for q in range(rows):
        bias = dot_nt(weight[...], pair_ref[q])
        bias = jnp.concatenate([bias, jnp.zeros((bias.shape[0], pad), F32)], 1)
        for layer, out in enumerate(outs):
            out[q] = bias[layer * heads : (layer + 1) * heads]


def prepare(sources, targets, sems):
    return [
        pltpu.make_async_copy(source, target, sems.at[i])
        for i, (source, target) in enumerate(zip(sources, targets))
    ]


def query_kernel(
    layer, xn_ref, act_ref, w_in, query, w_key, w_val, gate, w_query, w_gate, sems
):
    fetches = prepare(
        [w_in.at[layer, k] for k in range(4)], [w_query, w_key, w_val, w_gate], sems
    )
    for k in (0, 3, 1, 2):
        fetches[k].start()
    fetches[0].wait()
    query[...] = dot(xn_ref[...], w_query[...]).astype(BF16)
    fetches[3].wait()
    gate[...] = jax.nn.sigmoid(dot(normed(act_ref[...]).astype(BF16), w_gate[...]))
    fetches[1].wait()
    fetches[2].wait()


def attention_kernel(mask_ref, query, here_ref, came_ref, low, high, w_key, w_val, out_ref):
    rows, width = query.shape
    cols = here_ref.shape[0]
    heads = low.shape[1]
    hsize = width // heads
    span = low.shape[2]
    row, col, _ = device()
    mine = col * cols // rows == row
    key_xn = jnp.where(mine, here_ref[...].astype(F32), came_ref[...].astype(F32))
    key_xn = jnp.concatenate([key_xn, jnp.zeros((span - cols, width), F32)], 0).astype(BF16)
    keys = dot(key_xn, w_key[...]).astype(BF16)
    vals = dot(key_xn, w_val[...]).astype(BF16)
    tokens = mask_ref.shape[0]
    count = jnp.int32(0)
    for bit in range(tokens.bit_length() - 1, -1, -1):
        longer = count + (1 << bit)
        inside = longer <= tokens
        last = mask_ref[jnp.where(inside, longer - 1, 0)]
        count = jnp.where(inside & (last == 1), longer, count)
    valid = iota((1, span), 1) + col * cols < count
    valid = valid & (iota((1, span), 1) < cols)
    group = heads // 2
    part = group * hsize
    lane = iota((1, part), 1) // hsize
    spot = iota((1, span), 1)
    levels = jnp.zeros((rows, span), F32)
    for g in range(2):
        wide = slice(g * part, (g + 1) * part)
        kg, vg = keys[:, wide], vals[:, wide]
        picks = [(lane == h).astype(BF16) for h in range(group)]
        stacked = jnp.concatenate([kg * p for p in picks], 0)
        scores = dot_nt(query[:, wide], stacked) * (1.0 / math.sqrt(hsize))
        probs = []
        for h in range(group):
            head = g * group + h
            bias = jnp.concatenate([low[:, head, :], high[:, head, :]], 0)
            score = scores[:, h * span : (h + 1) * span] + bias
            score = jnp.where(valid, score, -1000000000.0)
            top = jnp.max(score, -1, keepdims=True)
            expd = jnp.exp(score - top)
            total = jnp.sum(expd, -1, keepdims=True)
            probs.append((expd / total).astype(BF16))
            levels = jnp.where(spot % heads == head, top + jnp.log(total), levels)
        stacked = jnp.concatenate([vg * p for p in picks], 0)
        out_ref[:, wide] = dot(jnp.concatenate(probs, 1), stacked).astype(BF16)
    high = levels.astype(BF16).astype(F32)
    rest = levels - high
    middle = rest.astype(BF16).astype(F32)
    low = rest - middle
    packed = jnp.where(spot < heads, high, jnp.where(spot < 2 * heads, middle, low))
    out_ref[:, width:] = jnp.where(spot < 3 * heads, packed, 0.0).astype(BF16)


def mix_kernel(layer, heads, message, act_ref, gate, w_out, act_out, w_mix, sems):
    (copy,) = prepare([w_out.at[layer]], [w_mix], sems)
    copy.start()
    width = act_ref.shape[1]
    hsize = width // heads
    parts = [message[j, :, width:].astype(F32) for j in range(message.shape[0])]
    span = parts[0].shape[1]
    levels = [
        p + pltpu.roll(p, span - heads, 1) + pltpu.roll(p, span - 2 * heads, 1) for p in parts
    ]
    top = functools.reduce(jnp.maximum, levels)
    weights = [jnp.exp(level - top) for level in levels]
    whole = functools.reduce(jnp.add, weights)
    lane = iota((1, span), 1)
    row = iota((span, width), 0)
    expand = (row % heads == iota((span, width), 1) // hsize) & (row < 2 * heads)
    expand = expand.astype(F32).astype(BF16)
    packed = []
    for weight in weights:
        weight = weight / whole
        high = weight.astype(BF16).astype(F32)
        both = jnp.where(lane < heads, high, pltpu.roll(weight - high, heads, 1))
        packed.append(jnp.where(lane < 2 * heads, both, 0.0))
    spread = dot(jnp.concatenate(packed, 0).astype(BF16), expand)
    own = act_ref.shape[0]
    attn = jnp.zeros(act_ref.shape, F32)
    for j in range(message.shape[0]):
        attn = attn + spread[j * own : (j + 1) * own] * message[j, :, :width].astype(F32)
    gated = (gate[...] * attn).astype(BF16)
    copy.wait()
    act_out[...] = act_ref[...] + dot(gated, w_mix[...])


def mix(layer, message, act, gate, w_out, heads):
    own, width = act.shape
    return call(
        functools.partial(mix_kernel, layer, heads),
        jax.ShapeDtypeStruct((own, width), F32),
        message,
        act,
        gate,
        far=(w_out,),
        scratch=[pltpu.VMEM((width, width), BF16), pltpu.SemaphoreType.DMA((1,))],
        grant=48,
        flops=4 * own * width * width,
        moved=4 * width * width,
    )


def transition_kernel(groups, pieces, act_ref, *refs):
    others, refs = refs[: groups - 1], refs[groups - 1 :]
    sources = []
    for number in pieces:
        sources.append(refs[:number])
        refs = refs[number:]
    base, send, w_first, w_second, sems = refs
    count, hid = w_second.shape[:2]
    plan = []
    for wanted, target in (((0, 2 * hid), w_first), ((2 * hid, 3 * hid), w_second)):
        for j, source in enumerate(sources):
            begin = 0
            for ref in source:
                end = begin + ref.shape[0]
                low, high = max(begin, wanted[0]), min(end, wanted[1])
                if low < high:
                    near = target.at[j, pl.ds(low - wanted[0], high - low)]
                    plan.append((target is w_first, j, ref.at[pl.ds(low - begin, high - low)], near))
                begin = end
    fetches = prepare([item[2] for item in plan], [item[3] for item in plan], sems)
    for copy in fetches:
        copy.start()

    def arrived(first, j):
        for item, copy in zip(plan, fetches):
            if item[:2] == (first, j):
                copy.wait()

    group = device()[1] // 4
    came = [ref[...] for ref in (act_ref, *others)]
    ordered = []
    for place in range(groups):
        rows = came[0]
        for d in range(1, groups):
            rows = jnp.where((group - place + groups) % groups == d, came[d], rows)
        ordered.append(rows)
    act = jnp.concatenate(ordered, 0)
    rows = normed(act).astype(BF16)
    total = jnp.zeros(act.shape, F32)
    hidden = []
    for j in range(count):
        arrived(True, j)
        both = dot_nt(rows, w_first[j])
        left, right = both[:, :hid], both[:, hid:]
        hidden.append((left * jax.nn.sigmoid(left) * right).astype(BF16))
    for j in range(count):
        arrived(False, j)
        total = total + dot(hidden[j], w_second[j])
    base[...] = act + total
    send[...] = total.astype(BF16)


def transition(act, others, weights):
    own, width = act.shape
    blocks = len(weights)
    hid = sum(part.shape[0] for part in weights[0]) // 3
    parts = [part for source in weights for part in source]
    return call(
        functools.partial(transition_kernel, len(others) + 1, [len(source) for source in weights]),
        [jax.ShapeDtypeStruct(((len(others) + 1) * own, width), kind) for kind in (F32, BF16)],
        act,
        *others,
        far=parts,
        scratch=[
            pltpu.VMEM((blocks, 2 * hid, width), BF16),
            pltpu.VMEM((blocks, hid, width), BF16),
            pltpu.SemaphoreType.DMA((2 * len(parts),)),
        ],
        grant=48,
        flops=12 * own * hid * width * blocks,
        moved=6 * hid * width * blocks,
    )


def close_kernel(project, act_ref, *refs):
    *refs, act_out, out = refs
    if project:
        *refs, tok_atom = refs
    act = act_ref[...]
    for ref in refs:
        act = act + ref[...].astype(F32)
    own = act_out.shape[0]
    mine = act[:own]
    for k in range(1, act.shape[0] // own):
        mine = jnp.where(device()[1] // 4 == k, act[k * own : (k + 1) * own], mine)
    act_out[...] = mine
    normal = normed(act).astype(BF16)
    if project:
        normal = dot(normal, tok_atom[...]).astype(BF16)
    out[...] = normal


def close(own, act, parts, tok_atom):
    rows, width = act.shape
    project = tok_atom is not None
    last = tok_atom.shape[1] if project else width
    return call(
        functools.partial(close_kernel, project),
        [jax.ShapeDtypeStruct((own, width), F32), jax.ShapeDtypeStruct((rows, last), BF16)],
        act,
        *parts,
        *([tok_atom] if project else []),
        flops=10**7,
        moved=10**6,
    )


def row_of(mine, own):
    nrow, ncol = lax.axis_size("row"), lax.axis_size("col")
    parts = [mine]
    for flip in range(1, 4):
        parts.append(
            lax.ppermute(mine, ("row", "col"), [(i, i ^ flip) for i in range(nrow * ncol)])
        )
    low = lax.axis_index("col") % 4
    ordered = []
    for place in range(4):
        rows = parts[place]
        for flip in range(1, 4):
            rows = jnp.where(low == flip, parts[place ^ flip], rows)
        ordered.append(rows.reshape(-1, 1, own, mine.shape[1]))
    return jnp.concatenate(ordered, 1).reshape(-1, mine.shape[1])


def key_source(rows, cols):
    nrow, ncol = lax.axis_size("row"), lax.axis_size("col")
    shares = rows // cols
    chips = ncol // shares
    pairs = []
    for owner in range(nrow):
        near = sorted(range(chips), key=lambda chip: bin((chip ^ owner) % chips).count("1"))
        others = sorted((r for r in range(nrow) if r != owner), key=lambda r: -abs(r - owner))
        for chip, r in zip(near, others):
            for share in range(shares):
                pairs.append((owner * ncol + chip * shares + share, r * ncol + owner * shares + share))
    return pairs


def body(
    atom_feat,
    atom_token,
    window_start,
    token_cond,
    token_mask,
    pair,
    enc_in,
    enc_out,
    pool_weight,
    tok_in,
    tok_out,
    pair_weight,
    trans_in,
    trans_out,
    tok_atom,
    dec_in,
    dec_out,
    pos_out,
):
    nrow, ncol = lax.axis_size("row"), lax.axis_size("col")
    everyone = ("row", "col")
    count = nrow * ncol
    me_col = lax.axis_index("col")
    rows, width = token_cond.shape
    cols = pair.shape[1]
    heads = pair_weight.shape[2]
    own = rows // ncol
    atoms, afeat = atom_feat.shape
    natom = atoms * count
    nblk = atoms // QB

    hid = trans_out.shape[1]
    feat = call(
        functools.partial(feat_kernel, rows),
        jax.ShapeDtypeStruct((atoms + EXTRA, afeat), BF16),
        atom_feat,
        atom_token[None],
        scalars=(window_start,),
        grant=48,
        moved=10**5,
    )
    up = [(i, i + 1) for i in range(count - 1)]
    prev = lax.ppermute(feat, everyone, up)
    after = lax.ppermute(feat, everyone, [(b, a) for a, b in up])
    _, first_part, second_part = lax.optimization_barrier(
        (feat, jnp.swapaxes(trans_in, 2, 3), trans_out)
    )
    matrix = jax.ShapeDtypeStruct((3 * hid, width), BF16)
    half = jax.ShapeDtypeStruct((3 * hid // 2, width), BF16)
    pieces = call(
        pack_kernel,
        [matrix, half, half] * BLOCKS,
        first_part,
        second_part,
        grant=60,
        moved=12 * trans_out.size,
    )
    packed, upper, lower = pieces[::3], pieces[1::3], pieces[2::3]
    prev, after, early = lax.optimization_barrier((prev, after, upper[0]))
    neighbour = [(i, i ^ 2) for i in range(count)]
    sibling = [(i, i ^ 1) for i in range(count)]
    across = [[lax.ppermute(early, everyone, neighbour)], []]

    ext, copies = call(
        functools.partial(encoder_kernel, natom),
        [
            jax.ShapeDtypeStruct((atoms + 2 * HALO, afeat), BF16),
            jax.ShapeDtypeStruct((ncol, atoms + EXTRA, afeat), BF16),
        ],
        feat,
        prev,
        after,
        enc_in,
        enc_out,
        flops=10**8,
        moved=10**6,
    )
    span = -(-cols // 128) * 128
    half = rows // 2
    step = 24

    def bias_of(part, weights):
        return pl.pallas_call(
            bias_kernel,
            grid=(half // step,),
            out_shape=[jax.ShapeDtypeStruct((half, heads, span), F32)] * BLOCKS,
            in_specs=[
                pl.BlockSpec(
                    (step, cols, pair.shape[2]), lambda i: (i + part * (half // step), 0, 0)
                ),
                pl.BlockSpec(weights.shape, lambda i: (0, 0)),
            ],
            out_specs=[pl.BlockSpec((step, heads, span), lambda i: (i, 0, 0))] * BLOCKS,
            compiler_params=pltpu.CompilerParams(vmem_limit_bytes=(52 if part else 60) * MIB),
            cost_estimate=pl.CostEstimate(
                flops=2 * 10**9, bytes_accessed=4 * 10**6, transcendentals=0
            ),
        )(pair, weights)

    weights = jnp.swapaxes(pair_weight, 1, 2).reshape(BLOCKS * heads, -1)
    copies, first_weights = lax.optimization_barrier((copies, weights))
    low = bias_of(0, first_weights)
    both = lax.all_to_all(copies, "col", 0, 0)
    both, low, across[0][0] = lax.optimization_barrier((both, low, across[0][0]))

    act, xn, send = call(
        pool_kernel,
        [
            jax.ShapeDtypeStruct((own, width), F32),
            jax.ShapeDtypeStruct((rows, width), BF16),
            jax.ShapeDtypeStruct((cols, width), BF16),
        ],
        both,
        pool_weight,
        token_cond,
        flops=10**9,
        moved=10**6,
    )

    pairs = key_source(rows, cols)
    share = me_col % (rows // cols)
    peers = ncol // 4
    shifts = [
        [(r * ncol + c, r * ncol + (c + 4 * d) % ncol) for r in range(nrow) for c in range(ncol)]
        for d in range(peers)
    ]
    xn, weights = lax.optimization_barrier((xn, weights))
    beside, beyond = [], [[], []]
    for layer in range(BLOCKS):
        last = layer == BLOCKS - 1
        if layer:
            send = lax.dynamic_slice_in_dim(xn, share * cols, cols, 0)
            send, xn = lax.optimization_barrier((send, xn))
        came = lax.ppermute(send, everyone, pairs)
        matrix = jax.ShapeDtypeStruct((width, width), BF16)
        query, w_key, w_val, gate = call(
            functools.partial(query_kernel, layer),
            [
                jax.ShapeDtypeStruct((rows, width), BF16),
                matrix,
                matrix,
                jax.ShapeDtypeStruct((own, width), F32),
            ],
            xn,
            act,
            far=(tok_in,),
            scratch=[pltpu.VMEM((width, width), BF16)] * 2 + [pltpu.SemaphoreType.DMA((4,))],
            grant=48,
            flops=2 * rows * width * width,
            moved=8 * width * width,
        )
        if not layer:
            high = list(bias_of(1, weights))
            high[0], late, *ready = lax.optimization_barrier(
                (high[0], lower[0], *packed)
            )
            across[0].append(lax.ppermute(late, everyone, neighbour))
            beside = [lax.ppermute(part, everyone, sibling) for part in ready]
        else:
            query, late = lax.optimization_barrier((query, lower[1]))
            across[1].append(lax.ppermute(late, everyone, neighbour))
        message = call(
            attention_kernel,
            jax.ShapeDtypeStruct((rows, width + span), BF16),
            query,
            send,
            came,
            low[layer],
            high[layer],
            w_key,
            w_val,
            scalars=(token_mask,),
            grant=16,
            flops=10**9,
            moved=8 * 10**6,
        )
        message = lax.all_to_all(message.reshape(ncol, own, -1), "col", 0, 0)
        if not layer:
            message, ready = lax.optimization_barrier((message, upper[1]))
            across[1].append(lax.ppermute(ready, everyone, neighbour))
        act = mix(layer, message, act, gate, tok_out, heads)
        came_rows = [lax.ppermute(act, everyone, shifts[d]) for d in range(1, peers)]
        act, *ready = lax.optimization_barrier((act, *across[layer]))
        beyond[layer] = [lax.ppermute(part, everyone, sibling) for part in ready]
        act, part = transition(
            act, came_rows, ([packed[layer]], [beside[layer]], across[layer], beyond[layer])
        )
        parts = [lax.ppermute(part, everyone, shifts[d]) for d in range(1, peers)]
        act, mine = close(own, act, parts, tok_atom if last else None)
        if not last:
            mine, across[1][0] = lax.optimization_barrier((mine, across[1][0]))
        gathered = row_of(mine, own)
        if not last:
            xn = gathered

    bounds = [(r * ncol, (r + 1) * ncol) for r in range(nrow - 1)]
    bounds += [((r + 2) * ncol - 1, (r + 1) * ncol - 1) for r in range(nrow - 1)]
    edge = jnp.where(me_col == 0, gathered[rows - HALO :], gathered[:HALO])
    edge = lax.ppermute(edge, everyone, bounds)

    return call(
        functools.partial(decoder_kernel, natom),
        jax.ShapeDtypeStruct((pos_out.shape[0], atoms), F32),
        ext,
        feat,
        prev,
        after,
        gathered,
        edge,
        dec_in,
        dec_out,
        pos_out,
        flops=10**8,
        moved=10**6,
    )


def solution(mesh):
    in_specs = (
        P(("row", "col"), None),
        P(("row", "col")),
        P(("row", "col")),
        P("row", None),
        P(),
        P("row", "col", None),
        P(),
        P(),
        P(),
        P(),
        P(),
        P(),
        P(None, None, None, "col"),
        P(None, "col", None),
        P(),
        P(),
        P(),
        P(),
    )
    out_specs = P(None, ("row", "col"))
    return jax.shard_map(body, mesh=mesh, in_specs=in_specs, out_specs=out_specs, check_vma=False)
```

```python
import functools
import math

import jax
import jax.numpy as jnp
from jax import lax
from jax.experimental import pallas as pl
from jax.experimental.pallas import tpu as pltpu
from jax.sharding import PartitionSpec as P

HA = 4
QB = 32
KW = 128
HALO = 64
BLOCKS = 2
EXTRA = 16
MIB = 1 << 20
F32 = jnp.float32
BF16 = jnp.bfloat16


def call(kernel, outs, *args, scalars=(), far=(), scratch=(), grant=8, flops=0, moved=0):
    smem = pl.BlockSpec(memory_space=pltpu.SMEM)
    vmem = pl.BlockSpec(memory_space=pltpu.VMEM)
    hbm = pl.BlockSpec(memory_space=pltpu.HBM)
    return pl.pallas_call(
        kernel,
        out_shape=outs,
        in_specs=[smem] * len(scalars) + [vmem] * len(args) + [hbm] * len(far),
        out_specs=jax.tree.map(lambda _: vmem, outs),
        scratch_shapes=list(scratch),
        compiler_params=pltpu.CompilerParams(vmem_limit_bytes=grant * MIB),
        cost_estimate=pl.CostEstimate(flops=flops, bytes_accessed=moved, transcendentals=0),
    )(*scalars, *args, *far)


def dot(a, b):
    return jnp.dot(a, b, preferred_element_type=F32)


def dot_nt(a, b):
    return lax.dot_general(a, b, (((1,), (1,)), ((), ())), preferred_element_type=F32)


def dot_tn(a, b):
    return lax.dot_general(a, b, (((0,), (0,)), ((), ())), preferred_element_type=F32)


def normed(x):
    x = x.astype(F32)
    cent = x - jnp.mean(x, -1, keepdims=True)
    var = jnp.mean(cent * cent, -1, keepdims=True)
    return cent * lax.rsqrt(var + 1e-05)


def iota(shape, dim):
    return lax.broadcasted_iota(jnp.int32, shape, dim)


def device():
    row, col = lax.axis_index("row"), lax.axis_index("col")
    return row, col, row * lax.axis_size("col") + col


def window_mask(shifts, first, natom, nkeys):
    shape = (len(shifts) * QB, nkeys)
    block = iota(shape, 0) // QB
    low = jnp.zeros(shape, jnp.int32)
    for i, shift in enumerate(shifts):
        low = jnp.where(block == i, shift + QB * i, low)
    key = iota(shape, 1)
    atom = key + first
    return (key >= low) & (key < low + KW) & (atom >= 0) & (atom < natom)


def attend(x, xn, gate, query, keys, vals, mask, w_out):
    width = x.shape[1]
    hsize = width // HA
    lane = iota((1, width), 1) // hsize
    outs = jnp.zeros(x.shape, F32)
    for h in range(HA):
        pick = (lane == h).astype(BF16)
        scores = dot_nt(query, keys * pick) * (1.0 / math.sqrt(hsize))
        scores = jnp.where(mask, scores, -1000000000.0)
        top = jnp.max(scores, -1, keepdims=True)
        expd = jnp.exp(scores - top)
        total = jnp.sum(expd, -1, keepdims=True)
        outs = outs + dot(expd.astype(BF16), vals * pick) / total
    gated = (jax.nn.sigmoid(gate) * outs).astype(BF16)
    return (x.astype(F32) + dot(gated, w_out)).astype(BF16)


def shifts_of(tail_ref, lanes):
    tail = tail_ref[tail_ref.shape[0] - EXTRA :, :].astype(F32)
    return [tail[1:2, k : k + 1].astype(jnp.int32) for k in lanes]


def encoder_kernel(natom, own_ref, prev_ref, next_ref, w_in, w_out, ext_ref, all_ref):
    rows = own_ref.shape[0] - EXTRA
    nblk = rows // QB
    half = HALO // QB
    x = jnp.concatenate([prev_ref[:rows], own_ref[:rows], next_ref[:rows]], 0)
    xn = normed(x).astype(BF16)
    keys = dot(xn, w_in[1]).astype(BF16)
    vals = dot(xn, w_in[2]).astype(BF16)
    qx, qn = x[HALO : 3 * rows - HALO], xn[HALO : 3 * rows - HALO]
    query = dot(qn, w_in[0]).astype(BF16)
    gate = dot(qn, w_in[3])
    shifts = (
        shifts_of(prev_ref, range(nblk - half, nblk))
        + shifts_of(own_ref, range(nblk))
        + shifts_of(next_ref, range(half))
    )
    first = device()[2] * rows - rows
    for part in range(2):
        mine = slice(part * rows, (part + 1) * rows)
        seen = slice(part * rows, (part + 2) * rows)
        mask = window_mask(
            shifts[part * nblk : (part + 1) * nblk], first + part * rows, natom, 2 * rows
        )
        ext_ref[mine] = attend(
            qx[mine], qn[mine], gate[mine], query[mine], keys[seen], vals[seen], mask, w_out[...]
        )
    new = ext_ref[HALO : HALO + rows]
    tail = own_ref[rows:]
    for j in range(all_ref.shape[0]):
        all_ref[j, :rows] = new
        all_ref[j, rows:] = tail


def pool_kernel(both_ref, weight, cond, act_ref, xn_ref, send_ref):
    count, rows = both_ref.shape[0], both_ref.shape[1] - EXTRA
    tokens = cond.shape[0]
    sums = jnp.zeros(cond.shape, F32)
    counts = jnp.zeros((tokens, 1), F32)
    step = 4 if count % 4 == 0 else 1
    for j in range(0, count, step):
        atoms = jnp.concatenate([both_ref[j + k, :rows] for k in range(step)], 0)
        feats = jnp.maximum(dot(atoms, weight[...]), 0.0).astype(BF16)
        spot = jnp.concatenate(
            [both_ref[j + k, rows:].astype(F32)[0:1] for k in range(step)], 1
        ).astype(jnp.int32)
        onehot = (iota((tokens, step * rows), 0) == spot).astype(F32)
        sums = sums + dot(onehot.astype(BF16), feats)
        counts = counts + jnp.sum(onehot, -1, keepdims=True)
    act = sums / counts + cond[...].astype(F32)
    xn = normed(act)
    xn_ref[...] = xn.astype(BF16)
    cols = send_ref.shape[0]
    part = xn[:cols]
    for k in range(1, tokens // cols):
        part = jnp.where(device()[1] % (tokens // cols) == k, xn[k * cols : (k + 1) * cols], part)
    send_ref[...] = part.astype(BF16)
    own = act_ref.shape[0]
    col = device()[1]
    mine = act[:own]
    for c in range(1, tokens // own):
        mine = jnp.where(col == c, act[c * own : (c + 1) * own], mine)
    act_ref[...] = mine


def decoder_kernel(
    natom, x1_ref, own_ref, prev_ref, next_ref, proj_ref, edge_ref, w_in, w_out, pos, out
):
    rows = own_ref.shape[0] - EXTRA
    proj = proj_ref[...].astype(F32)
    edge = edge_ref[...].astype(F32)
    tokens = proj.shape[0]
    _, col, me = device()
    rest = tokens - HALO
    below = jnp.where(col == 0, edge, proj[rest:])
    above = jnp.where(col == lax.axis_size("col") - 1, edge, proj[:HALO])
    tables = (
        jnp.concatenate([proj[:rest], below], 0),
        proj,
        jnp.concatenate([above, proj[HALO:]], 0),
    )
    spread = []
    for table, ref in zip(tables, (prev_ref, own_ref, next_ref)):
        spot = ref[rows:].astype(F32)[0:1].astype(jnp.int32)
        onehot = (iota((tokens, rows), 0) == spot).astype(F32).astype(BF16)
        spread.append(dot_tn(onehot, table.astype(BF16)))
    spread = jnp.concatenate([spread[0][rows - HALO :], spread[1], spread[2][:HALO]], 0)
    x = (x1_ref[...].astype(F32) + spread).astype(BF16)
    xn = normed(x).astype(BF16)
    keys = dot(xn, w_in[1]).astype(BF16)
    vals = dot(xn, w_in[2]).astype(BF16)
    qx, qn = x[HALO : HALO + rows], xn[HALO : HALO + rows]
    query = dot(qn, w_in[0]).astype(BF16)
    gate = dot(qn, w_in[3])
    shifts = shifts_of(own_ref, range(rows // QB))
    mask = window_mask(shifts, me * rows - HALO, natom, 2 * rows)
    third = attend(qx, qn, gate, query, keys, vals, mask, w_out[...])
    out[...] = dot_nt(pos[...], normed(third).astype(BF16))


def feat_kernel(row_tokens, starts, feat, token, own):
    rows, width = feat.shape
    row, _, me = device()
    nblk = starts.shape[0]
    lane = iota((EXTRA, width), 1)
    line = iota((EXTRA, width), 0)
    tail = jnp.where(line == 0, token[...] - row * row_tokens, 0)
    for k in range(nblk):
        shift = starts[k] - QB * (me * nblk + k) + HALO
        tail = jnp.where((line == 1) & (lane == k), shift, tail)
    own[:rows] = feat[...]
    own[rows:] = tail.astype(F32).astype(BF16)


def pack_kernel(cuts, first, second, *outs):
    hid = second.shape[1]
    outs = list(outs)
    for layer, cut in enumerate(cuts):
        whole = outs.pop(0)
        whole[:hid] = first[layer, 0]
        whole[hid : 2 * hid] = first[layer, 1]
        whole[2 * hid :] = second[layer]
        size = 3 * hid // cut
        for k in range(cut):
            outs.pop(0)[...] = whole[k * size : (k + 1) * size]


def bias_kernel(pair_ref, weight, *outs):
    rows, cols, _ = pair_ref.shape
    _, heads, pad = outs[0].shape
    pad = pad - cols

    for q in range(rows):
        bias = dot_nt(weight[...], pair_ref[q])
        bias = jnp.concatenate([bias, jnp.zeros((bias.shape[0], pad), F32)], 1)
        for layer, out in enumerate(outs):
            out[q] = bias[layer * heads : (layer + 1) * heads]


def prepare(sources, targets, sems):
    return [
        pltpu.make_async_copy(source, target, sems.at[i])
        for i, (source, target) in enumerate(zip(sources, targets))
    ]


def query_kernel(
    layer, xn_ref, act_ref, w_in, query, w_key, w_val, gate, w_query, w_gate, sems
):
    fetches = prepare(
        [w_in.at[layer, k] for k in range(4)], [w_query, w_key, w_val, w_gate], sems
    )
    for k in (0, 3, 1, 2):
        fetches[k].start()
    fetches[0].wait()
    query[...] = dot(xn_ref[...], w_query[...]).astype(BF16)
    fetches[3].wait()
    gate[...] = jax.nn.sigmoid(dot(normed(act_ref[...]).astype(BF16), w_gate[...]))
    fetches[1].wait()
    fetches[2].wait()


def attention_kernel(mask_ref, query, here_ref, came_ref, low, high, w_key, w_val, out_ref):
    rows, width = query.shape
    cols = here_ref.shape[0]
    heads = low.shape[1]
    hsize = width // heads
    span = low.shape[2]
    row, col, _ = device()
    mine = col * cols // rows == row
    key_xn = jnp.where(mine, here_ref[...].astype(F32), came_ref[...].astype(F32))
    key_xn = jnp.concatenate([key_xn, jnp.zeros((span - cols, width), F32)], 0).astype(BF16)
    keys = dot(key_xn, w_key[...]).astype(BF16)
    vals = dot(key_xn, w_val[...]).astype(BF16)
    tokens = mask_ref.shape[0]
    count = jnp.int32(0)
    for bit in range(tokens.bit_length() - 1, -1, -1):
        longer = count + (1 << bit)
        inside = longer <= tokens
        last = mask_ref[jnp.where(inside, longer - 1, 0)]
        count = jnp.where(inside & (last == 1), longer, count)
    valid = iota((1, span), 1) + col * cols < count
    valid = valid & (iota((1, span), 1) < cols)
    group = heads // 2
    part = group * hsize
    lane = iota((1, part), 1) // hsize
    spot = iota((1, span), 1)
    levels = jnp.zeros((rows, span), F32)
    for g in range(2):
        wide = slice(g * part, (g + 1) * part)
        kg, vg = keys[:, wide], vals[:, wide]
        picks = [(lane == h).astype(BF16) for h in range(group)]
        stacked = jnp.concatenate([kg * p for p in picks], 0)
        scores = dot_nt(query[:, wide], stacked) * (1.0 / math.sqrt(hsize))
        probs = []
        for h in range(group):
            head = g * group + h
            bias = jnp.concatenate([low[:, head, :], high[:, head, :]], 0)
            score = scores[:, h * span : (h + 1) * span] + bias
            score = jnp.where(valid, score, -1000000000.0)
            top = jnp.max(score, -1, keepdims=True)
            expd = jnp.exp(score - top)
            total = jnp.sum(expd, -1, keepdims=True)
            probs.append((expd / total).astype(BF16))
            levels = jnp.where(spot % heads == head, top + jnp.log(total), levels)
        stacked = jnp.concatenate([vg * p for p in picks], 0)
        out_ref[:, wide] = dot(jnp.concatenate(probs, 1), stacked).astype(BF16)
    high = levels.astype(BF16).astype(F32)
    rest = levels - high
    middle = rest.astype(BF16).astype(F32)
    low = rest - middle
    packed = jnp.where(spot < heads, high, jnp.where(spot < 2 * heads, middle, low))
    out_ref[:, width:] = jnp.where(spot < 3 * heads, packed, 0.0).astype(BF16)


def mix_kernel(layer, heads, message, act_ref, gate, w_out, act_out, w_mix, sems):
    (copy,) = prepare([w_out.at[layer]], [w_mix], sems)
    copy.start()
    width = act_ref.shape[1]
    hsize = width // heads
    parts = [message[j, :, width:].astype(F32) for j in range(message.shape[0])]
    span = parts[0].shape[1]
    levels = [
        p + pltpu.roll(p, span - heads, 1) + pltpu.roll(p, span - 2 * heads, 1) for p in parts
    ]
    top = functools.reduce(jnp.maximum, levels)
    weights = [jnp.exp(level - top) for level in levels]
    whole = functools.reduce(jnp.add, weights)
    lane = iota((1, span), 1)
    row = iota((span, width), 0)
    expand = (row % heads == iota((span, width), 1) // hsize) & (row < 2 * heads)
    expand = expand.astype(F32).astype(BF16)
    packed = []
    for weight in weights:
        weight = weight / whole
        high = weight.astype(BF16).astype(F32)
        both = jnp.where(lane < heads, high, pltpu.roll(weight - high, heads, 1))
        packed.append(jnp.where(lane < 2 * heads, both, 0.0))
    spread = dot(jnp.concatenate(packed, 0).astype(BF16), expand)
    own = act_ref.shape[0]
    attn = jnp.zeros(act_ref.shape, F32)
    for j in range(message.shape[0]):
        attn = attn + spread[j * own : (j + 1) * own] * message[j, :, :width].astype(F32)
    gated = (gate[...] * attn).astype(BF16)
    copy.wait()
    act_out[...] = act_ref[...] + dot(gated, w_mix[...])


def mix(layer, message, act, gate, w_out, heads):
    own, width = act.shape
    return call(
        functools.partial(mix_kernel, layer, heads),
        jax.ShapeDtypeStruct((own, width), F32),
        message,
        act,
        gate,
        far=(w_out,),
        scratch=[pltpu.VMEM((width, width), BF16), pltpu.SemaphoreType.DMA((1,))],
        grant=48,
        flops=4 * own * width * width,
        moved=4 * width * width,
    )


def transition_kernel(groups, pieces, act_ref, *refs):
    others, refs = refs[: groups - 1], refs[groups - 1 :]
    sources = []
    for number in pieces:
        sources.append(refs[:number])
        refs = refs[number:]
    base, send, w_first, w_second, sems = refs
    count, hid = w_second.shape[:2]
    plan = []
    for wanted, target in (((0, 2 * hid), w_first), ((2 * hid, 3 * hid), w_second)):
        for j, source in enumerate(sources):
            begin = 0
            for ref in source:
                end = begin + ref.shape[0]
                low, high = max(begin, wanted[0]), min(end, wanted[1])
                if low < high:
                    near = target.at[j, pl.ds(low - wanted[0], high - low)]
                    plan.append((target is w_first, j, ref.at[pl.ds(low - begin, high - low)], near))
                begin = end
    fetches = prepare([item[2] for item in plan], [item[3] for item in plan], sems)
    for copy in fetches:
        copy.start()

    def arrived(first, j):
        for item, copy in zip(plan, fetches):
            if item[:2] == (first, j):
                copy.wait()

    group = device()[1] // 4
    came = [ref[...] for ref in (act_ref, *others)]
    ordered = []
    for place in range(groups):
        rows = came[0]
        for d in range(1, groups):
            rows = jnp.where((group - place + groups) % groups == d, came[d], rows)
        ordered.append(rows)
    act = jnp.concatenate(ordered, 0)
    rows = normed(act).astype(BF16)
    total = jnp.zeros(act.shape, F32)
    hidden = []
    for j in range(count):
        arrived(True, j)
        both = dot_nt(rows, w_first[j])
        left, right = both[:, :hid], both[:, hid:]
        hidden.append((left * jax.nn.sigmoid(left) * right).astype(BF16))
    for j in range(count):
        arrived(False, j)
        total = total + dot(hidden[j], w_second[j])
    base[...] = act + total
    send[...] = total.astype(BF16)


def transition(act, others, weights):
    own, width = act.shape
    blocks = len(weights)
    hid = sum(part.shape[0] for part in weights[0]) // 3
    parts = [part for source in weights for part in source]
    return call(
        functools.partial(transition_kernel, len(others) + 1, [len(source) for source in weights]),
        [jax.ShapeDtypeStruct(((len(others) + 1) * own, width), kind) for kind in (F32, BF16)],
        act,
        *others,
        far=parts,
        scratch=[
            pltpu.VMEM((blocks, 2 * hid, width), BF16),
            pltpu.VMEM((blocks, hid, width), BF16),
            pltpu.SemaphoreType.DMA((2 * len(parts),)),
        ],
        grant=48,
        flops=12 * own * hid * width * blocks,
        moved=6 * hid * width * blocks,
    )


def close_kernel(project, act_ref, *refs):
    *refs, act_out, out = refs
    if project:
        *refs, tok_atom = refs
    act = act_ref[...]
    for ref in refs:
        act = act + ref[...].astype(F32)
    own = act_out.shape[0]
    mine = act[:own]
    for k in range(1, act.shape[0] // own):
        mine = jnp.where(device()[1] // 4 == k, act[k * own : (k + 1) * own], mine)
    act_out[...] = mine
    normal = normed(act).astype(BF16)
    if project:
        normal = dot(normal, tok_atom[...]).astype(BF16)
    out[...] = normal


def close(own, act, parts, tok_atom):
    rows, width = act.shape
    project = tok_atom is not None
    last = tok_atom.shape[1] if project else width
    return call(
        functools.partial(close_kernel, project),
        [jax.ShapeDtypeStruct((own, width), F32), jax.ShapeDtypeStruct((rows, last), BF16)],
        act,
        *parts,
        *([tok_atom] if project else []),
        flops=10**7,
        moved=10**6,
    )


def row_of(mine, own):
    nrow, ncol = lax.axis_size("row"), lax.axis_size("col")
    parts = [mine]
    for flip in range(1, 4):
        parts.append(
            lax.ppermute(mine, ("row", "col"), [(i, i ^ flip) for i in range(nrow * ncol)])
        )
    low = lax.axis_index("col") % 4
    ordered = []
    for place in range(4):
        rows = parts[place]
        for flip in range(1, 4):
            rows = jnp.where(low == flip, parts[place ^ flip], rows)
        ordered.append(rows.reshape(-1, 1, own, mine.shape[1]))
    return jnp.concatenate(ordered, 1).reshape(-1, mine.shape[1])


def key_source(rows, cols):
    nrow, ncol = lax.axis_size("row"), lax.axis_size("col")
    shares = rows // cols
    chips = ncol // shares
    pairs = []
    for owner in range(nrow):
        near = sorted(range(chips), key=lambda chip: bin((chip ^ owner) % chips).count("1"))
        others = sorted((r for r in range(nrow) if r != owner), key=lambda r: -abs(r - owner))
        for chip, r in zip(near, others):
            for share in range(shares):
                pairs.append((owner * ncol + chip * shares + share, r * ncol + owner * shares + share))
    return pairs


def body(
    atom_feat,
    atom_token,
    window_start,
    token_cond,
    token_mask,
    pair,
    enc_in,
    enc_out,
    pool_weight,
    tok_in,
    tok_out,
    pair_weight,
    trans_in,
    trans_out,
    tok_atom,
    dec_in,
    dec_out,
    pos_out,
):
    nrow, ncol = lax.axis_size("row"), lax.axis_size("col")
    everyone = ("row", "col")
    count = nrow * ncol
    me_col = lax.axis_index("col")
    rows, width = token_cond.shape
    cols = pair.shape[1]
    heads = pair_weight.shape[2]
    own = rows // ncol
    atoms, afeat = atom_feat.shape
    natom = atoms * count
    nblk = atoms // QB

    hid = trans_out.shape[1]
    feat = call(
        functools.partial(feat_kernel, rows),
        jax.ShapeDtypeStruct((atoms + EXTRA, afeat), BF16),
        atom_feat,
        atom_token[None],
        scalars=(window_start,),
        grant=48,
        moved=10**5,
    )
    up = [(i, i + 1) for i in range(count - 1)]
    prev = lax.ppermute(feat, everyone, up)
    after = lax.ppermute(feat, everyone, [(b, a) for a, b in up])
    _, first_part, second_part = lax.optimization_barrier(
        (feat, jnp.swapaxes(trans_in, 2, 3), trans_out)
    )
    matrix = jax.ShapeDtypeStruct((3 * hid, width), BF16)
    cuts = (3, 2)
    pieces = call(
        functools.partial(pack_kernel, cuts),
        [
            jax.ShapeDtypeStruct((3 * hid // parts, width), BF16)
            for cut in cuts
            for parts in [1] + [cut] * cut
        ],
        first_part,
        second_part,
        grant=60,
        moved=12 * trans_out.size,
    )
    packed, cut_up = [], []
    for cut in cuts:
        packed.append(pieces[0])
        cut_up.append(pieces[1 : 1 + cut])
        pieces = pieces[1 + cut :]
    prev, after, early = lax.optimization_barrier((prev, after, cut_up[0][0]))
    neighbour = [(i, i ^ 2) for i in range(count)]
    sibling = [(i, i ^ 1) for i in range(count)]
    across = [[lax.ppermute(early, everyone, neighbour)], []]

    ext, copies = call(
        functools.partial(encoder_kernel, natom),
        [
            jax.ShapeDtypeStruct((atoms + 2 * HALO, afeat), BF16),
            jax.ShapeDtypeStruct((ncol, atoms + EXTRA, afeat), BF16),
        ],
        feat,
        prev,
        after,
        enc_in,
        enc_out,
        flops=10**8,
        moved=10**6,
    )
    span = -(-cols // 128) * 128
    step = 24
    early_steps = rows // step * 5 // 8

    def bias_of(part, weights):
        begin, end = ((0, early_steps), (early_steps, rows // step))[part]
        return pl.pallas_call(
            bias_kernel,
            grid=(end - begin,),
            out_shape=[jax.ShapeDtypeStruct(((end - begin) * step, heads, span), F32)] * BLOCKS,
            in_specs=[
                pl.BlockSpec((step, cols, pair.shape[2]), lambda i: (i + begin, 0, 0)),
                pl.BlockSpec(weights.shape, lambda i: (0, 0)),
            ],
            out_specs=[pl.BlockSpec((step, heads, span), lambda i: (i, 0, 0))] * BLOCKS,
            compiler_params=pltpu.CompilerParams(vmem_limit_bytes=(52 if part else 60) * MIB),
            cost_estimate=pl.CostEstimate(
                flops=2 * 10**9, bytes_accessed=4 * 10**6, transcendentals=0
            ),
        )(pair, weights)

    weights = jnp.swapaxes(pair_weight, 1, 2).reshape(BLOCKS * heads, -1)
    copies, first_weights = lax.optimization_barrier((copies, weights))
    low = bias_of(0, first_weights)
    both = lax.all_to_all(copies, "col", 0, 0)
    both, low, across[0][0] = lax.optimization_barrier((both, low, across[0][0]))

    act, xn, send = call(
        pool_kernel,
        [
            jax.ShapeDtypeStruct((own, width), F32),
            jax.ShapeDtypeStruct((rows, width), BF16),
            jax.ShapeDtypeStruct((cols, width), BF16),
        ],
        both,
        pool_weight,
        token_cond,
        flops=10**9,
        moved=10**6,
    )

    pairs = key_source(rows, cols)
    share = me_col % (rows // cols)
    peers = ncol // 4
    shifts = [
        [(r * ncol + c, r * ncol + (c + 4 * d) % ncol) for r in range(nrow) for c in range(ncol)]
        for d in range(peers)
    ]
    xn, weights = lax.optimization_barrier((xn, weights))
    beside, beyond = [], [[], []]
    for layer in range(BLOCKS):
        last = layer == BLOCKS - 1
        if layer:
            send = lax.dynamic_slice_in_dim(xn, share * cols, cols, 0)
            send, xn = lax.optimization_barrier((send, xn))
        came = lax.ppermute(send, everyone, pairs)
        matrix = jax.ShapeDtypeStruct((width, width), BF16)
        query, w_key, w_val, gate = call(
            functools.partial(query_kernel, layer),
            [
                jax.ShapeDtypeStruct((rows, width), BF16),
                matrix,
                matrix,
                jax.ShapeDtypeStruct((own, width), F32),
            ],
            xn,
            act,
            far=(tok_in,),
            scratch=[pltpu.VMEM((width, width), BF16)] * 2 + [pltpu.SemaphoreType.DMA((4,))],
            grant=48,
            flops=2 * rows * width * width,
            moved=8 * width * width,
        )
        if not layer:
            high = list(bias_of(1, weights))
            high[0], *late = lax.optimization_barrier((high[0], *cut_up[0][1:]))
            across[0] += [lax.ppermute(part, everyone, neighbour) for part in late]
            high[0], *ready = lax.optimization_barrier((high[0], *packed))
            beside = [lax.ppermute(part, everyone, sibling) for part in ready]
        else:
            query, late = lax.optimization_barrier((query, cut_up[1][1]))
            across[1].append(lax.ppermute(late, everyone, neighbour))
        message = call(
            attention_kernel,
            jax.ShapeDtypeStruct((rows, width + span), BF16),
            query,
            send,
            came,
            low[layer],
            high[layer],
            w_key,
            w_val,
            scalars=(token_mask,),
            grant=16,
            flops=10**9,
            moved=8 * 10**6,
        )
        message = lax.all_to_all(message.reshape(ncol, own, -1), "col", 0, 0)
        if not layer:
            message, ready = lax.optimization_barrier((message, cut_up[1][0]))
            across[1].append(lax.ppermute(ready, everyone, neighbour))
        act = mix(layer, message, act, gate, tok_out, heads)
        came_rows = [lax.ppermute(act, everyone, shifts[d]) for d in range(1, peers)]
        act, *ready = lax.optimization_barrier((act, *across[layer]))
        beyond[layer] = [lax.ppermute(part, everyone, sibling) for part in ready]
        act, part = transition(
            act, came_rows, ([packed[layer]], [beside[layer]], across[layer], beyond[layer])
        )
        parts = [lax.ppermute(part, everyone, shifts[d]) for d in range(1, peers)]
        act, mine = close(own, act, parts, tok_atom if last else None)
        if not last:
            mine, across[1][0] = lax.optimization_barrier((mine, across[1][0]))
        gathered = row_of(mine, own)
        if not last:
            xn = gathered

    bounds = [(r * ncol, (r + 1) * ncol) for r in range(nrow - 1)]
    bounds += [((r + 2) * ncol - 1, (r + 1) * ncol - 1) for r in range(nrow - 1)]
    edge = jnp.where(me_col == 0, gathered[rows - HALO :], gathered[:HALO])
    edge = lax.ppermute(edge, everyone, bounds)

    return call(
        functools.partial(decoder_kernel, natom),
        jax.ShapeDtypeStruct((pos_out.shape[0], atoms), F32),
        ext,
        feat,
        prev,
        after,
        gathered,
        edge,
        dec_in,
        dec_out,
        pos_out,
        flops=10**8,
        moved=10**6,
    )


def solution(mesh):
    in_specs = (
        P(("row", "col"), None),
        P(("row", "col")),
        P(("row", "col")),
        P("row", None),
        P(),
        P("row", "col", None),
        P(),
        P(),
        P(),
        P(),
        P(),
        P(),
        P(None, None, None, "col"),
        P(None, "col", None),
        P(),
        P(),
        P(),
        P(),
    )
    out_specs = P(None, ("row", "col"))
    return jax.shard_map(body, mesh=mesh, in_specs=in_specs, out_specs=out_specs, check_vma=False)
```

```python
import functools
import math

import jax
import jax.numpy as jnp
from jax import lax
from jax.experimental import pallas as pl
from jax.experimental.pallas import tpu as pltpu
from jax.sharding import PartitionSpec as P

HA = 4
QB = 32
KW = 128
HALO = 64
BLOCKS = 2
EXTRA = 16
MIB = 1 << 20
F32 = jnp.float32
BF16 = jnp.bfloat16


def call(kernel, outs, *args, scalars=(), far=(), scratch=(), grant=8, flops=0, moved=0):
    smem = pl.BlockSpec(memory_space=pltpu.SMEM)
    vmem = pl.BlockSpec(memory_space=pltpu.VMEM)
    hbm = pl.BlockSpec(memory_space=pltpu.HBM)
    return pl.pallas_call(
        kernel,
        out_shape=outs,
        in_specs=[smem] * len(scalars) + [vmem] * len(args) + [hbm] * len(far),
        out_specs=jax.tree.map(lambda _: vmem, outs),
        scratch_shapes=list(scratch),
        compiler_params=pltpu.CompilerParams(vmem_limit_bytes=grant * MIB),
        cost_estimate=pl.CostEstimate(flops=flops, bytes_accessed=moved, transcendentals=0),
    )(*scalars, *args, *far)


def dot(a, b):
    return jnp.dot(a, b, preferred_element_type=F32)


def dot_nt(a, b):
    return lax.dot_general(a, b, (((1,), (1,)), ((), ())), preferred_element_type=F32)


def dot_tn(a, b):
    return lax.dot_general(a, b, (((0,), (0,)), ((), ())), preferred_element_type=F32)


def normed(x):
    x = x.astype(F32)
    cent = x - jnp.mean(x, -1, keepdims=True)
    var = jnp.mean(cent * cent, -1, keepdims=True)
    return cent * lax.rsqrt(var + 1e-05)


def iota(shape, dim):
    return lax.broadcasted_iota(jnp.int32, shape, dim)


def device():
    row, col = lax.axis_index("row"), lax.axis_index("col")
    return row, col, row * lax.axis_size("col") + col


def window_mask(shifts, first, natom, nkeys):
    shape = (len(shifts) * QB, nkeys)
    block = iota(shape, 0) // QB
    low = jnp.zeros(shape, jnp.int32)
    for i, shift in enumerate(shifts):
        low = jnp.where(block == i, shift + QB * i, low)
    key = iota(shape, 1)
    atom = key + first
    return (key >= low) & (key < low + KW) & (atom >= 0) & (atom < natom)


def attend(x, xn, gate, query, keys, vals, mask, w_out):
    width = x.shape[1]
    hsize = width // HA
    lane = iota((1, width), 1) // hsize
    outs = jnp.zeros(x.shape, F32)
    for h in range(HA):
        pick = (lane == h).astype(BF16)
        scores = dot_nt(query, keys * pick) * (1.0 / math.sqrt(hsize))
        scores = jnp.where(mask, scores, -1000000000.0)
        top = jnp.max(scores, -1, keepdims=True)
        expd = jnp.exp(scores - top)
        total = jnp.sum(expd, -1, keepdims=True)
        outs = outs + dot(expd.astype(BF16), vals * pick) / total
    gated = (jax.nn.sigmoid(gate) * outs).astype(BF16)
    return (x.astype(F32) + dot(gated, w_out)).astype(BF16)


def shifts_of(tail_ref, lanes):
    tail = tail_ref[tail_ref.shape[0] - EXTRA :, :].astype(F32)
    return [tail[1:2, k : k + 1].astype(jnp.int32) for k in lanes]


def encoder_kernel(natom, own_ref, prev_ref, next_ref, w_in, w_out, ext_ref, all_ref):
    rows = own_ref.shape[0] - EXTRA
    nblk = rows // QB
    half = HALO // QB
    x = jnp.concatenate([prev_ref[:rows], own_ref[:rows], next_ref[:rows]], 0)
    xn = normed(x).astype(BF16)
    keys = dot(xn, w_in[1]).astype(BF16)
    vals = dot(xn, w_in[2]).astype(BF16)
    qx, qn = x[HALO : 3 * rows - HALO], xn[HALO : 3 * rows - HALO]
    query = dot(qn, w_in[0]).astype(BF16)
    gate = dot(qn, w_in[3])
    shifts = (
        shifts_of(prev_ref, range(nblk - half, nblk))
        + shifts_of(own_ref, range(nblk))
        + shifts_of(next_ref, range(half))
    )
    first = device()[2] * rows - rows
    for part in range(2):
        mine = slice(part * rows, (part + 1) * rows)
        seen = slice(part * rows, (part + 2) * rows)
        mask = window_mask(
            shifts[part * nblk : (part + 1) * nblk], first + part * rows, natom, 2 * rows
        )
        ext_ref[mine] = attend(
            qx[mine], qn[mine], gate[mine], query[mine], keys[seen], vals[seen], mask, w_out[...]
        )
    new = ext_ref[HALO : HALO + rows]
    tail = own_ref[rows:]
    for j in range(all_ref.shape[0]):
        all_ref[j, :rows] = new
        all_ref[j, rows:] = tail


def pool_kernel(both_ref, weight, cond, act_ref, xn_ref, send_ref):
    count, rows = both_ref.shape[0], both_ref.shape[1] - EXTRA
    tokens = cond.shape[0]
    sums = jnp.zeros(cond.shape, F32)
    counts = jnp.zeros((tokens, 1), F32)
    step = 4 if count % 4 == 0 else 1
    for j in range(0, count, step):
        atoms = jnp.concatenate([both_ref[j + k, :rows] for k in range(step)], 0)
        feats = jnp.maximum(dot(atoms, weight[...]), 0.0).astype(BF16)
        spot = jnp.concatenate(
            [both_ref[j + k, rows:].astype(F32)[0:1] for k in range(step)], 1
        ).astype(jnp.int32)
        onehot = (iota((tokens, step * rows), 0) == spot).astype(F32)
        sums = sums + dot(onehot.astype(BF16), feats)
        counts = counts + jnp.sum(onehot, -1, keepdims=True)
    act = sums / counts + cond[...].astype(F32)
    xn = normed(act)
    xn_ref[...] = xn.astype(BF16)
    cols = send_ref.shape[0]
    part = xn[:cols]
    for k in range(1, tokens // cols):
        part = jnp.where(device()[1] % (tokens // cols) == k, xn[k * cols : (k + 1) * cols], part)
    send_ref[...] = part.astype(BF16)
    own = act_ref.shape[0]
    col = device()[1]
    mine = act[:own]
    for c in range(1, tokens // own):
        mine = jnp.where(col == c, act[c * own : (c + 1) * own], mine)
    act_ref[...] = mine


def decoder_kernel(
    natom, x1_ref, own_ref, prev_ref, next_ref, proj_ref, edge_ref, w_in, w_out, pos, out
):
    rows = own_ref.shape[0] - EXTRA
    proj = proj_ref[...].astype(F32)
    edge = edge_ref[...].astype(F32)
    tokens = proj.shape[0]
    _, col, me = device()
    rest = tokens - HALO
    below = jnp.where(col == 0, edge, proj[rest:])
    above = jnp.where(col == lax.axis_size("col") - 1, edge, proj[:HALO])
    tables = (
        jnp.concatenate([proj[:rest], below], 0),
        proj,
        jnp.concatenate([above, proj[HALO:]], 0),
    )
    spread = []
    for table, ref in zip(tables, (prev_ref, own_ref, next_ref)):
        spot = ref[rows:].astype(F32)[0:1].astype(jnp.int32)
        onehot = (iota((tokens, rows), 0) == spot).astype(F32).astype(BF16)
        spread.append(dot_tn(onehot, table.astype(BF16)))
    spread = jnp.concatenate([spread[0][rows - HALO :], spread[1], spread[2][:HALO]], 0)
    x = (x1_ref[...].astype(F32) + spread).astype(BF16)
    xn = normed(x).astype(BF16)
    keys = dot(xn, w_in[1]).astype(BF16)
    vals = dot(xn, w_in[2]).astype(BF16)
    qx, qn = x[HALO : HALO + rows], xn[HALO : HALO + rows]
    query = dot(qn, w_in[0]).astype(BF16)
    gate = dot(qn, w_in[3])
    shifts = shifts_of(own_ref, range(rows // QB))
    mask = window_mask(shifts, me * rows - HALO, natom, 2 * rows)
    third = attend(qx, qn, gate, query, keys, vals, mask, w_out[...])
    out[...] = dot_nt(pos[...], normed(third).astype(BF16))


def feat_kernel(row_tokens, starts, feat, token, own):
    rows, width = feat.shape
    row, _, me = device()
    nblk = starts.shape[0]
    lane = iota((EXTRA, width), 1)
    line = iota((EXTRA, width), 0)
    tail = jnp.where(line == 0, token[...] - row * row_tokens, 0)
    for k in range(nblk):
        shift = starts[k] - QB * (me * nblk + k) + HALO
        tail = jnp.where((line == 1) & (lane == k), shift, tail)
    own[:rows] = feat[...]
    own[rows:] = tail.astype(F32).astype(BF16)


def pack_kernel(cuts, first, second, *outs):
    hid = second.shape[1]
    outs = list(outs)
    for layer, cut in enumerate(cuts):
        whole = outs.pop(0)
        whole[:hid] = first[layer, 0]
        whole[hid : 2 * hid] = first[layer, 1]
        whole[2 * hid :] = second[layer]
        begin = 0
        for sixths in cut:
            end = begin + sixths * (3 * hid // 6)
            outs.pop(0)[...] = whole[begin:end]
            begin = end


def bias_kernel(pair_ref, weight, *outs):
    rows, cols, _ = pair_ref.shape
    _, heads, pad = outs[0].shape
    pad = pad - cols

    for q in range(rows):
        bias = dot_nt(weight[...], pair_ref[q])
        bias = jnp.concatenate([bias, jnp.zeros((bias.shape[0], pad), F32)], 1)
        for layer, out in enumerate(outs):
            out[q] = bias[layer * heads : (layer + 1) * heads]


def prepare(sources, targets, sems):
    return [
        pltpu.make_async_copy(source, target, sems.at[i])
        for i, (source, target) in enumerate(zip(sources, targets))
    ]


def query_kernel(
    layer, xn_ref, act_ref, w_in, query, w_key, w_val, gate, w_query, w_gate, sems
):
    fetches = prepare(
        [w_in.at[layer, k] for k in range(4)], [w_query, w_key, w_val, w_gate], sems
    )
    for k in (0, 3, 1, 2):
        fetches[k].start()
    fetches[0].wait()
    query[...] = dot(xn_ref[...], w_query[...]).astype(BF16)
    fetches[3].wait()
    gate[...] = jax.nn.sigmoid(dot(normed(act_ref[...]).astype(BF16), w_gate[...]))
    fetches[1].wait()
    fetches[2].wait()


def attention_kernel(mask_ref, query, here_ref, came_ref, low, high, w_key, w_val, out_ref):
    rows, width = query.shape
    cols = here_ref.shape[0]
    heads = low.shape[1]
    hsize = width // heads
    span = low.shape[2]
    row, col, _ = device()
    mine = col * cols // rows == row
    key_xn = jnp.where(mine, here_ref[...].astype(F32), came_ref[...].astype(F32))
    key_xn = jnp.concatenate([key_xn, jnp.zeros((span - cols, width), F32)], 0).astype(BF16)
    keys = dot(key_xn, w_key[...]).astype(BF16)
    vals = dot(key_xn, w_val[...]).astype(BF16)
    tokens = mask_ref.shape[0]
    count = jnp.int32(0)
    for bit in range(tokens.bit_length() - 1, -1, -1):
        longer = count + (1 << bit)
        inside = longer <= tokens
        last = mask_ref[jnp.where(inside, longer - 1, 0)]
        count = jnp.where(inside & (last == 1), longer, count)
    valid = iota((1, span), 1) + col * cols < count
    valid = valid & (iota((1, span), 1) < cols)
    group = heads // 2
    part = group * hsize
    lane = iota((1, part), 1) // hsize
    spot = iota((1, span), 1)
    levels = jnp.zeros((rows, span), F32)
    for g in range(2):
        wide = slice(g * part, (g + 1) * part)
        kg, vg = keys[:, wide], vals[:, wide]
        picks = [(lane == h).astype(BF16) for h in range(group)]
        stacked = jnp.concatenate([kg * p for p in picks], 0)
        scores = dot_nt(query[:, wide], stacked) * (1.0 / math.sqrt(hsize))
        probs = []
        for h in range(group):
            head = g * group + h
            bias = jnp.concatenate([low[:, head, :], high[:, head, :]], 0)
            score = scores[:, h * span : (h + 1) * span] + bias
            score = jnp.where(valid, score, -1000000000.0)
            top = jnp.max(score, -1, keepdims=True)
            expd = jnp.exp(score - top)
            total = jnp.sum(expd, -1, keepdims=True)
            probs.append((expd / total).astype(BF16))
            levels = jnp.where(spot % heads == head, top + jnp.log(total), levels)
        stacked = jnp.concatenate([vg * p for p in picks], 0)
        out_ref[:, wide] = dot(jnp.concatenate(probs, 1), stacked).astype(BF16)
    high = levels.astype(BF16).astype(F32)
    rest = levels - high
    middle = rest.astype(BF16).astype(F32)
    low = rest - middle
    packed = jnp.where(spot < heads, high, jnp.where(spot < 2 * heads, middle, low))
    out_ref[:, width:] = jnp.where(spot < 3 * heads, packed, 0.0).astype(BF16)


def mix_kernel(layer, heads, message, act_ref, gate, w_out, act_out, w_mix, sems):
    (copy,) = prepare([w_out.at[layer]], [w_mix], sems)
    copy.start()
    width = act_ref.shape[1]
    hsize = width // heads
    parts = [message[j, :, width:].astype(F32) for j in range(message.shape[0])]
    span = parts[0].shape[1]
    levels = [
        p + pltpu.roll(p, span - heads, 1) + pltpu.roll(p, span - 2 * heads, 1) for p in parts
    ]
    top = functools.reduce(jnp.maximum, levels)
    weights = [jnp.exp(level - top) for level in levels]
    whole = functools.reduce(jnp.add, weights)
    lane = iota((1, span), 1)
    row = iota((span, width), 0)
    expand = (row % heads == iota((span, width), 1) // hsize) & (row < 2 * heads)
    expand = expand.astype(F32).astype(BF16)
    packed = []
    for weight in weights:
        weight = weight / whole
        high = weight.astype(BF16).astype(F32)
        both = jnp.where(lane < heads, high, pltpu.roll(weight - high, heads, 1))
        packed.append(jnp.where(lane < 2 * heads, both, 0.0))
    spread = dot(jnp.concatenate(packed, 0).astype(BF16), expand)
    own = act_ref.shape[0]
    attn = jnp.zeros(act_ref.shape, F32)
    for j in range(message.shape[0]):
        attn = attn + spread[j * own : (j + 1) * own] * message[j, :, :width].astype(F32)
    gated = (gate[...] * attn).astype(BF16)
    copy.wait()
    act_out[...] = act_ref[...] + dot(gated, w_mix[...])


def mix(layer, message, act, gate, w_out, heads):
    own, width = act.shape
    return call(
        functools.partial(mix_kernel, layer, heads),
        jax.ShapeDtypeStruct((own, width), F32),
        message,
        act,
        gate,
        far=(w_out,),
        scratch=[pltpu.VMEM((width, width), BF16), pltpu.SemaphoreType.DMA((1,))],
        grant=48,
        flops=4 * own * width * width,
        moved=4 * width * width,
    )


def transition_kernel(groups, pieces, act_ref, *refs):
    others, refs = refs[: groups - 1], refs[groups - 1 :]
    sources = []
    for number in pieces:
        sources.append(refs[:number])
        refs = refs[number:]
    base, send, w_first, w_second, sems = refs
    count, hid = w_second.shape[:2]
    plan = []
    for wanted, target in (((0, 2 * hid), w_first), ((2 * hid, 3 * hid), w_second)):
        for j, source in enumerate(sources):
            begin = 0
            for ref in source:
                end = begin + ref.shape[0]
                low, high = max(begin, wanted[0]), min(end, wanted[1])
                if low < high:
                    near = target.at[j, pl.ds(low - wanted[0], high - low)]
                    plan.append((target is w_first, j, ref.at[pl.ds(low - begin, high - low)], near))
                begin = end
    fetches = prepare([item[2] for item in plan], [item[3] for item in plan], sems)
    for copy in fetches:
        copy.start()

    def arrived(first, j):
        for item, copy in zip(plan, fetches):
            if item[:2] == (first, j):
                copy.wait()

    group = device()[1] // 4
    came = [ref[...] for ref in (act_ref, *others)]
    ordered = []
    for place in range(groups):
        rows = came[0]
        for d in range(1, groups):
            rows = jnp.where((group - place + groups) % groups == d, came[d], rows)
        ordered.append(rows)
    act = jnp.concatenate(ordered, 0)
    rows = normed(act).astype(BF16)
    total = jnp.zeros(act.shape, F32)
    hidden = []
    for j in range(count):
        arrived(True, j)
        both = dot_nt(rows, w_first[j])
        left, right = both[:, :hid], both[:, hid:]
        hidden.append((left * jax.nn.sigmoid(left) * right).astype(BF16))
    for j in range(count):
        arrived(False, j)
        total = total + dot(hidden[j], w_second[j])
    base[...] = act + total
    send[...] = total.astype(BF16)


def transition(act, others, weights):
    own, width = act.shape
    blocks = len(weights)
    hid = sum(part.shape[0] for part in weights[0]) // 3
    parts = [part for source in weights for part in source]
    return call(
        functools.partial(transition_kernel, len(others) + 1, [len(source) for source in weights]),
        [jax.ShapeDtypeStruct(((len(others) + 1) * own, width), kind) for kind in (F32, BF16)],
        act,
        *others,
        far=parts,
        scratch=[
            pltpu.VMEM((blocks, 2 * hid, width), BF16),
            pltpu.VMEM((blocks, hid, width), BF16),
            pltpu.SemaphoreType.DMA((2 * len(parts),)),
        ],
        grant=48,
        flops=12 * own * hid * width * blocks,
        moved=6 * hid * width * blocks,
    )


def close_kernel(project, act_ref, *refs):
    *refs, act_out, out = refs
    if project:
        *refs, tok_atom = refs
    act = act_ref[...]
    for ref in refs:
        act = act + ref[...].astype(F32)
    own = act_out.shape[0]
    mine = act[:own]
    for k in range(1, act.shape[0] // own):
        mine = jnp.where(device()[1] // 4 == k, act[k * own : (k + 1) * own], mine)
    act_out[...] = mine
    normal = normed(act).astype(BF16)
    if project:
        normal = dot(normal, tok_atom[...]).astype(BF16)
    out[...] = normal


def close(own, act, parts, tok_atom):
    rows, width = act.shape
    project = tok_atom is not None
    last = tok_atom.shape[1] if project else width
    return call(
        functools.partial(close_kernel, project),
        [jax.ShapeDtypeStruct((own, width), F32), jax.ShapeDtypeStruct((rows, last), BF16)],
        act,
        *parts,
        *([tok_atom] if project else []),
        flops=10**7,
        moved=10**6,
    )


def row_of(mine, own):
    nrow, ncol = lax.axis_size("row"), lax.axis_size("col")
    parts = [mine]
    for flip in range(1, 4):
        parts.append(
            lax.ppermute(mine, ("row", "col"), [(i, i ^ flip) for i in range(nrow * ncol)])
        )
    low = lax.axis_index("col") % 4
    ordered = []
    for place in range(4):
        rows = parts[place]
        for flip in range(1, 4):
            rows = jnp.where(low == flip, parts[place ^ flip], rows)
        ordered.append(rows.reshape(-1, 1, own, mine.shape[1]))
    return jnp.concatenate(ordered, 1).reshape(-1, mine.shape[1])


def key_source(rows, cols):
    nrow, ncol = lax.axis_size("row"), lax.axis_size("col")
    shares = rows // cols
    chips = ncol // shares
    pairs = []
    for owner in range(nrow):
        near = sorted(range(chips), key=lambda chip: bin((chip ^ owner) % chips).count("1"))
        others = sorted((r for r in range(nrow) if r != owner), key=lambda r: -abs(r - owner))
        for chip, r in zip(near, others):
            for share in range(shares):
                pairs.append((owner * ncol + chip * shares + share, r * ncol + owner * shares + share))
    return pairs


def body(
    atom_feat,
    atom_token,
    window_start,
    token_cond,
    token_mask,
    pair,
    enc_in,
    enc_out,
    pool_weight,
    tok_in,
    tok_out,
    pair_weight,
    trans_in,
    trans_out,
    tok_atom,
    dec_in,
    dec_out,
    pos_out,
):
    nrow, ncol = lax.axis_size("row"), lax.axis_size("col")
    everyone = ("row", "col")
    count = nrow * ncol
    me_col = lax.axis_index("col")
    rows, width = token_cond.shape
    cols = pair.shape[1]
    heads = pair_weight.shape[2]
    own = rows // ncol
    atoms, afeat = atom_feat.shape
    natom = atoms * count
    nblk = atoms // QB

    hid = trans_out.shape[1]
    feat = call(
        functools.partial(feat_kernel, rows),
        jax.ShapeDtypeStruct((atoms + EXTRA, afeat), BF16),
        atom_feat,
        atom_token[None],
        scalars=(window_start,),
        grant=48,
        moved=10**5,
    )
    up = [(i, i + 1) for i in range(count - 1)]
    prev = lax.ppermute(feat, everyone, up)
    after = lax.ppermute(feat, everyone, [(b, a) for a, b in up])
    _, first_part, second_part = lax.optimization_barrier(
        (feat, jnp.swapaxes(trans_in, 2, 3), trans_out)
    )
    matrix = jax.ShapeDtypeStruct((3 * hid, width), BF16)
    cuts = ((2, 3, 1), (3, 3))
    pieces = call(
        functools.partial(pack_kernel, cuts),
        [
            jax.ShapeDtypeStruct((sixths * (3 * hid // 6), width), BF16)
            for cut in cuts
            for sixths in (6,) + cut
        ],
        first_part,
        second_part,
        grant=60,
        moved=12 * trans_out.size,
    )
    packed, cut_up = [], []
    for cut in cuts:
        packed.append(pieces[0])
        cut_up.append(pieces[1 : 1 + len(cut)])
        pieces = pieces[1 + len(cut) :]
    prev, after, early = lax.optimization_barrier((prev, after, cut_up[0][0]))
    neighbour = [(i, i ^ 2) for i in range(count)]
    sibling = [(i, i ^ 1) for i in range(count)]
    across = [[lax.ppermute(early, everyone, neighbour)], []]

    ext, copies = call(
        functools.partial(encoder_kernel, natom),
        [
            jax.ShapeDtypeStruct((atoms + 2 * HALO, afeat), BF16),
            jax.ShapeDtypeStruct((ncol, atoms + EXTRA, afeat), BF16),
        ],
        feat,
        prev,
        after,
        enc_in,
        enc_out,
        flops=10**8,
        moved=10**6,
    )
    span = -(-cols // 128) * 128
    step = 24
    early_steps = rows // step * 5 // 8

    def bias_of(part, weights):
        begin, end = ((0, early_steps), (early_steps, rows // step))[part]
        return pl.pallas_call(
            bias_kernel,
            grid=(end - begin,),
            out_shape=[jax.ShapeDtypeStruct(((end - begin) * step, heads, span), F32)] * BLOCKS,
            in_specs=[
                pl.BlockSpec((step, cols, pair.shape[2]), lambda i: (i + begin, 0, 0)),
                pl.BlockSpec(weights.shape, lambda i: (0, 0)),
            ],
            out_specs=[pl.BlockSpec((step, heads, span), lambda i: (i, 0, 0))] * BLOCKS,
            compiler_params=pltpu.CompilerParams(vmem_limit_bytes=(52 if part else 60) * MIB),
            cost_estimate=pl.CostEstimate(
                flops=2 * 10**9, bytes_accessed=4 * 10**6, transcendentals=0
            ),
        )(pair, weights)

    weights = jnp.swapaxes(pair_weight, 1, 2).reshape(BLOCKS * heads, -1)
    copies, first_weights = lax.optimization_barrier((copies, weights))
    low = bias_of(0, first_weights)
    both = lax.all_to_all(copies, "col", 0, 0)
    both, low, across[0][0] = lax.optimization_barrier((both, low, across[0][0]))

    act, xn, send = call(
        pool_kernel,
        [
            jax.ShapeDtypeStruct((own, width), F32),
            jax.ShapeDtypeStruct((rows, width), BF16),
            jax.ShapeDtypeStruct((cols, width), BF16),
        ],
        both,
        pool_weight,
        token_cond,
        flops=10**9,
        moved=10**6,
    )

    pairs = key_source(rows, cols)
    share = me_col % (rows // cols)
    peers = ncol // 4
    shifts = [
        [(r * ncol + c, r * ncol + (c + 4 * d) % ncol) for r in range(nrow) for c in range(ncol)]
        for d in range(peers)
    ]
    xn, weights = lax.optimization_barrier((xn, weights))
    beside, beyond = [], [[], []]
    for layer in range(BLOCKS):
        last = layer == BLOCKS - 1
        if layer:
            send = lax.dynamic_slice_in_dim(xn, share * cols, cols, 0)
            send, xn = lax.optimization_barrier((send, xn))
        came = lax.ppermute(send, everyone, pairs)
        matrix = jax.ShapeDtypeStruct((width, width), BF16)
        query, w_key, w_val, gate = call(
            functools.partial(query_kernel, layer),
            [
                jax.ShapeDtypeStruct((rows, width), BF16),
                matrix,
                matrix,
                jax.ShapeDtypeStruct((own, width), F32),
            ],
            xn,
            act,
            far=(tok_in,),
            scratch=[pltpu.VMEM((width, width), BF16)] * 2 + [pltpu.SemaphoreType.DMA((4,))],
            grant=48,
            flops=2 * rows * width * width,
            moved=8 * width * width,
        )
        if not layer:
            high = list(bias_of(1, weights))
            high[0], *late = lax.optimization_barrier((high[0], *cut_up[0][1:]))
            across[0] += [lax.ppermute(part, everyone, neighbour) for part in late]
            high[0], *ready = lax.optimization_barrier((high[0], *packed))
            beside = [lax.ppermute(part, everyone, sibling) for part in ready]
        else:
            query, late = lax.optimization_barrier((query, cut_up[1][1]))
            across[1].append(lax.ppermute(late, everyone, neighbour))
        message = call(
            attention_kernel,
            jax.ShapeDtypeStruct((rows, width + span), BF16),
            query,
            send,
            came,
            low[layer],
            high[layer],
            w_key,
            w_val,
            scalars=(token_mask,),
            grant=16,
            flops=10**9,
            moved=8 * 10**6,
        )
        message = lax.all_to_all(message.reshape(ncol, own, -1), "col", 0, 0)
        if not layer:
            message, ready = lax.optimization_barrier((message, cut_up[1][0]))
            across[1].append(lax.ppermute(ready, everyone, neighbour))
        act = mix(layer, message, act, gate, tok_out, heads)
        came_rows = [lax.ppermute(act, everyone, shifts[d]) for d in range(1, peers)]
        act, *ready = lax.optimization_barrier((act, *across[layer]))
        beyond[layer] = [lax.ppermute(part, everyone, sibling) for part in ready]
        act, part = transition(
            act, came_rows, ([packed[layer]], [beside[layer]], across[layer], beyond[layer])
        )
        parts = [lax.ppermute(part, everyone, shifts[d]) for d in range(1, peers)]
        act, mine = close(own, act, parts, tok_atom if last else None)
        if not last:
            mine, across[1][0] = lax.optimization_barrier((mine, across[1][0]))
        gathered = row_of(mine, own)
        if not last:
            xn = gathered

    bounds = [(r * ncol, (r + 1) * ncol) for r in range(nrow - 1)]
    bounds += [((r + 2) * ncol - 1, (r + 1) * ncol - 1) for r in range(nrow - 1)]
    edge = jnp.where(me_col == 0, gathered[rows - HALO :], gathered[:HALO])
    edge = lax.ppermute(edge, everyone, bounds)

    return call(
        functools.partial(decoder_kernel, natom),
        jax.ShapeDtypeStruct((pos_out.shape[0], atoms), F32),
        ext,
        feat,
        prev,
        after,
        gathered,
        edge,
        dec_in,
        dec_out,
        pos_out,
        flops=10**8,
        moved=10**6,
    )


def solution(mesh):
    in_specs = (
        P(("row", "col"), None),
        P(("row", "col")),
        P(("row", "col")),
        P("row", None),
        P(),
        P("row", "col", None),
        P(),
        P(),
        P(),
        P(),
        P(),
        P(),
        P(None, None, None, "col"),
        P(None, "col", None),
        P(),
        P(),
        P(),
        P(),
    )
    out_specs = P(None, ("row", "col"))
    return jax.shard_map(body, mesh=mesh, in_specs=in_specs, out_specs=out_specs, check_vma=False)
```

```python
import functools
import math

import jax
import jax.numpy as jnp
from jax import lax
from jax.experimental import pallas as pl
from jax.experimental.pallas import tpu as pltpu
from jax.sharding import PartitionSpec as P

HA = 4
QB = 32
KW = 128
HALO = 64
BLOCKS = 2
EXTRA = 16
MIB = 1 << 20
F32 = jnp.float32
BF16 = jnp.bfloat16


def call(kernel, outs, *args, scalars=(), far=(), scratch=(), grant=8, flops=0, moved=0):
    smem = pl.BlockSpec(memory_space=pltpu.SMEM)
    vmem = pl.BlockSpec(memory_space=pltpu.VMEM)
    hbm = pl.BlockSpec(memory_space=pltpu.HBM)
    return pl.pallas_call(
        kernel,
        out_shape=outs,
        in_specs=[smem] * len(scalars) + [vmem] * len(args) + [hbm] * len(far),
        out_specs=jax.tree.map(lambda _: vmem, outs),
        scratch_shapes=list(scratch),
        compiler_params=pltpu.CompilerParams(vmem_limit_bytes=grant * MIB),
        cost_estimate=pl.CostEstimate(flops=flops, bytes_accessed=moved, transcendentals=0),
    )(*scalars, *args, *far)


def dot(a, b):
    return jnp.dot(a, b, preferred_element_type=F32)


def dot_nt(a, b):
    return lax.dot_general(a, b, (((1,), (1,)), ((), ())), preferred_element_type=F32)


def dot_tn(a, b):
    return lax.dot_general(a, b, (((0,), (0,)), ((), ())), preferred_element_type=F32)


def normed(x):
    x = x.astype(F32)
    cent = x - jnp.mean(x, -1, keepdims=True)
    var = jnp.mean(cent * cent, -1, keepdims=True)
    return cent * lax.rsqrt(var + 1e-05)


def iota(shape, dim):
    return lax.broadcasted_iota(jnp.int32, shape, dim)


def device():
    row, col = lax.axis_index("row"), lax.axis_index("col")
    return row, col, row * lax.axis_size("col") + col


def window_mask(shifts, first, natom, nkeys):
    shape = (len(shifts) * QB, nkeys)
    block = iota(shape, 0) // QB
    low = jnp.zeros(shape, jnp.int32)
    for i, shift in enumerate(shifts):
        low = jnp.where(block == i, shift + QB * i, low)
    key = iota(shape, 1)
    atom = key + first
    return (key >= low) & (key < low + KW) & (atom >= 0) & (atom < natom)


def attend(x, xn, gate, query, keys, vals, mask, w_out):
    width = x.shape[1]
    hsize = width // HA
    lane = iota((1, width), 1) // hsize
    outs = jnp.zeros(x.shape, F32)
    for h in range(HA):
        pick = (lane == h).astype(BF16)
        scores = dot_nt(query, keys * pick) * (1.0 / math.sqrt(hsize))
        scores = jnp.where(mask, scores, -1000000000.0)
        top = jnp.max(scores, -1, keepdims=True)
        expd = jnp.exp(scores - top)
        total = jnp.sum(expd, -1, keepdims=True)
        outs = outs + dot(expd.astype(BF16), vals * pick) / total
    gated = (jax.nn.sigmoid(gate) * outs).astype(BF16)
    return (x.astype(F32) + dot(gated, w_out)).astype(BF16)


def shifts_of(tail_ref, lanes):
    tail = tail_ref[tail_ref.shape[0] - EXTRA :, :].astype(F32)
    return [tail[1:2, k : k + 1].astype(jnp.int32) for k in lanes]


def encoder_kernel(natom, own_ref, prev_ref, next_ref, w_in, w_out, ext_ref, all_ref):
    rows = own_ref.shape[0] - EXTRA
    nblk = rows // QB
    half = HALO // QB
    x = jnp.concatenate([prev_ref[:rows], own_ref[:rows], next_ref[:rows]], 0)
    xn = normed(x).astype(BF16)
    keys = dot(xn, w_in[1]).astype(BF16)
    vals = dot(xn, w_in[2]).astype(BF16)
    qx, qn = x[HALO : 3 * rows - HALO], xn[HALO : 3 * rows - HALO]
    query = dot(qn, w_in[0]).astype(BF16)
    gate = dot(qn, w_in[3])
    shifts = (
        shifts_of(prev_ref, range(nblk - half, nblk))
        + shifts_of(own_ref, range(nblk))
        + shifts_of(next_ref, range(half))
    )
    first = device()[2] * rows - rows
    for part in range(2):
        mine = slice(part * rows, (part + 1) * rows)
        seen = slice(part * rows, (part + 2) * rows)
        mask = window_mask(
            shifts[part * nblk : (part + 1) * nblk], first + part * rows, natom, 2 * rows
        )
        ext_ref[mine] = attend(
            qx[mine], qn[mine], gate[mine], query[mine], keys[seen], vals[seen], mask, w_out[...]
        )
    new = ext_ref[HALO : HALO + rows]
    tail = own_ref[rows:]
    for j in range(all_ref.shape[0]):
        all_ref[j, :rows] = new
        all_ref[j, rows:] = tail


def pool_kernel(both_ref, weight, cond, act_ref, xn_ref, send_ref):
    count, rows = both_ref.shape[0], both_ref.shape[1] - EXTRA
    tokens = cond.shape[0]
    sums = jnp.zeros(cond.shape, F32)
    counts = jnp.zeros((tokens, 1), F32)
    step = 4 if count % 4 == 0 else 1
    for j in range(0, count, step):
        atoms = jnp.concatenate([both_ref[j + k, :rows] for k in range(step)], 0)
        feats = jnp.maximum(dot(atoms, weight[...]), 0.0).astype(BF16)
        spot = jnp.concatenate(
            [both_ref[j + k, rows:].astype(F32)[0:1] for k in range(step)], 1
        ).astype(jnp.int32)
        onehot = (iota((tokens, step * rows), 0) == spot).astype(F32)
        sums = sums + dot(onehot.astype(BF16), feats)
        counts = counts + jnp.sum(onehot, -1, keepdims=True)
    act = sums / counts + cond[...].astype(F32)
    xn = normed(act)
    xn_ref[...] = xn.astype(BF16)
    cols = send_ref.shape[0]
    part = xn[:cols]
    for k in range(1, tokens // cols):
        part = jnp.where(device()[1] % (tokens // cols) == k, xn[k * cols : (k + 1) * cols], part)
    send_ref[...] = part.astype(BF16)
    own = act_ref.shape[0]
    col = device()[1]
    mine = act[:own]
    for c in range(1, tokens // own):
        mine = jnp.where(col == c, act[c * own : (c + 1) * own], mine)
    act_ref[...] = mine


def decoder_kernel(
    natom, x1_ref, own_ref, prev_ref, next_ref, proj_ref, edge_ref, w_in, w_out, pos, out
):
    rows = own_ref.shape[0] - EXTRA
    proj = proj_ref[...].astype(F32)
    edge = edge_ref[...].astype(F32)
    tokens = proj.shape[0]
    _, col, me = device()
    rest = tokens - HALO
    below = jnp.where(col == 0, edge, proj[rest:])
    above = jnp.where(col == lax.axis_size("col") - 1, edge, proj[:HALO])
    tables = (
        jnp.concatenate([proj[:rest], below], 0),
        proj,
        jnp.concatenate([above, proj[HALO:]], 0),
    )
    spread = []
    for table, ref in zip(tables, (prev_ref, own_ref, next_ref)):
        spot = ref[rows:].astype(F32)[0:1].astype(jnp.int32)
        onehot = (iota((tokens, rows), 0) == spot).astype(F32).astype(BF16)
        spread.append(dot_tn(onehot, table.astype(BF16)))
    spread = jnp.concatenate([spread[0][rows - HALO :], spread[1], spread[2][:HALO]], 0)
    x = (x1_ref[...].astype(F32) + spread).astype(BF16)
    xn = normed(x).astype(BF16)
    keys = dot(xn, w_in[1]).astype(BF16)
    vals = dot(xn, w_in[2]).astype(BF16)
    qx, qn = x[HALO : HALO + rows], xn[HALO : HALO + rows]
    query = dot(qn, w_in[0]).astype(BF16)
    gate = dot(qn, w_in[3])
    shifts = shifts_of(own_ref, range(rows // QB))
    mask = window_mask(shifts, me * rows - HALO, natom, 2 * rows)
    third = attend(qx, qn, gate, query, keys, vals, mask, w_out[...])
    out[...] = dot_nt(pos[...], normed(third).astype(BF16))


def feat_kernel(row_tokens, starts, feat, token, own):
    rows, width = feat.shape
    row, _, me = device()
    nblk = starts.shape[0]
    lane = iota((EXTRA, width), 1)
    line = iota((EXTRA, width), 0)
    tail = jnp.where(line == 0, token[...] - row * row_tokens, 0)
    for k in range(nblk):
        shift = starts[k] - QB * (me * nblk + k) + HALO
        tail = jnp.where((line == 1) & (lane == k), shift, tail)
    own[:rows] = feat[...]
    own[rows:] = tail.astype(F32).astype(BF16)


def pack_kernel(cuts, first, second, *outs):
    hid = second.shape[1]
    outs = list(outs)
    for layer, cut in enumerate(cuts):
        whole = outs.pop(0)
        whole[:hid] = first[layer, 0]
        whole[hid : 2 * hid] = first[layer, 1]
        whole[2 * hid :] = second[layer]
        begin = 0
        for sixths in cut:
            end = begin + sixths * (3 * hid // 6)
            outs.pop(0)[...] = whole[begin:end]
            begin = end


def bias_kernel(pair_ref, weight, *outs):
    rows, cols, _ = pair_ref.shape
    _, heads, pad = outs[0].shape
    pad = pad - cols

    for q in range(rows):
        bias = dot_nt(weight[...], pair_ref[q])
        bias = jnp.concatenate([bias, jnp.zeros((bias.shape[0], pad), F32)], 1)
        for layer, out in enumerate(outs):
            out[q] = bias[layer * heads : (layer + 1) * heads]


def prepare(sources, targets, sems):
    return [
        pltpu.make_async_copy(source, target, sems.at[i])
        for i, (source, target) in enumerate(zip(sources, targets))
    ]


def query_kernel(
    layer, xn_ref, act_ref, w_in, query, w_key, w_val, gate, w_query, w_gate, sems
):
    fetches = prepare(
        [w_in.at[layer, k] for k in range(4)], [w_query, w_key, w_val, w_gate], sems
    )
    for k in (0, 3, 1, 2):
        fetches[k].start()
    fetches[0].wait()
    query[...] = dot(xn_ref[...], w_query[...]).astype(BF16)
    fetches[3].wait()
    gate[...] = jax.nn.sigmoid(dot(normed(act_ref[...]).astype(BF16), w_gate[...]))
    fetches[1].wait()
    fetches[2].wait()


def attention_kernel(mask_ref, query, here_ref, came_ref, low, high, w_key, w_val, out_ref):
    rows, width = query.shape
    cols = here_ref.shape[0]
    heads = low.shape[1]
    hsize = width // heads
    span = low.shape[2]
    row, col, _ = device()
    mine = col * cols // rows == row
    key_xn = jnp.where(mine, here_ref[...].astype(F32), came_ref[...].astype(F32))
    key_xn = jnp.concatenate([key_xn, jnp.zeros((span - cols, width), F32)], 0).astype(BF16)
    keys = dot(key_xn, w_key[...]).astype(BF16)
    vals = dot(key_xn, w_val[...]).astype(BF16)
    tokens = mask_ref.shape[0]
    count = jnp.int32(0)
    for bit in range(tokens.bit_length() - 1, -1, -1):
        longer = count + (1 << bit)
        inside = longer <= tokens
        last = mask_ref[jnp.where(inside, longer - 1, 0)]
        count = jnp.where(inside & (last == 1), longer, count)
    valid = iota((1, span), 1) + col * cols < count
    valid = valid & (iota((1, span), 1) < cols)
    group = heads // 2
    part = group * hsize
    lane = iota((1, part), 1) // hsize
    spot = iota((1, span), 1)
    levels = jnp.zeros((rows, span), F32)
    for g in range(2):
        wide = slice(g * part, (g + 1) * part)
        kg, vg = keys[:, wide], vals[:, wide]
        picks = [(lane == h).astype(BF16) for h in range(group)]
        stacked = jnp.concatenate([kg * p for p in picks], 0)
        scores = dot_nt(query[:, wide], stacked) * (1.0 / math.sqrt(hsize))
        probs = []
        for h in range(group):
            head = g * group + h
            bias = jnp.concatenate([low[:, head, :], high[:, head, :]], 0)
            score = scores[:, h * span : (h + 1) * span] + bias
            score = jnp.where(valid, score, -1000000000.0)
            top = jnp.max(score, -1, keepdims=True)
            expd = jnp.exp(score - top)
            total = jnp.sum(expd, -1, keepdims=True)
            probs.append((expd / total).astype(BF16))
            levels = jnp.where(spot % heads == head, top + jnp.log(total), levels)
        stacked = jnp.concatenate([vg * p for p in picks], 0)
        out_ref[:, wide] = dot(jnp.concatenate(probs, 1), stacked).astype(BF16)
    high = levels.astype(BF16).astype(F32)
    rest = levels - high
    middle = rest.astype(BF16).astype(F32)
    low = rest - middle
    packed = jnp.where(spot < heads, high, jnp.where(spot < 2 * heads, middle, low))
    out_ref[:, width:] = jnp.where(spot < 3 * heads, packed, 0.0).astype(BF16)


def mix_kernel(layer, heads, message, act_ref, gate, w_out, act_out, w_mix, sems):
    (copy,) = prepare([w_out.at[layer]], [w_mix], sems)
    copy.start()
    width = act_ref.shape[1]
    hsize = width // heads
    parts = [message[j, :, width:].astype(F32) for j in range(message.shape[0])]
    span = parts[0].shape[1]
    levels = [
        p + pltpu.roll(p, span - heads, 1) + pltpu.roll(p, span - 2 * heads, 1) for p in parts
    ]
    top = functools.reduce(jnp.maximum, levels)
    weights = [jnp.exp(level - top) for level in levels]
    whole = functools.reduce(jnp.add, weights)
    lane = iota((1, span), 1)
    row = iota((span, width), 0)
    expand = (row % heads == iota((span, width), 1) // hsize) & (row < 2 * heads)
    expand = expand.astype(F32).astype(BF16)
    packed = []
    for weight in weights:
        weight = weight / whole
        high = weight.astype(BF16).astype(F32)
        both = jnp.where(lane < heads, high, pltpu.roll(weight - high, heads, 1))
        packed.append(jnp.where(lane < 2 * heads, both, 0.0))
    spread = dot(jnp.concatenate(packed, 0).astype(BF16), expand)
    own = act_ref.shape[0]
    attn = jnp.zeros(act_ref.shape, F32)
    for j in range(message.shape[0]):
        attn = attn + spread[j * own : (j + 1) * own] * message[j, :, :width].astype(F32)
    gated = (gate[...] * attn).astype(BF16)
    copy.wait()
    act_out[...] = act_ref[...] + dot(gated, w_mix[...])


def mix(layer, message, act, gate, w_out, heads):
    own, width = act.shape
    return call(
        functools.partial(mix_kernel, layer, heads),
        jax.ShapeDtypeStruct((own, width), F32),
        message,
        act,
        gate,
        far=(w_out,),
        scratch=[pltpu.VMEM((width, width), BF16), pltpu.SemaphoreType.DMA((1,))],
        grant=48,
        flops=4 * own * width * width,
        moved=4 * width * width,
    )


def transition_kernel(groups, pieces, act_ref, *refs):
    others, refs = refs[: groups - 1], refs[groups - 1 :]
    sources = []
    for number in pieces:
        sources.append(refs[:number])
        refs = refs[number:]
    base, send, w_first, w_second, sems = refs
    count, hid = w_second.shape[:2]
    plan = []
    for wanted, target in (((0, 2 * hid), w_first), ((2 * hid, 3 * hid), w_second)):
        for j, source in enumerate(sources):
            begin = 0
            for ref in source:
                end = begin + ref.shape[0]
                low, high = max(begin, wanted[0]), min(end, wanted[1])
                if low < high:
                    near = target.at[j, pl.ds(low - wanted[0], high - low)]
                    plan.append((target is w_first, j, ref.at[pl.ds(low - begin, high - low)], near))
                begin = end
    fetches = prepare([item[2] for item in plan], [item[3] for item in plan], sems)
    for copy in fetches:
        copy.start()

    def arrived(first, j):
        for item, copy in zip(plan, fetches):
            if item[:2] == (first, j):
                copy.wait()

    group = device()[1] // 4
    came = [ref[...] for ref in (act_ref, *others)]
    ordered = []
    for place in range(groups):
        rows = came[0]
        for d in range(1, groups):
            rows = jnp.where((group - place + groups) % groups == d, came[d], rows)
        ordered.append(rows)
    act = jnp.concatenate(ordered, 0)
    rows = normed(act).astype(BF16)
    total = jnp.zeros(act.shape, F32)
    hidden = []
    for j in range(count):
        arrived(True, j)
        both = dot_nt(rows, w_first[j])
        left, right = both[:, :hid], both[:, hid:]
        hidden.append((left * jax.nn.sigmoid(left) * right).astype(BF16))
    for j in range(count):
        arrived(False, j)
        total = total + dot(hidden[j], w_second[j])
    base[...] = act + total
    send[...] = total.astype(BF16)


def transition(act, others, weights):
    own, width = act.shape
    blocks = len(weights)
    hid = sum(part.shape[0] for part in weights[0]) // 3
    parts = [part for source in weights for part in source]
    return call(
        functools.partial(transition_kernel, len(others) + 1, [len(source) for source in weights]),
        [jax.ShapeDtypeStruct(((len(others) + 1) * own, width), kind) for kind in (F32, BF16)],
        act,
        *others,
        far=parts,
        scratch=[
            pltpu.VMEM((blocks, 2 * hid, width), BF16),
            pltpu.VMEM((blocks, hid, width), BF16),
            pltpu.SemaphoreType.DMA((2 * len(parts),)),
        ],
        grant=48,
        flops=12 * own * hid * width * blocks,
        moved=6 * hid * width * blocks,
    )


def close_kernel(project, act_ref, *refs):
    *refs, act_out, out = refs
    if project:
        *refs, tok_atom = refs
    act = act_ref[...]
    for ref in refs:
        act = act + ref[...].astype(F32)
    own = act_out.shape[0]
    mine = act[:own]
    for k in range(1, act.shape[0] // own):
        mine = jnp.where(device()[1] // 4 == k, act[k * own : (k + 1) * own], mine)
    act_out[...] = mine
    normal = normed(act).astype(BF16)
    if project:
        normal = dot(normal, tok_atom[...]).astype(BF16)
    out[...] = normal


def close(own, act, parts, tok_atom):
    rows, width = act.shape
    project = tok_atom is not None
    last = tok_atom.shape[1] if project else width
    return call(
        functools.partial(close_kernel, project),
        [jax.ShapeDtypeStruct((own, width), F32), jax.ShapeDtypeStruct((rows, last), BF16)],
        act,
        *parts,
        *([tok_atom] if project else []),
        flops=10**7,
        moved=10**6,
    )


def row_of(mine, own):
    nrow, ncol = lax.axis_size("row"), lax.axis_size("col")
    parts = [mine]
    for flip in range(1, 4):
        parts.append(
            lax.ppermute(mine, ("row", "col"), [(i, i ^ flip) for i in range(nrow * ncol)])
        )
    low = lax.axis_index("col") % 4
    ordered = []
    for place in range(4):
        rows = parts[place]
        for flip in range(1, 4):
            rows = jnp.where(low == flip, parts[place ^ flip], rows)
        ordered.append(rows.reshape(-1, 1, own, mine.shape[1]))
    return jnp.concatenate(ordered, 1).reshape(-1, mine.shape[1])


def key_source(rows, cols):
    nrow, ncol = lax.axis_size("row"), lax.axis_size("col")
    shares = rows // cols
    chips = ncol // shares
    pairs = []
    for owner in range(nrow):
        near = sorted(range(chips), key=lambda chip: bin((chip ^ owner) % chips).count("1"))
        others = sorted((r for r in range(nrow) if r != owner), key=lambda r: -abs(r - owner))
        for chip, r in zip(near, others):
            for share in range(shares):
                pairs.append((owner * ncol + chip * shares + share, r * ncol + owner * shares + share))
    return pairs


def body(
    atom_feat,
    atom_token,
    window_start,
    token_cond,
    token_mask,
    pair,
    enc_in,
    enc_out,
    pool_weight,
    tok_in,
    tok_out,
    pair_weight,
    trans_in,
    trans_out,
    tok_atom,
    dec_in,
    dec_out,
    pos_out,
):
    nrow, ncol = lax.axis_size("row"), lax.axis_size("col")
    everyone = ("row", "col")
    count = nrow * ncol
    me_col = lax.axis_index("col")
    rows, width = token_cond.shape
    cols = pair.shape[1]
    heads = pair_weight.shape[2]
    own = rows // ncol
    atoms, afeat = atom_feat.shape
    natom = atoms * count
    nblk = atoms // QB

    hid = trans_out.shape[1]
    feat = call(
        functools.partial(feat_kernel, rows),
        jax.ShapeDtypeStruct((atoms + EXTRA, afeat), BF16),
        atom_feat,
        atom_token[None],
        scalars=(window_start,),
        grant=48,
        moved=10**5,
    )
    up = [(i, i + 1) for i in range(count - 1)]
    prev = lax.ppermute(feat, everyone, up)
    after = lax.ppermute(feat, everyone, [(b, a) for a, b in up])
    _, first_part, second_part = lax.optimization_barrier(
        (feat, jnp.swapaxes(trans_in, 2, 3), trans_out)
    )
    matrix = jax.ShapeDtypeStruct((3 * hid, width), BF16)
    cuts = ((2, 3, 1), (3, 3))
    pieces = call(
        functools.partial(pack_kernel, cuts),
        [
            jax.ShapeDtypeStruct((sixths * (3 * hid // 6), width), BF16)
            for cut in cuts
            for sixths in (6,) + cut
        ],
        first_part,
        second_part,
        grant=60,
        moved=12 * trans_out.size,
    )
    packed, cut_up = [], []
    for cut in cuts:
        packed.append(pieces[0])
        cut_up.append(pieces[1 : 1 + len(cut)])
        pieces = pieces[1 + len(cut) :]
    prev, after, early = lax.optimization_barrier((prev, after, cut_up[0][0]))
    neighbour = [(i, i ^ 2) for i in range(count)]
    sibling = [(i, i ^ 1) for i in range(count)]
    across = [[lax.ppermute(early, everyone, neighbour)], []]

    ext, copies = call(
        functools.partial(encoder_kernel, natom),
        [
            jax.ShapeDtypeStruct((atoms + 2 * HALO, afeat), BF16),
            jax.ShapeDtypeStruct((ncol, atoms + EXTRA, afeat), BF16),
        ],
        feat,
        prev,
        after,
        enc_in,
        enc_out,
        flops=10**8,
        moved=10**6,
    )
    span = -(-cols // 128) * 128
    step = 24
    early_steps = rows // step * 5 // 8

    def bias_of(part, weights):
        begin, end = ((0, early_steps), (early_steps, rows // step))[part]
        return pl.pallas_call(
            bias_kernel,
            grid=(end - begin,),
            out_shape=[jax.ShapeDtypeStruct(((end - begin) * step, heads, span), F32)] * BLOCKS,
            in_specs=[
                pl.BlockSpec((step, cols, pair.shape[2]), lambda i: (i + begin, 0, 0)),
                pl.BlockSpec(weights.shape, lambda i: (0, 0)),
            ],
            out_specs=[pl.BlockSpec((step, heads, span), lambda i: (i, 0, 0))] * BLOCKS,
            compiler_params=pltpu.CompilerParams(vmem_limit_bytes=(52 if part else 60) * MIB),
            cost_estimate=pl.CostEstimate(
                flops=2 * 10**9, bytes_accessed=4 * 10**6, transcendentals=0
            ),
        )(pair, weights)

    weights = jnp.swapaxes(pair_weight, 1, 2).reshape(BLOCKS * heads, -1)
    copies, first_weights = lax.optimization_barrier((copies, weights))
    low = bias_of(0, first_weights)
    both = lax.all_to_all(copies, "col", 0, 0)
    both, low, across[0][0] = lax.optimization_barrier((both, low, across[0][0]))

    act, xn, send = call(
        pool_kernel,
        [
            jax.ShapeDtypeStruct((own, width), F32),
            jax.ShapeDtypeStruct((rows, width), BF16),
            jax.ShapeDtypeStruct((cols, width), BF16),
        ],
        both,
        pool_weight,
        token_cond,
        flops=10**9,
        moved=10**6,
    )

    pairs = key_source(rows, cols)
    share = me_col % (rows // cols)
    peers = ncol // 4
    shifts = [
        [(r * ncol + c, r * ncol + (c + 4 * d) % ncol) for r in range(nrow) for c in range(ncol)]
        for d in range(peers)
    ]
    xn, weights = lax.optimization_barrier((xn, weights))
    beside, beyond = [], [[], []]
    for layer in range(BLOCKS):
        last = layer == BLOCKS - 1
        if layer:
            send = lax.dynamic_slice_in_dim(xn, share * cols, cols, 0)
            send, xn = lax.optimization_barrier((send, xn))
        came = lax.ppermute(send, everyone, pairs)
        matrix = jax.ShapeDtypeStruct((width, width), BF16)
        query, w_key, w_val, gate = call(
            functools.partial(query_kernel, layer),
            [
                jax.ShapeDtypeStruct((rows, width), BF16),
                matrix,
                matrix,
                jax.ShapeDtypeStruct((own, width), F32),
            ],
            xn,
            act,
            far=(tok_in,),
            scratch=[pltpu.VMEM((width, width), BF16)] * 2 + [pltpu.SemaphoreType.DMA((4,))],
            grant=48,
            flops=2 * rows * width * width,
            moved=8 * width * width,
        )
        if not layer:
            high = list(bias_of(1, weights))
            high[0], late = lax.optimization_barrier((high[0], cut_up[0][1]))
            across[0].append(lax.ppermute(late, everyone, neighbour))
            high[0], *ready = lax.optimization_barrier((high[0], *packed))
            beside = [lax.ppermute(part, everyone, sibling) for part in ready]
        else:
            query, late = lax.optimization_barrier((query, cut_up[1][1]))
            across[1].append(lax.ppermute(late, everyone, neighbour))
        message = call(
            attention_kernel,
            jax.ShapeDtypeStruct((rows, width + span), BF16),
            query,
            send,
            came,
            low[layer],
            high[layer],
            w_key,
            w_val,
            scalars=(token_mask,),
            grant=16,
            flops=10**9,
            moved=8 * 10**6,
        )
        message = lax.all_to_all(message.reshape(ncol, own, -1), "col", 0, 0)
        if not layer:
            message, late, ready = lax.optimization_barrier((message, cut_up[0][2], cut_up[1][0]))
            across[0].append(lax.ppermute(late, everyone, neighbour))
            across[1].append(lax.ppermute(ready, everyone, neighbour))
        act = mix(layer, message, act, gate, tok_out, heads)
        came_rows = [lax.ppermute(act, everyone, shifts[d]) for d in range(1, peers)]
        act, *ready = lax.optimization_barrier((act, *across[layer]))
        beyond[layer] = [lax.ppermute(part, everyone, sibling) for part in ready]
        act, part = transition(
            act, came_rows, ([packed[layer]], [beside[layer]], across[layer], beyond[layer])
        )
        parts = [lax.ppermute(part, everyone, shifts[d]) for d in range(1, peers)]
        act, mine = close(own, act, parts, tok_atom if last else None)
        if not last:
            mine, across[1][0] = lax.optimization_barrier((mine, across[1][0]))
        gathered = row_of(mine, own)
        if not last:
            xn = gathered

    bounds = [(r * ncol, (r + 1) * ncol) for r in range(nrow - 1)]
    bounds += [((r + 2) * ncol - 1, (r + 1) * ncol - 1) for r in range(nrow - 1)]
    edge = jnp.where(me_col == 0, gathered[rows - HALO :], gathered[:HALO])
    edge = lax.ppermute(edge, everyone, bounds)

    return call(
        functools.partial(decoder_kernel, natom),
        jax.ShapeDtypeStruct((pos_out.shape[0], atoms), F32),
        ext,
        feat,
        prev,
        after,
        gathered,
        edge,
        dec_in,
        dec_out,
        pos_out,
        flops=10**8,
        moved=10**6,
    )


def solution(mesh):
    in_specs = (
        P(("row", "col"), None),
        P(("row", "col")),
        P(("row", "col")),
        P("row", None),
        P(),
        P("row", "col", None),
        P(),
        P(),
        P(),
        P(),
        P(),
        P(),
        P(None, None, None, "col"),
        P(None, "col", None),
        P(),
        P(),
        P(),
        P(),
    )
    out_specs = P(None, ("row", "col"))
    return jax.shard_map(body, mesh=mesh, in_specs=in_specs, out_specs=out_specs, check_vma=False)
```

```python
import functools
import math

import jax
import jax.numpy as jnp
from jax import lax
from jax.experimental import pallas as pl
from jax.experimental.pallas import tpu as pltpu
from jax.sharding import PartitionSpec as P

HA = 4
QB = 32
KW = 128
HALO = 64
BLOCKS = 2
EXTRA = 16
MIB = 1 << 20
F32 = jnp.float32
BF16 = jnp.bfloat16


def call(kernel, outs, *args, scalars=(), far=(), scratch=(), grant=8, flops=0, moved=0):
    smem = pl.BlockSpec(memory_space=pltpu.SMEM)
    vmem = pl.BlockSpec(memory_space=pltpu.VMEM)
    hbm = pl.BlockSpec(memory_space=pltpu.HBM)
    return pl.pallas_call(
        kernel,
        out_shape=outs,
        in_specs=[smem] * len(scalars) + [vmem] * len(args) + [hbm] * len(far),
        out_specs=jax.tree.map(lambda _: vmem, outs),
        scratch_shapes=list(scratch),
        compiler_params=pltpu.CompilerParams(vmem_limit_bytes=grant * MIB),
        cost_estimate=pl.CostEstimate(flops=flops, bytes_accessed=moved, transcendentals=0),
    )(*scalars, *args, *far)


def dot(a, b):
    return jnp.dot(a, b, preferred_element_type=F32)


def dot_nt(a, b):
    return lax.dot_general(a, b, (((1,), (1,)), ((), ())), preferred_element_type=F32)


def dot_tn(a, b):
    return lax.dot_general(a, b, (((0,), (0,)), ((), ())), preferred_element_type=F32)


def normed(x):
    x = x.astype(F32)
    cent = x - jnp.mean(x, -1, keepdims=True)
    var = jnp.mean(cent * cent, -1, keepdims=True)
    return cent * lax.rsqrt(var + 1e-05)


def iota(shape, dim):
    return lax.broadcasted_iota(jnp.int32, shape, dim)


def device():
    row, col = lax.axis_index("row"), lax.axis_index("col")
    return row, col, row * lax.axis_size("col") + col


def window_mask(shifts, first, natom, nkeys):
    shape = (len(shifts) * QB, nkeys)
    block = iota(shape, 0) // QB
    low = jnp.zeros(shape, jnp.int32)
    for i, shift in enumerate(shifts):
        low = jnp.where(block == i, shift + QB * i, low)
    key = iota(shape, 1)
    atom = key + first
    return (key >= low) & (key < low + KW) & (atom >= 0) & (atom < natom)


def attend(x, xn, gate, query, keys, vals, mask, w_out):
    width = x.shape[1]
    hsize = width // HA
    lane = iota((1, width), 1) // hsize
    outs = jnp.zeros(x.shape, F32)
    for h in range(HA):
        pick = (lane == h).astype(BF16)
        scores = dot_nt(query, keys * pick) * (1.0 / math.sqrt(hsize))
        scores = jnp.where(mask, scores, -1000000000.0)
        top = jnp.max(scores, -1, keepdims=True)
        expd = jnp.exp(scores - top)
        total = jnp.sum(expd, -1, keepdims=True)
        outs = outs + dot(expd.astype(BF16), vals * pick) / total
    gated = (jax.nn.sigmoid(gate) * outs).astype(BF16)
    return (x.astype(F32) + dot(gated, w_out)).astype(BF16)


def shifts_of(tail_ref, lanes):
    tail = tail_ref[tail_ref.shape[0] - EXTRA :, :].astype(F32)
    return [tail[1:2, k : k + 1].astype(jnp.int32) for k in lanes]


def encoder_kernel(natom, own_ref, prev_ref, next_ref, w_in, w_out, ext_ref, all_ref):
    rows = own_ref.shape[0] - EXTRA
    nblk = rows // QB
    half = HALO // QB
    x = jnp.concatenate([prev_ref[:rows], own_ref[:rows], next_ref[:rows]], 0)
    xn = normed(x).astype(BF16)
    keys = dot(xn, w_in[1]).astype(BF16)
    vals = dot(xn, w_in[2]).astype(BF16)
    qx, qn = x[HALO : 3 * rows - HALO], xn[HALO : 3 * rows - HALO]
    query = dot(qn, w_in[0]).astype(BF16)
    gate = dot(qn, w_in[3])
    shifts = (
        shifts_of(prev_ref, range(nblk - half, nblk))
        + shifts_of(own_ref, range(nblk))
        + shifts_of(next_ref, range(half))
    )
    first = device()[2] * rows - rows
    for part in range(2):
        mine = slice(part * rows, (part + 1) * rows)
        seen = slice(part * rows, (part + 2) * rows)
        mask = window_mask(
            shifts[part * nblk : (part + 1) * nblk], first + part * rows, natom, 2 * rows
        )
        ext_ref[mine] = attend(
            qx[mine], qn[mine], gate[mine], query[mine], keys[seen], vals[seen], mask, w_out[...]
        )
    new = ext_ref[HALO : HALO + rows]
    tail = own_ref[rows:]
    for j in range(all_ref.shape[0]):
        all_ref[j, :rows] = new
        all_ref[j, rows:] = tail


def pool_kernel(both_ref, weight, cond, act_ref, xn_ref, send_ref):
    count, rows = both_ref.shape[0], both_ref.shape[1] - EXTRA
    tokens = cond.shape[0]
    sums = jnp.zeros(cond.shape, F32)
    counts = jnp.zeros((tokens, 1), F32)
    step = 4 if count % 4 == 0 else 1
    for j in range(0, count, step):
        atoms = jnp.concatenate([both_ref[j + k, :rows] for k in range(step)], 0)
        feats = jnp.maximum(dot(atoms, weight[...]), 0.0).astype(BF16)
        spot = jnp.concatenate(
            [both_ref[j + k, rows:].astype(F32)[0:1] for k in range(step)], 1
        ).astype(jnp.int32)
        onehot = (iota((tokens, step * rows), 0) == spot).astype(F32)
        sums = sums + dot(onehot.astype(BF16), feats)
        counts = counts + jnp.sum(onehot, -1, keepdims=True)
    act = sums / counts + cond[...].astype(F32)
    xn = normed(act)
    xn_ref[...] = xn.astype(BF16)
    cols = send_ref.shape[0]
    part = xn[:cols]
    for k in range(1, tokens // cols):
        part = jnp.where(device()[1] % (tokens // cols) == k, xn[k * cols : (k + 1) * cols], part)
    send_ref[...] = part.astype(BF16)
    own = act_ref.shape[0]
    col = device()[1]
    mine = act[:own]
    for c in range(1, tokens // own):
        mine = jnp.where(col == c, act[c * own : (c + 1) * own], mine)
    act_ref[...] = mine


def decoder_kernel(
    natom, x1_ref, own_ref, prev_ref, next_ref, proj_ref, edge_ref, w_in, w_out, pos, out
):
    rows = own_ref.shape[0] - EXTRA
    proj = proj_ref[...].astype(F32)
    edge = edge_ref[...].astype(F32)
    tokens = proj.shape[0]
    _, col, me = device()
    rest = tokens - HALO
    below = jnp.where(col == 0, edge, proj[rest:])
    above = jnp.where(col == lax.axis_size("col") - 1, edge, proj[:HALO])
    tables = (
        jnp.concatenate([proj[:rest], below], 0),
        proj,
        jnp.concatenate([above, proj[HALO:]], 0),
    )
    spread = []
    for table, ref in zip(tables, (prev_ref, own_ref, next_ref)):
        spot = ref[rows:].astype(F32)[0:1].astype(jnp.int32)
        onehot = (iota((tokens, rows), 0) == spot).astype(F32).astype(BF16)
        spread.append(dot_tn(onehot, table.astype(BF16)))
    spread = jnp.concatenate([spread[0][rows - HALO :], spread[1], spread[2][:HALO]], 0)
    x = (x1_ref[...].astype(F32) + spread).astype(BF16)
    xn = normed(x).astype(BF16)
    keys = dot(xn, w_in[1]).astype(BF16)
    vals = dot(xn, w_in[2]).astype(BF16)
    qx, qn = x[HALO : HALO + rows], xn[HALO : HALO + rows]
    query = dot(qn, w_in[0]).astype(BF16)
    gate = dot(qn, w_in[3])
    shifts = shifts_of(own_ref, range(rows // QB))
    mask = window_mask(shifts, me * rows - HALO, natom, 2 * rows)
    third = attend(qx, qn, gate, query, keys, vals, mask, w_out[...])
    out[...] = dot_nt(pos[...], normed(third).astype(BF16))


def feat_kernel(row_tokens, starts, feat, token, own):
    rows, width = feat.shape
    row, _, me = device()
    nblk = starts.shape[0]
    lane = iota((EXTRA, width), 1)
    line = iota((EXTRA, width), 0)
    tail = jnp.where(line == 0, token[...] - row * row_tokens, 0)
    for k in range(nblk):
        shift = starts[k] - QB * (me * nblk + k) + HALO
        tail = jnp.where((line == 1) & (lane == k), shift, tail)
    own[:rows] = feat[...]
    own[rows:] = tail.astype(F32).astype(BF16)


def pack_kernel(cuts, first, second, *outs):
    hid = second.shape[1]
    outs = list(outs)
    for layer, cut in enumerate(cuts):
        whole = outs.pop(0)
        whole[:hid] = first[layer, 0]
        whole[hid : 2 * hid] = first[layer, 1]
        whole[2 * hid :] = second[layer]
        begin = 0
        for sixths in cut:
            end = begin + sixths * (3 * hid // 6)
            outs.pop(0)[...] = whole[begin:end]
            begin = end


def bias_kernel(pair_ref, weight, *outs):
    rows, cols, _ = pair_ref.shape
    _, heads, pad = outs[0].shape
    pad = pad - cols

    for q in range(rows):
        bias = dot_nt(weight[...], pair_ref[q])
        bias = jnp.concatenate([bias, jnp.zeros((bias.shape[0], pad), F32)], 1)
        for layer, out in enumerate(outs):
            out[q] = bias[layer * heads : (layer + 1) * heads]


def prepare(sources, targets, sems):
    return [
        pltpu.make_async_copy(source, target, sems.at[i])
        for i, (source, target) in enumerate(zip(sources, targets))
    ]


def query_kernel(
    layer, xn_ref, act_ref, w_in, query, w_key, w_val, gate, w_query, w_gate, sems
):
    fetches = prepare(
        [w_in.at[layer, k] for k in range(4)], [w_query, w_key, w_val, w_gate], sems
    )
    for k in (0, 3, 1, 2):
        fetches[k].start()
    fetches[0].wait()
    query[...] = dot(xn_ref[...], w_query[...]).astype(BF16)
    fetches[3].wait()
    gate[...] = jax.nn.sigmoid(dot(normed(act_ref[...]).astype(BF16), w_gate[...]))
    fetches[1].wait()
    fetches[2].wait()


def attention_kernel(mask_ref, query, here_ref, came_ref, low, high, w_key, w_val, out_ref):
    rows, width = query.shape
    cols = here_ref.shape[0]
    heads = low.shape[1]
    hsize = width // heads
    span = low.shape[2]
    row, col, _ = device()
    mine = col * cols // rows == row
    key_xn = jnp.where(mine, here_ref[...].astype(F32), came_ref[...].astype(F32))
    key_xn = jnp.concatenate([key_xn, jnp.zeros((span - cols, width), F32)], 0).astype(BF16)
    keys = dot(key_xn, w_key[...]).astype(BF16)
    vals = dot(key_xn, w_val[...]).astype(BF16)
    tokens = mask_ref.shape[0]
    count = jnp.int32(0)
    for bit in range(tokens.bit_length() - 1, -1, -1):
        longer = count + (1 << bit)
        inside = longer <= tokens
        last = mask_ref[jnp.where(inside, longer - 1, 0)]
        count = jnp.where(inside & (last == 1), longer, count)
    valid = iota((1, span), 1) + col * cols < count
    valid = valid & (iota((1, span), 1) < cols)
    group = heads // 2
    part = group * hsize
    lane = iota((1, part), 1) // hsize
    spot = iota((1, span), 1)
    levels = jnp.zeros((rows, span), F32)
    for g in range(2):
        wide = slice(g * part, (g + 1) * part)
        kg, vg = keys[:, wide], vals[:, wide]
        picks = [(lane == h).astype(BF16) for h in range(group)]
        stacked = jnp.concatenate([kg * p for p in picks], 0)
        scores = dot_nt(query[:, wide], stacked) * (1.0 / math.sqrt(hsize))
        probs = []
        for h in range(group):
            head = g * group + h
            bias = jnp.concatenate([low[:, head, :], high[:, head, :]], 0)
            score = scores[:, h * span : (h + 1) * span] + bias
            score = jnp.where(valid, score, -1000000000.0)
            top = jnp.max(score, -1, keepdims=True)
            expd = jnp.exp(score - top)
            total = jnp.sum(expd, -1, keepdims=True)
            probs.append((expd / total).astype(BF16))
            levels = jnp.where(spot % heads == head, top + jnp.log(total), levels)
        stacked = jnp.concatenate([vg * p for p in picks], 0)
        out_ref[:, wide] = dot(jnp.concatenate(probs, 1), stacked).astype(BF16)
    high = levels.astype(BF16).astype(F32)
    rest = levels - high
    middle = rest.astype(BF16).astype(F32)
    low = rest - middle
    packed = jnp.where(spot < heads, high, jnp.where(spot < 2 * heads, middle, low))
    out_ref[:, width:] = jnp.where(spot < 3 * heads, packed, 0.0).astype(BF16)


def mix_kernel(layer, heads, message, act_ref, gate, w_out, act_out, w_mix, sems):
    (copy,) = prepare([w_out.at[layer]], [w_mix], sems)
    copy.start()
    width = act_ref.shape[1]
    hsize = width // heads
    parts = [message[j, :, width:].astype(F32) for j in range(message.shape[0])]
    span = parts[0].shape[1]
    levels = [
        p + pltpu.roll(p, span - heads, 1) + pltpu.roll(p, span - 2 * heads, 1) for p in parts
    ]
    top = functools.reduce(jnp.maximum, levels)
    weights = [jnp.exp(level - top) for level in levels]
    whole = functools.reduce(jnp.add, weights)
    lane = iota((1, span), 1)
    row = iota((span, width), 0)
    expand = (row % heads == iota((span, width), 1) // hsize) & (row < 2 * heads)
    expand = expand.astype(F32).astype(BF16)
    packed = []
    for weight in weights:
        weight = weight / whole
        high = weight.astype(BF16).astype(F32)
        both = jnp.where(lane < heads, high, pltpu.roll(weight - high, heads, 1))
        packed.append(jnp.where(lane < 2 * heads, both, 0.0))
    spread = dot(jnp.concatenate(packed, 0).astype(BF16), expand)
    own = act_ref.shape[0]
    attn = jnp.zeros(act_ref.shape, F32)
    for j in range(message.shape[0]):
        attn = attn + spread[j * own : (j + 1) * own] * message[j, :, :width].astype(F32)
    gated = (gate[...] * attn).astype(BF16)
    copy.wait()
    act_out[...] = act_ref[...] + dot(gated, w_mix[...])


def mix(layer, message, act, gate, w_out, heads):
    own, width = act.shape
    return call(
        functools.partial(mix_kernel, layer, heads),
        jax.ShapeDtypeStruct((own, width), F32),
        message,
        act,
        gate,
        far=(w_out,),
        scratch=[pltpu.VMEM((width, width), BF16), pltpu.SemaphoreType.DMA((1,))],
        grant=48,
        flops=4 * own * width * width,
        moved=4 * width * width,
    )


def transition_kernel(groups, pieces, act_ref, *refs):
    others, refs = refs[: groups - 1], refs[groups - 1 :]
    sources = []
    for number in pieces:
        sources.append(refs[:number])
        refs = refs[number:]
    base, send, w_first, w_second, sems = refs
    count, hid = w_second.shape[:2]
    plan = []
    for wanted, target in (((0, 2 * hid), w_first), ((2 * hid, 3 * hid), w_second)):
        for j, source in enumerate(sources):
            begin = 0
            for ref in source:
                end = begin + ref.shape[0]
                low, high = max(begin, wanted[0]), min(end, wanted[1])
                if low < high:
                    near = target.at[j, pl.ds(low - wanted[0], high - low)]
                    plan.append((target is w_first, j, ref.at[pl.ds(low - begin, high - low)], near))
                begin = end
    fetches = prepare([item[2] for item in plan], [item[3] for item in plan], sems)
    for copy in fetches:
        copy.start()

    def arrived(first, j):
        for item, copy in zip(plan, fetches):
            if item[:2] == (first, j):
                copy.wait()

    group = device()[1] // 4
    came = [ref[...] for ref in (act_ref, *others)]
    ordered = []
    for place in range(groups):
        rows = came[0]
        for d in range(1, groups):
            rows = jnp.where((group - place + groups) % groups == d, came[d], rows)
        ordered.append(rows)
    act = jnp.concatenate(ordered, 0)
    rows = normed(act).astype(BF16)
    total = jnp.zeros(act.shape, F32)
    hidden = []
    for j in range(count):
        arrived(True, j)
        both = dot_nt(rows, w_first[j])
        left, right = both[:, :hid], both[:, hid:]
        hidden.append((left * jax.nn.sigmoid(left) * right).astype(BF16))
    for j in range(count):
        arrived(False, j)
        total = total + dot(hidden[j], w_second[j])
    base[...] = act + total
    send[...] = total.astype(BF16)


def transition(act, others, weights):
    own, width = act.shape
    blocks = len(weights)
    hid = sum(part.shape[0] for part in weights[0]) // 3
    parts = [part for source in weights for part in source]
    return call(
        functools.partial(transition_kernel, len(others) + 1, [len(source) for source in weights]),
        [jax.ShapeDtypeStruct(((len(others) + 1) * own, width), kind) for kind in (F32, BF16)],
        act,
        *others,
        far=parts,
        scratch=[
            pltpu.VMEM((blocks, 2 * hid, width), BF16),
            pltpu.VMEM((blocks, hid, width), BF16),
            pltpu.SemaphoreType.DMA((2 * len(parts),)),
        ],
        grant=48,
        flops=12 * own * hid * width * blocks,
        moved=6 * hid * width * blocks,
    )


def close_kernel(project, act_ref, *refs):
    *refs, act_out, out = refs
    if project:
        *refs, tok_atom = refs
    act = act_ref[...]
    for ref in refs:
        act = act + ref[...].astype(F32)
    own = act_out.shape[0]
    mine = act[:own]
    for k in range(1, act.shape[0] // own):
        mine = jnp.where(device()[1] // 4 == k, act[k * own : (k + 1) * own], mine)
    act_out[...] = mine
    normal = normed(act).astype(BF16)
    if project:
        normal = dot(normal, tok_atom[...]).astype(BF16)
    out[...] = normal


def close(own, act, parts, tok_atom):
    rows, width = act.shape
    project = tok_atom is not None
    last = tok_atom.shape[1] if project else width
    return call(
        functools.partial(close_kernel, project),
        [jax.ShapeDtypeStruct((own, width), F32), jax.ShapeDtypeStruct((rows, last), BF16)],
        act,
        *parts,
        *([tok_atom] if project else []),
        flops=10**7,
        moved=10**6,
    )


def row_of(mine, own):
    nrow, ncol = lax.axis_size("row"), lax.axis_size("col")
    parts = [mine]
    for flip in range(1, 4):
        parts.append(
            lax.ppermute(mine, ("row", "col"), [(i, i ^ flip) for i in range(nrow * ncol)])
        )
    low = lax.axis_index("col") % 4
    ordered = []
    for place in range(4):
        rows = parts[place]
        for flip in range(1, 4):
            rows = jnp.where(low == flip, parts[place ^ flip], rows)
        ordered.append(rows.reshape(-1, 1, own, mine.shape[1]))
    return jnp.concatenate(ordered, 1).reshape(-1, mine.shape[1])


def key_source(rows, cols):
    nrow, ncol = lax.axis_size("row"), lax.axis_size("col")
    shares = rows // cols
    chips = ncol // shares
    pairs = []
    for owner in range(nrow):
        near = sorted(range(chips), key=lambda chip: bin((chip ^ owner) % chips).count("1"))
        others = sorted((r for r in range(nrow) if r != owner), key=lambda r: -abs(r - owner))
        for chip, r in zip(near, others):
            for share in range(shares):
                pairs.append((owner * ncol + chip * shares + share, r * ncol + owner * shares + share))
    return pairs


def body(
    atom_feat,
    atom_token,
    window_start,
    token_cond,
    token_mask,
    pair,
    enc_in,
    enc_out,
    pool_weight,
    tok_in,
    tok_out,
    pair_weight,
    trans_in,
    trans_out,
    tok_atom,
    dec_in,
    dec_out,
    pos_out,
):
    nrow, ncol = lax.axis_size("row"), lax.axis_size("col")
    everyone = ("row", "col")
    count = nrow * ncol
    me_col = lax.axis_index("col")
    rows, width = token_cond.shape
    cols = pair.shape[1]
    heads = pair_weight.shape[2]
    own = rows // ncol
    atoms, afeat = atom_feat.shape
    natom = atoms * count
    nblk = atoms // QB

    hid = trans_out.shape[1]
    feat = call(
        functools.partial(feat_kernel, rows),
        jax.ShapeDtypeStruct((atoms + EXTRA, afeat), BF16),
        atom_feat,
        atom_token[None],
        scalars=(window_start,),
        grant=48,
        moved=10**5,
    )
    up = [(i, i + 1) for i in range(count - 1)]
    prev = lax.ppermute(feat, everyone, up)
    after = lax.ppermute(feat, everyone, [(b, a) for a, b in up])
    _, first_part, second_part = lax.optimization_barrier(
        (feat, jnp.swapaxes(trans_in, 2, 3), trans_out)
    )
    matrix = jax.ShapeDtypeStruct((3 * hid, width), BF16)
    cuts = ((3, 3), (3, 3))
    pieces = call(
        functools.partial(pack_kernel, cuts),
        [
            jax.ShapeDtypeStruct((sixths * (3 * hid // 6), width), BF16)
            for cut in cuts
            for sixths in (6,) + cut
        ],
        first_part,
        second_part,
        grant=60,
        moved=12 * trans_out.size,
    )
    packed, cut_up = [], []
    for cut in cuts:
        packed.append(pieces[0])
        cut_up.append(pieces[1 : 1 + len(cut)])
        pieces = pieces[1 + len(cut) :]
    prev, after, early = lax.optimization_barrier((prev, after, cut_up[0][0]))
    neighbour = [(i, i ^ 2) for i in range(count)]
    sibling = [(i, i ^ 1) for i in range(count)]
    across = [[lax.ppermute(early, everyone, neighbour)], []]

    ext, copies = call(
        functools.partial(encoder_kernel, natom),
        [
            jax.ShapeDtypeStruct((atoms + 2 * HALO, afeat), BF16),
            jax.ShapeDtypeStruct((ncol, atoms + EXTRA, afeat), BF16),
        ],
        feat,
        prev,
        after,
        enc_in,
        enc_out,
        flops=10**8,
        moved=10**6,
    )
    span = -(-cols // 128) * 128
    step = 24
    early_steps = rows // step * 5 // 8

    def bias_of(part, weights):
        begin, end = ((0, early_steps), (early_steps, rows // step))[part]
        return pl.pallas_call(
            bias_kernel,
            grid=(end - begin,),
            out_shape=[jax.ShapeDtypeStruct(((end - begin) * step, heads, span), F32)] * BLOCKS,
            in_specs=[
                pl.BlockSpec((step, cols, pair.shape[2]), lambda i: (i + begin, 0, 0)),
                pl.BlockSpec(weights.shape, lambda i: (0, 0)),
            ],
            out_specs=[pl.BlockSpec((step, heads, span), lambda i: (i, 0, 0))] * BLOCKS,
            compiler_params=pltpu.CompilerParams(vmem_limit_bytes=(52 if part else 60) * MIB),
            cost_estimate=pl.CostEstimate(
                flops=2 * 10**9, bytes_accessed=4 * 10**6, transcendentals=0
            ),
        )(pair, weights)

    weights = jnp.swapaxes(pair_weight, 1, 2).reshape(BLOCKS * heads, -1)
    copies, first_weights = lax.optimization_barrier((copies, weights))
    low = bias_of(0, first_weights)
    both = lax.all_to_all(copies, "col", 0, 0)
    both, low, across[0][0] = lax.optimization_barrier((both, low, across[0][0]))

    act, xn, send = call(
        pool_kernel,
        [
            jax.ShapeDtypeStruct((own, width), F32),
            jax.ShapeDtypeStruct((rows, width), BF16),
            jax.ShapeDtypeStruct((cols, width), BF16),
        ],
        both,
        pool_weight,
        token_cond,
        flops=10**9,
        moved=10**6,
    )

    pairs = key_source(rows, cols)
    share = me_col % (rows // cols)
    peers = ncol // 4
    shifts = [
        [(r * ncol + c, r * ncol + (c + 4 * d) % ncol) for r in range(nrow) for c in range(ncol)]
        for d in range(peers)
    ]
    xn, weights = lax.optimization_barrier((xn, weights))
    beside, beyond = [], [[], []]
    for layer in range(BLOCKS):
        last = layer == BLOCKS - 1
        if layer:
            send = lax.dynamic_slice_in_dim(xn, share * cols, cols, 0)
            send, xn = lax.optimization_barrier((send, xn))
        came = lax.ppermute(send, everyone, pairs)
        matrix = jax.ShapeDtypeStruct((width, width), BF16)
        query, w_key, w_val, gate = call(
            functools.partial(query_kernel, layer),
            [
                jax.ShapeDtypeStruct((rows, width), BF16),
                matrix,
                matrix,
                jax.ShapeDtypeStruct((own, width), F32),
            ],
            xn,
            act,
            far=(tok_in,),
            scratch=[pltpu.VMEM((width, width), BF16)] * 2 + [pltpu.SemaphoreType.DMA((4,))],
            grant=48,
            flops=2 * rows * width * width,
            moved=8 * width * width,
        )
        if not layer:
            high = list(bias_of(1, weights))
            high[0], *late = lax.optimization_barrier((high[0], *cut_up[0][1:]))
            across[0] += [lax.ppermute(part, everyone, neighbour) for part in late]
            high[0], *ready = lax.optimization_barrier((high[0], *packed))
            beside = [lax.ppermute(part, everyone, sibling) for part in ready]
        else:
            query, late = lax.optimization_barrier((query, cut_up[1][1]))
            across[1].append(lax.ppermute(late, everyone, neighbour))
        message = call(
            attention_kernel,
            jax.ShapeDtypeStruct((rows, width + span), BF16),
            query,
            send,
            came,
            low[layer],
            high[layer],
            w_key,
            w_val,
            scalars=(token_mask,),
            grant=16,
            flops=10**9,
            moved=8 * 10**6,
        )
        message = lax.all_to_all(message.reshape(ncol, own, -1), "col", 0, 0)
        if not layer:
            message, ready = lax.optimization_barrier((message, cut_up[1][0]))
            across[1].append(lax.ppermute(ready, everyone, neighbour))
        act = mix(layer, message, act, gate, tok_out, heads)
        came_rows = [lax.ppermute(act, everyone, shifts[d]) for d in range(1, peers)]
        act, *ready = lax.optimization_barrier((act, *across[layer]))
        beyond[layer] = [lax.ppermute(part, everyone, sibling) for part in ready]
        act, part = transition(
            act, came_rows, ([packed[layer]], [beside[layer]], across[layer], beyond[layer])
        )
        parts = [lax.ppermute(part, everyone, shifts[d]) for d in range(1, peers)]
        act, mine = close(own, act, parts, tok_atom if last else None)
        if not last:
            mine, across[1][0] = lax.optimization_barrier((mine, across[1][0]))
        gathered = row_of(mine, own)
        if not last:
            xn = gathered

    bounds = [(r * ncol, (r + 1) * ncol) for r in range(nrow - 1)]
    bounds += [((r + 2) * ncol - 1, (r + 1) * ncol - 1) for r in range(nrow - 1)]
    edge = jnp.where(me_col == 0, gathered[rows - HALO :], gathered[:HALO])
    edge = lax.ppermute(edge, everyone, bounds)

    return call(
        functools.partial(decoder_kernel, natom),
        jax.ShapeDtypeStruct((pos_out.shape[0], atoms), F32),
        ext,
        feat,
        prev,
        after,
        gathered,
        edge,
        dec_in,
        dec_out,
        pos_out,
        flops=10**8,
        moved=10**6,
    )


def solution(mesh):
    in_specs = (
        P(("row", "col"), None),
        P(("row", "col")),
        P(("row", "col")),
        P("row", None),
        P(),
        P("row", "col", None),
        P(),
        P(),
        P(),
        P(),
        P(),
        P(),
        P(None, None, None, "col"),
        P(None, "col", None),
        P(),
        P(),
        P(),
        P(),
    )
    out_specs = P(None, ("row", "col"))
    return jax.shard_map(body, mesh=mesh, in_specs=in_specs, out_specs=out_specs, check_vma=False)
```
